256 devices in a mesh: gx: 16 (over y_lo, x, core), gy: 16 (over y_hi, z).
Axes of the slice: x: 4, y: 4 (y_hi: 2, y_lo: 2; y = y_hi * 2 + y_lo), z: 8, core: 2. Of those that a mesh axis runs over, the one named last changes fastest.
Arguments:
- scalar_field: float32 [128, 8192], P('gx', 'gy'), may hold values from -6 to 6
- field_cotangent: float32 [128, 8192], P('gx', 'gy'), may hold values from -6 to 6
- diffusivity: float32 [128, 8192], P('gx', 'gy'), may hold values from 0.2 to 1
- velocity: float32 [3, 128, 8192], P(None, 'gx', 'gy'), may hold values from -3 to 3
- conv_in: bfloat16 [27, 32], replicated, may hold values from -1.25 to 1.25
- bias_in: float32 [32], replicated, may hold values from -3 to 3
- conv_mid: bfloat16 [27, 32, 32], replicated, may hold values from -0.21875 to 0.21875
- bias_mid: float32 [32], replicated, may hold values from -3 to 3
- flux_out: bfloat16 [32, 3], replicated, may hold values from -1 to 1
Outputs:
- grad_field: float32 [128, 8192], P('gx', 'gy')
- grad_conv_in: float32 [27, 32], replicated
- grad_bias_in: float32 [32], replicated
- grad_conv_mid: float32 [27, 32, 32], replicated
- grad_bias_mid: float32 [32], replicated
- grad_flux_out: float32 [32, 3], replicated
The draws below stay inside these ranges and needn't reach their ends.
All inputs are finite; a program needn't handle non-finite values.
Results may differ from the reference program's by a relative error of at most 0.012.
The reference program's roundings to bfloat16 on the way (of `rounded`, `hidden_one`, `hidden_two`, `grad_two` and `grad_one`) count: a program that leaves them out, or rounds other values in their place, can miss the bound.
Values may be sent and summed in bfloat16 or wider, within the bound.
A program may use at most 64 MiB of HBM per device.

```python
import math
import jax
import jax.numpy as jnp
from jax import lax

NZ = 32
C = 32
NX = 128
NY = 256


def block_scale(own_key, dims, cuts, low, high):
    def one(axis_at, parts):
        draws = jax.random.uniform(jax.random.fold_in(jax.random.fold_in(own_key, 6), axis_at), (parts,), jnp.float32, low / len(cuts), high / len(cuts))
        return jnp.repeat(jnp.exp(draws), dims[axis_at] // parts).reshape((-1,) + (1,) * (len(dims) - axis_at - 1))

    level = one(*cuts[0])
    for cut in cuts[1:]:
        level = level * one(*cut)
    return level


def centred(own_key, shape, spread, bound, shards=(), kind=jnp.bfloat16):
    values = spread * jax.random.normal(own_key, shape, jnp.float32)
    if shards:
        values = values * block_scale(own_key, shape, shards, -0.22, 0.18)
    return jnp.clip(values, -bound, bound).astype(kind)


def setup_inputs(seed: int = 0) -> dict:
    streams_of = jax.random.split(jax.random.key(seed), 10)
    scalar_field = centred(streams_of[0], (NX, NY * NZ), 1.0, 6.0, ((0, 16), (1, 16)), jnp.float32)
    field_cotangent = centred(streams_of[1], (NX, NY * NZ), 1.0, 6.0, ((0, 16), (1, 16)), jnp.float32)
    diffusivity = jnp.clip(jnp.exp(math.log(1.0) - 1.609438 * jax.random.uniform(streams_of[2], (NX, NY * NZ), jnp.float32) ** block_scale(streams_of[2], (NX, NY * NZ), ((0, 16), (1, 16)), -0.2, 0.2)), 0.2, 1.0)
    velocity = centred(streams_of[3], (3, NX, NY * NZ), 0.5, 3.0, ((1, 16), (2, 16)), jnp.float32)
    conv_in = centred(streams_of[4], (27, C), 27 ** -0.5, 1.25)
    bias_in = centred(streams_of[5], (C,), 0.5, 3.0, (), jnp.float32)
    conv_mid = centred(streams_of[6], (27, C, C), (27 * C) ** -0.5, 0.21875)
    bias_mid = centred(streams_of[7], (C,), 0.5, 3.0, (), jnp.float32)
    flux_out = centred(streams_of[8], (C, 3), C ** -0.5, 1.0)
    return dict(scalar_field=scalar_field, field_cotangent=field_cotangent, diffusivity=diffusivity, velocity=velocity, conv_in=conv_in, bias_in=bias_in, conv_mid=conv_mid, bias_mid=bias_mid, flux_out=flux_out)


time_step = 0.2
highest = lax.Precision.HIGHEST

def offsets():
    return [(step_x, step_y, step_z) for step_x in (-1, 0, 1) for step_y in (-1, 0, 1) for step_z in (-1, 0, 1)]

def negate(offset):
    return (-offset[0], -offset[1], -offset[2])

def unit(dimension, factor):
    return tuple((factor if position == dimension else 0 for position in range(3)))

def moved(values, offset):
    rolled = jnp.roll(values, (-offset[0], -offset[1]), axis=(-3, -2))
    if offset[2] == 0:
        return rolled
    padding = jnp.zeros_like(rolled[..., :1])
    if offset[2] == 1:
        return jnp.concatenate([rolled[..., 1:], padding], axis=-1)
    return jnp.concatenate([padding, rolled[..., :-1]], axis=-1)

def central(values, dimension):
    return 0.5 * (moved(values, unit(dimension, 1)) - moved(values, unit(dimension, -1)))

def laplace(values):
    running = -6.0 * values
    for dimension in range(3):
        running = running + moved(values, unit(dimension, 1)) + moved(values, unit(dimension, -1))
    return running

def advance(current, diffusivity, velocity, conv_in, bias_in, conv_mid, bias_mid, flux_out):
    rounded = current.astype(jnp.bfloat16)
    channels = conv_in.shape[1]
    running = jnp.zeros((channels,) + current.shape, jnp.float32)
    for number, offset in enumerate(offsets()):
        running = running + conv_in[number].astype(jnp.float32)[:, None, None, None] * moved(rounded, offset).astype(jnp.float32)[None]
    hidden_one = jnp.tanh(running + bias_in[:, None, None, None]).astype(jnp.bfloat16)
    running = jnp.zeros((channels,) + current.shape, jnp.float32)
    for number, offset in enumerate(offsets()):
        running = running + jnp.einsum('cxyz,co->oxyz', moved(hidden_one, offset).astype(jnp.float32), conv_mid[number].astype(jnp.float32))
    hidden_two = jnp.tanh(running + bias_mid[:, None, None, None]).astype(jnp.bfloat16)
    fluxes = jnp.einsum('cxyz,cd->dxyz', hidden_two.astype(jnp.float32), flux_out.astype(jnp.float32))
    correction = central(fluxes[0], 0) + central(fluxes[1], 1) + central(fluxes[2], 2)
    physics = diffusivity * laplace(current)
    for dimension in range(3):
        physics = physics - velocity[dimension] * central(current, dimension)
    return (current + time_step * (physics + correction), (rounded, hidden_one, hidden_two))

def retreat(adjoint, stored, diffusivity, velocity, conv_in, conv_mid, flux_out):
    rounded, hidden_one, hidden_two = stored
    grad_flux = jnp.stack([-time_step * central(adjoint, dimension) for dimension in range(3)])
    two_wide = hidden_two.astype(jnp.float32)
    term_out = jnp.einsum('cxyz,dxyz->cd', two_wide, grad_flux, precision=highest)
    back_two = jnp.einsum('cd,dxyz->cxyz', flux_out.astype(jnp.float32), grad_flux, precision=highest)
    grad_two = (back_two * (1.0 - two_wide * two_wide)).astype(jnp.bfloat16)
    grad_two_wide = grad_two.astype(jnp.float32)
    term_bias_mid = lax.optimization_barrier(jnp.sum(grad_two_wide, axis=(1, 2, 3)))
    terms_mid = []
    back_one = jnp.zeros(hidden_one.shape, jnp.float32)
    for number, offset in enumerate(offsets()):
        terms_mid.append(jnp.einsum('cxyz,oxyz->co', moved(hidden_one, offset).astype(jnp.float32), grad_two_wide))
        back_one = back_one + jnp.einsum('co,oxyz->cxyz', conv_mid[number].astype(jnp.float32), moved(grad_two, negate(offset)).astype(jnp.float32))
    one_wide = hidden_one.astype(jnp.float32)
    grad_one = (back_one * (1.0 - one_wide * one_wide)).astype(jnp.bfloat16)
    grad_one_wide = grad_one.astype(jnp.float32)
    term_bias_in = lax.optimization_barrier(jnp.sum(grad_one_wide, axis=(1, 2, 3)))
    terms_in = []
    back_field = jnp.zeros(adjoint.shape, jnp.float32)
    for number, offset in enumerate(offsets()):
        terms_in.append(jnp.einsum('xyz,cxyz->c', moved(rounded, offset).astype(jnp.float32), grad_one_wide))
        back_field = back_field + jnp.einsum('c,cxyz->xyz', conv_in[number].astype(jnp.float32), moved(grad_one, negate(offset)).astype(jnp.float32))
    physics = laplace(diffusivity * adjoint)
    for dimension in range(3):
        physics = physics + central(velocity[dimension] * adjoint, dimension)
    previous = adjoint + time_step * physics + back_field
    return (previous, (jnp.stack(terms_in), term_bias_in, jnp.stack(terms_mid), term_bias_mid, term_out))

def reference(scalar_field, field_cotangent, diffusivity, velocity, conv_in, bias_in, conv_mid, bias_mid, flux_out):
    grid_shape = (NX, NY, NZ)
    current = scalar_field.reshape(grid_shape)
    grid_kappa = diffusivity.reshape(grid_shape)
    grid_velocity = velocity.reshape((3,) + grid_shape)
    field_one, stored_one = advance(current, grid_kappa, grid_velocity, conv_in, bias_in, conv_mid, bias_mid, flux_out)
    stored_two = advance(field_one, grid_kappa, grid_velocity, conv_in, bias_in, conv_mid, bias_mid, flux_out)[1]
    adjoint_one, terms_two = retreat(field_cotangent.reshape(grid_shape), stored_two, grid_kappa, grid_velocity, conv_in, conv_mid, flux_out)
    adjoint_zero, terms_one = retreat(adjoint_one, stored_one, grid_kappa, grid_velocity, conv_in, conv_mid, flux_out)
    scale = 1.0 / math.sqrt(NX * NY * NZ)
    grads = [(first + second) * scale for first, second in zip(terms_one, terms_two)]
    return (adjoint_zero.reshape(NX, NY * NZ), grads[0], grads[1], grads[2], grads[3], grads[4])
```

```python
import math

import jax
import jax.numpy as jnp
import numpy as np
from jax import lax
from jax.experimental import pallas as pl
from jax.experimental.pallas import tpu as pltpu
from jax.sharding import PartitionSpec as P

NZ = 32
C = 32
ROWS = 8
LANES = 512
HALO = 128
WIDE = LANES + 2 * HALO
TALL = 3 * ROWS
time_step = 0.2
MESH = pl.DeviceIdType.MESH
STEPS = (-1, 0, 1)
AROUND = tuple((dx, dy) for dx in STEPS for dy in STEPS if (dx, dy) != (0, 0))
OWN_ROWS = slice(ROWS, 2 * ROWS)
OWN_LANES = slice(HALO, HALO + LANES)
bf16 = jnp.bfloat16
f32 = jnp.float32


def shifted(values, count):
    if count == 0:
        return values
    return pltpu.roll(values, (-count) % values.shape[-1], axis=values.ndim - 1)


def lane_index(values):
    return lax.broadcasted_iota(jnp.int32, values.shape, values.ndim - 1)


def lifted(values, step_z):
    if step_z == 0:
        return values
    edge = NZ - 1 if step_z == 1 else 0
    moved = shifted(values, step_z)
    return jnp.where(lane_index(values) % NZ == edge, jnp.zeros_like(moved), moved)


def own_lanes_only(values):
    lane = lane_index(values)
    return jnp.where((lane >= HALO) & (lane < HALO + LANES), values, jnp.zeros_like(values))


def dot(left, right):
    return lax.dot_general(left, right, (((1,), (0,)), ((), ())), preferred_element_type=f32)


def dot_lanes(left, right):
    return lax.dot_general(left, right, (((1,), (1,)), ((), ())), preferred_element_type=f32)


def central_y(values):
    return 0.5 * (shifted(values, NZ) - shifted(values, -NZ))


def central_z(values):
    return 0.5 * (lifted(values, 1) - lifted(values, -1))


def column_to_row(column):
    size = column.shape[0]
    wide = jnp.broadcast_to(column, (size, size))
    row = lax.broadcasted_iota(jnp.int32, (size, size), 0)
    col = lax.broadcasted_iota(jnp.int32, (size, size), 1)
    return jnp.sum(jnp.where(row == col, wide, 0.0), axis=0, keepdims=True)


def first_stack(field_ext):
    rounded = field_ext[4:20, :].astype(bf16).astype(f32)
    moves = [lifted(shifted(rounded, NZ * b), c) for b in STEPS for c in STEPS]
    return jnp.concatenate(moves, axis=0).astype(bf16)


def z_stack(values, target, sign):
    count = target.shape[0]
    wide = values.astype(f32)
    for number, c in enumerate(STEPS):
        moved = lifted(wide, sign * c).astype(bf16) if c else values
        target[:, number * C : (number + 1) * C, :] = moved.reshape(count, C, WIDE)


def middle_conv(weights, stack, start, sign):
    window = stack[start : start + 5].reshape(5 * 3 * C, WIDE)
    out = dot(weights[...], window).reshape(3, 3, C, WIDE)
    result = out[:, 1]
    for number, b in ((0, -1), (2, 1)):
        part = out[:, number].reshape(3 * C, WIDE)
        result = result + shifted(part, sign * NZ * b).reshape(3, C, WIDE)
    return result


def forward(field_ext, b0, bias_in, w_fwd, bias_mid, stack, hidden_two):
    first = first_stack(field_ext)
    pre = dot(b0[...], first).reshape(14, C, WIDE)
    hidden_one = jnp.tanh(pre + bias_in[...][None]).astype(bf16).reshape(14 * C, WIDE)
    z_stack(hidden_one, stack, 1)
    for start in (0, 3, 6, 9):
        pre = middle_conv(w_fwd, stack, start, 1)
        hidden_two[start : start + 3] = jnp.tanh(pre + bias_mid[...][None]).astype(bf16)
    return first


def stepped(field_ext, kappa, vel, bf, hidden_two):
    flux = dot(bf[...], hidden_two[...].reshape(12 * C, WIDE))
    correction = flux[0:8] + central_y(flux[8:16]) + central_z(flux[16:24])
    here, up, down = field_ext[8:16, :], field_ext[9:17, :], field_ext[7:15, :]
    laplace = (
        up + down + shifted(here, NZ) + shifted(here, -NZ) + lifted(here, 1) + lifted(here, -1)
    )
    laplace = laplace - 6.0 * here
    own = lambda values: values[:, OWN_LANES]
    physics = kappa[...] * own(laplace)
    physics = physics - vel[0] * own(0.5 * (up - down))
    physics = physics - vel[1] * own(central_y(here))
    physics = physics - vel[2] * own(central_z(here))
    return own(here) + time_step * (physics + own(correction))


def cotangent_two(g_ext, bb, hidden_two, grad_two):
    here = g_ext[4:20, :]
    parts = [
        -0.5 * time_step * (g_ext[5:21, :] - g_ext[3:19, :]),
        -time_step * central_y(here),
        -time_step * central_z(here),
    ]
    flux = jnp.concatenate(parts, axis=0)
    high = flux.astype(bf16)
    low = (flux - high.astype(f32)).astype(bf16)
    pair = jnp.concatenate([high, low], axis=0)
    two = hidden_two[...].astype(f32)
    back = dot(bb[...], pair).reshape(12, C, WIDE)
    grad_two[...] = (back * (1.0 - two * two)).astype(bf16)
    return pair


def middle_terms(pair, stack, hidden_two, grad_two, spread):
    own = own_lanes_only(grad_two[2:10].reshape(8 * C, WIDE).astype(f32))
    for number, b in enumerate(STEPS):
        moved = shifted(own, -NZ * b).astype(bf16)
        spread[:, number * C : (number + 1) * C, :] = moved.reshape(8, C, WIDE)
    term_mid = jnp.zeros((9 * C, 3 * C), f32)
    for x in range(ROWS):
        window = stack[x + 2 : x + 5].reshape(9 * C, WIDE)
        term_mid = term_mid + dot_lanes(window, spread[x])
    bias_mid = jnp.sum(jnp.sum(own.reshape(8, C, WIDE), axis=0), axis=1, keepdims=True)
    masked = own_lanes_only(pair.astype(f32)).astype(bf16)
    outer = dot_lanes(hidden_two[2:10].reshape(8 * C, WIDE), masked)
    row_x = lax.broadcasted_iota(jnp.int32, outer.shape, 0) // C
    col = lax.broadcasted_iota(jnp.int32, outer.shape, 1)
    outer = jnp.where(col % 16 == row_x + 4, outer, 0.0)
    outer = jnp.sum(outer.reshape(8, C, outer.shape[1]), axis=0)
    kind = (lax.broadcasted_iota(jnp.int32, outer.shape, 1) // 16) % 3
    term_out = [
        jnp.sum(jnp.where(kind == d, outer, 0.0), axis=1, keepdims=True) for d in range(3)
    ]
    return term_mid, bias_mid, term_out


def cotangent_one(w_bwd, stack, grad_two, grad_stack, grad_one):
    z_stack(grad_two[...].reshape(12 * C, WIDE), grad_stack, -1)
    for start in (0, 3, 6, 7):
        back = middle_conv(w_bwd, grad_stack, start, -1)
        one = stack[start + 2 : start + 5, C : 2 * C, :].astype(f32)
        grad_one[start : start + 3] = (back * (1.0 - one * one)).astype(bf16)


def first_terms(first, grad_one):
    own = own_lanes_only(grad_one[1:9].reshape(8 * C, WIDE).astype(f32))
    outer = dot_lanes(first, own.astype(bf16))
    row_x = lax.broadcasted_iota(jnp.int32, outer.shape, 0) % 16
    col_x = lax.broadcasted_iota(jnp.int32, outer.shape, 1) // C
    parts = []
    for a in range(3):
        kept = jnp.where(row_x - col_x == a + 3, outer, 0.0)
        parts.append(jnp.sum(kept.reshape(9, 16, 8 * C), axis=1))
    folded = jnp.concatenate(parts, axis=0)
    folded = folded[:, :128] + folded[:, 128:]
    folded = folded + pltpu.roll(folded, 64, axis=1)
    folded = folded + pltpu.roll(folded, 32, axis=1)
    bias_in = jnp.sum(jnp.sum(own.reshape(8, C, WIDE), axis=0), axis=1, keepdims=True)
    return folded[:, :C], bias_in


def previous(g_ext, k_ext, v0_ext, v1_ext, vel, bq, grad_one):
    spread = dot(bq[...], grad_one[...].reshape(10 * C, WIDE))
    total = 0.0
    for number, (b, c) in enumerate([(b, c) for b in STEPS for c in STEPS]):
        total = total + lifted(shifted(spread[number * 8 : number * 8 + 8], -NZ * b), -c)
    here = g_ext[8:16, :]
    scaled = k_ext[8:16, :] * here
    up = k_ext[9:17, :] * g_ext[9:17, :]
    down = k_ext[7:15, :] * g_ext[7:15, :]
    physics = up + down + shifted(scaled, NZ) + shifted(scaled, -NZ)
    physics = physics + lifted(scaled, 1) + lifted(scaled, -1) - 6.0 * scaled
    physics = physics + 0.5 * (
        v0_ext[9:17, :] * g_ext[9:17, :] - v0_ext[7:15, :] * g_ext[7:15, :]
    )
    physics = physics + central_y(v1_ext[8:16, :] * here)
    lifted_part = central_z(vel[2] * here[:, OWN_LANES])
    own = lambda values: values[:, OWN_LANES]
    return own(here) + time_step * (own(physics) + lifted_part) + own(total)


def copies_around(ext, send_sem, recv_sem, number, gx, gy, around):
    (me_x, size_x), (me_y, size_y) = gx, gy
    started = []
    for dx, dy in around:
        slot = AROUND.index((dx, dy))
        source = {0: OWN_LANES, 1: slice(LANES, LANES + HALO), -1: slice(HALO, 2 * HALO)}[dy]
        lanes = {0: OWN_LANES, 1: slice(0, HALO), -1: slice(HALO + LANES, WIDE)}[dy]
        rows = {0: OWN_ROWS, 1: slice(0, ROWS), -1: slice(2 * ROWS, TALL)}[dx]
        copy = pltpu.make_async_remote_copy(
            src_ref=ext.at[OWN_ROWS, source],
            dst_ref=ext.at[rows, lanes],
            send_sem=send_sem.at[number, slot],
            recv_sem=recv_sem.at[number, slot],
            device_id=(
                lax.rem(me_x + dx + size_x, size_x),
                lax.rem(me_y + dy + size_y, size_y),
            ),
            device_id_type=MESH,
        )
        copy.start()
        started.append(copy)
    return started


def kernel(
    size_x, size_y, scale,
    field, cotangent, kappa, vel, b0, bias_in, w_fwd, bias_mid, bf, bb, w_bwd, bq,
    out_field, out_in, out_bias_in, out_mid, out_bias_mid, out_out,
    f_ext, f1_ext, g_ext, a_ext, k_ext, v0_ext, v1_ext,
    stack_one, stack_two, two_one, two_two, grad_two, spread, grad_stack, grad_one,
    sums, recv_x, recv_y, gathered,
    send_sem, recv_sem, sum_send, sum_recv,
):
    me_x, me_y = lax.axis_index("gx"), lax.axis_index("gy")
    gx, gy = (me_x, size_x), (me_y, size_y)
    peers = [(lax.rem(me_x + k, size_x), me_y) for k in range(1, size_x)]
    peers += [(me_x, lax.rem(me_y + k, size_y)) for k in range(1, size_y)]
    peers += [
        (lax.rem(me_x + dx + size_x, size_x), lax.rem(me_y + dy + size_y, size_y))
        for dx in (-1, 1)
        for dy in (-1, 1)
    ]
    barrier = pltpu.get_barrier_semaphore()
    for peer in peers:
        pl.semaphore_signal(barrier, inc=1, device_id=peer, device_id_type=MESH)
    for ext, block in (
        (f_ext, field), (g_ext, cotangent), (k_ext, kappa),
        (v0_ext, vel.at[0]), (v1_ext, vel.at[1]),
    ):
        ext[OWN_ROWS, OWN_LANES] = block[...]
    pl.semaphore_wait(barrier, len(peers))

    sides_x, sides_y = ((-1, 0), (1, 0)), ((0, -1), (0, 1))
    send = lambda ext, number, around: copies_around(
        ext, send_sem, recv_sem, number, gx, gy, around
    )
    field_copies = send(f_ext, 0, AROUND)
    g_copies = send(g_ext, 1, AROUND)
    late = send(k_ext, 2, sides_x + sides_y)
    late += send(v0_ext, 3, sides_x) + send(v1_ext, 4, sides_y)

    for copy in field_copies:
        copy.wait_recv()
    first_one = forward(f_ext, b0, bias_in, w_fwd, bias_mid, stack_one, two_one)
    f1_ext[OWN_ROWS, OWN_LANES] = stepped(f_ext, kappa, vel, bf, two_one)
    field_one_copies = send(f1_ext, 5, AROUND)

    for copy in field_one_copies:
        copy.wait_recv()
    first_two = forward(f1_ext, b0, bias_in, w_fwd, bias_mid, stack_two, two_two)

    for copy in g_copies:
        copy.wait_recv()
    pair = cotangent_two(g_ext, bb, two_two, grad_two)
    cotangent_one(w_bwd, stack_two, grad_two, grad_stack, grad_one)
    for copy in late:
        copy.wait_recv()
    a_ext[OWN_ROWS, OWN_LANES] = previous(g_ext, k_ext, v0_ext, v1_ext, vel, bq, grad_one)
    adjoint_copies = send(a_ext, 6, AROUND)
    mid_two, bias_mid_two, out_two = middle_terms(pair, stack_two, two_two, grad_two, spread)
    in_two, bias_in_two = first_terms(first_two, grad_one)

    for copy in adjoint_copies:
        copy.wait_recv()
    pair = cotangent_two(a_ext, bb, two_one, grad_two)
    mid_one, bias_mid_one, out_one = middle_terms(pair, stack_one, two_one, grad_two, spread)
    cotangent_one(w_bwd, stack_one, grad_two, grad_stack, grad_one)
    in_one, bias_in_one = first_terms(first_one, grad_one)

    mid = mid_one + mid_two
    sums[:, 0 : 3 * C] = mid[0 : 8 * C]
    for number in range(3):
        sums[number * C : (number + 1) * C, 3 * C :] = mid[
            8 * C : 9 * C, number * C : (number + 1) * C
        ]
    sums[96:123, 3 * C :] = in_one + in_two
    columns = [bias_in_one + bias_in_two, bias_mid_one + bias_mid_two]
    columns += [one + two for one, two in zip(out_one, out_two)]
    lane = lax.broadcasted_iota(jnp.int32, (C, C), 1)
    block = jnp.zeros((C, C), f32)
    for number, column in enumerate(columns):
        block = jnp.where(lane == number, jnp.broadcast_to(column, (C, C)), block)
    sums[128:160, 3 * C :] = block

    part = sums.shape[0] // size_x
    mine = pl.ds(pl.multiple_of(me_x * part, part), part)
    scatter = []
    for k in range(1, size_x):
        peer = lax.rem(me_x + k, size_x)
        copy = pltpu.make_async_remote_copy(
            src_ref=sums.at[pl.ds(pl.multiple_of(peer * part, part), part)],
            dst_ref=recv_x.at[k],
            send_sem=sum_send.at[0, k],
            recv_sem=sum_recv.at[0, k],
            device_id=(peer, me_y),
            device_id_type=MESH,
        )
        copy.start()
        scatter.append(copy)
    out_field[...] = previous(a_ext, k_ext, v0_ext, v1_ext, vel, bq, grad_one)
    total = sums[mine, :]
    for k, copy in enumerate(scatter):
        copy.wait_recv()
        total = total + recv_x[k + 1]
    recv_y[me_y] = total
    exchange = []
    for k in range(1, size_y):
        copy = pltpu.make_async_remote_copy(
            src_ref=recv_y.at[me_y],
            dst_ref=recv_y.at[me_y],
            send_sem=sum_send.at[1, k],
            recv_sem=sum_recv.at[1, k],
            device_id=(me_x, lax.rem(me_y + k, size_y)),
            device_id_type=MESH,
        )
        copy.start()
        exchange.append(copy)
    for copy in exchange:
        copy.wait_recv()
    total = recv_y[0]
    for k in range(1, size_y):
        total = total + recv_y[k]
    gathered[mine, :] = total * scale
    gather = []
    for k in range(1, size_x):
        copy = pltpu.make_async_remote_copy(
            src_ref=gathered.at[mine],
            dst_ref=gathered.at[mine],
            send_sem=sum_send.at[2, k],
            recv_sem=sum_recv.at[2, k],
            device_id=(lax.rem(me_x + k, size_x), me_y),
            device_id_type=MESH,
        )
        copy.start()
        gather.append(copy)
    for copy in gather:
        copy.wait_recv()

    for a in range(3):
        for b in range(3):
            for c in range(3):
                row = (a * 3 + c) * C
                if row < 8 * C:
                    value = gathered[row : row + C, b * C : (b + 1) * C]
                else:
                    value = gathered[b * C : (b + 1) * C, 3 * C :]
                out_mid[a * 9 + b * 3 + c] = value
    out_in[...] = gathered[96:123, 3 * C :]
    block = gathered[128:160, 3 * C :]
    out_bias_in[...] = column_to_row(block[:, 0:1])
    out_bias_mid[...] = column_to_row(block[:, 1:2])
    out_out[...] = block[:, 2:5]

    everything = field_copies + g_copies + late + field_one_copies + adjoint_copies
    for copy in everything + scatter + exchange + gather:
        copy.wait_send()


def band(rows, cols, place):
    out = np.zeros((3, rows, cols), np.float32)
    for a in range(3):
        for row in range(rows):
            if 0 <= place(row, a) < cols:
                out[a, row, place(row, a)] = 1.0
    return jnp.asarray(out, bf16)


def prepared(conv_in, conv_mid, flux_out):
    first = conv_in.reshape(3, 9, C)
    exact = dict(preferred_element_type=bf16)
    b0 = jnp.einsum("aij,asc->icsj", band(14, 16, lambda i, a: i + a), first, **exact)
    bq = jnp.einsum("axi,asc->sxic", band(8, 10, lambda x, a: x + 2 - a), first, **exact)
    middle = conv_mid.reshape(3, 3, 3, C, C)
    w_fwd = jnp.einsum("axi,abzcd->xbdizc", band(3, 5, lambda x, a: x + a), middle, **exact)
    w_bwd = jnp.einsum("axi,abzcd->xbcizd", band(3, 5, lambda x, a: x + 2 - a), middle, **exact)
    halves = np.zeros((3, 8, 12), np.float32)
    for x in range(8):
        halves[0, x, x + 3], halves[0, x, x + 1] = 0.5, -0.5
        halves[1, x, x + 2] = halves[2, x, x + 2] = 1.0
    bf = jnp.einsum("dxi,cd->dxic", jnp.asarray(halves, bf16), flux_out, **exact)
    pick = np.zeros((2, 12, 16), np.float32)
    for i in range(12):
        pick[:, i, i + 2] = 1.0
    bb = jnp.einsum("hij,cd->ichdj", jnp.asarray(pick, bf16), flux_out, **exact)
    return (
        b0.reshape(14 * C, 144),
        w_fwd.reshape(288, 480),
        bf.reshape(24, 12 * C),
        bb.reshape(12 * C, 96),
        w_bwd.reshape(288, 480),
        bq.reshape(72, 320),
    )


def solution(mesh):
    size_x, size_y = mesh.shape["gx"], mesh.shape["gy"]

    def shards(
        scalar_field, field_cotangent, diffusivity, velocity,
        conv_in, bias_in, conv_mid, bias_mid, flux_out,
    ):
        cells = scalar_field.size * size_x * size_y
        b0, w_fwd, bf, bb, w_bwd, bq = prepared(conv_in, conv_mid, flux_out)
        vmem = pl.BlockSpec(memory_space=pltpu.VMEM)
        ext = pltpu.VMEM((TALL, WIDE), f32)
        part = 256 // size_x
        outs = pl.pallas_call(
            lambda *refs: kernel(size_x, size_y, 1.0 / math.sqrt(cells), *refs),
            out_shape=[
                jax.ShapeDtypeStruct((ROWS, LANES), f32),
                jax.ShapeDtypeStruct((27, C), f32),
                jax.ShapeDtypeStruct((1, C), f32),
                jax.ShapeDtypeStruct((27, C, C), f32),
                jax.ShapeDtypeStruct((1, C), f32),
                jax.ShapeDtypeStruct((C, 3), f32),
            ],
            in_specs=[vmem] * 12,
            out_specs=[vmem] * 6,
            scratch_shapes=[
                ext, ext, ext, ext, ext, ext, ext,
                pltpu.VMEM((14, 3 * C, WIDE), bf16),
                pltpu.VMEM((14, 3 * C, WIDE), bf16),
                pltpu.VMEM((12, C, WIDE), bf16),
                pltpu.VMEM((12, C, WIDE), bf16),
                pltpu.VMEM((12, C, WIDE), bf16),
                pltpu.VMEM((8, 3 * C, WIDE), bf16),
                pltpu.VMEM((12, 3 * C, WIDE), bf16),
                pltpu.VMEM((10, C, WIDE), bf16),
                pltpu.VMEM((256, 128), f32),
                pltpu.VMEM((size_x, part, 128), f32),
                pltpu.VMEM((size_y, part, 128), f32),
                pltpu.VMEM((256, 128), f32),
                pltpu.SemaphoreType.DMA((7, 8)),
                pltpu.SemaphoreType.DMA((7, 8)),
                pltpu.SemaphoreType.DMA((3, max(size_x, size_y))),
                pltpu.SemaphoreType.DMA((3, max(size_x, size_y))),
            ],
            compiler_params=pltpu.CompilerParams(
                collective_id=0, has_side_effects=True, vmem_limit_bytes=48 * 1024 * 1024
            ),
        )(
            scalar_field, field_cotangent, diffusivity, velocity,
            b0, bias_in.reshape(C, 1), w_fwd, bias_mid.reshape(C, 1), bf, bb, w_bwd, bq,
        )
        return (outs[0], outs[1], outs[2].reshape(C), outs[3], outs[4].reshape(C), outs[5])

    return jax.shard_map(
        shards,
        mesh=mesh,
        in_specs=(
            P("gx", "gy"), P("gx", "gy"), P("gx", "gy"), P(None, "gx", "gy"),
            P(), P(), P(), P(), P(),
        ),
        out_specs=(P("gx", "gy"), P(), P(), P(), P(), P()),
        check_vma=False,
    )
```

```python
import math

import jax
import jax.numpy as jnp
from jax import lax
from jax.experimental import pallas as pl
from jax.experimental.pallas import tpu as pltpu
from jax.sharding import PartitionSpec as P

NZ = 32
C = 32
ROWS = 8
LANES = 512
HALO = 128
WIDE = LANES + 2 * HALO
TALL = 3 * ROWS
time_step = 0.2
MESH = pl.DeviceIdType.MESH
STEPS = (-1, 0, 1)
AROUND = tuple((dx, dy) for dx in STEPS for dy in STEPS if (dx, dy) != (0, 0))
OWN_ROWS = slice(ROWS, 2 * ROWS)
OWN_LANES = slice(HALO, HALO + LANES)
bf16 = jnp.bfloat16
f32 = jnp.float32


def shifted(values, count):
    if count == 0:
        return values
    return pltpu.roll(values, (-count) % values.shape[-1], axis=values.ndim - 1)


def lane_index(values):
    return lax.broadcasted_iota(jnp.int32, values.shape, values.ndim - 1)


def lifted(values, step_z):
    if step_z == 0:
        return values
    edge = NZ - 1 if step_z == 1 else 0
    moved = shifted(values, step_z)
    return jnp.where(lane_index(values) % NZ == edge, jnp.zeros_like(moved), moved)


def own_lanes_only(values):
    lane = lane_index(values)
    return jnp.where((lane >= HALO) & (lane < HALO + LANES), values, jnp.zeros_like(values))


def dot(left, right):
    return lax.dot_general(left, right, (((1,), (0,)), ((), ())), preferred_element_type=f32)


def dot_lanes(left, right):
    return lax.dot_general(left, right, (((1,), (1,)), ((), ())), preferred_element_type=f32)


def central_y(values):
    return 0.5 * (shifted(values, NZ) - shifted(values, -NZ))


def central_z(values):
    return 0.5 * (lifted(values, 1) - lifted(values, -1))


def column_to_row(column):
    size = column.shape[0]
    wide = jnp.broadcast_to(column, (size, size))
    row = lax.broadcasted_iota(jnp.int32, (size, size), 0)
    col = lax.broadcasted_iota(jnp.int32, (size, size), 1)
    return jnp.sum(jnp.where(row == col, wide, 0.0), axis=0, keepdims=True)


def first_stack(field_ext):
    rounded = field_ext[...].astype(bf16).astype(f32)
    moves = [lifted(shifted(rounded, NZ * b), c) for b in STEPS for c in STEPS]
    stack = jnp.concatenate(moves, axis=0).astype(bf16)
    margin = (stack.shape[1] - WIDE) // 2
    return stack[:, margin : margin + WIDE]


def z_stack(values, target, sign, start):
    count = values.shape[0] // C
    wide = values.astype(f32)
    for number, c in enumerate(STEPS):
        moved = lifted(wide, sign * c).astype(bf16) if c else values
        target[start : start + count, number * C : (number + 1) * C, :] = moved.reshape(
            count, C, WIDE
        )


def middle_conv(weights, stack, start, sign):
    window = stack[start : start + 5].reshape(5 * 3 * C, WIDE)
    out = dot(weights[...], window).reshape(3, 3, C, WIDE)
    result = out[:, 1]
    for number, b in ((0, -1), (2, 1)):
        part = out[:, number].reshape(3 * C, WIDE)
        result = result + shifted(part, sign * NZ * b).reshape(3, C, WIDE)
    return result


def forward(field_ext, near, weights, stack, hidden_two):
    b0, bias_in, w_fwd, bias_mid = weights
    first = first_stack(field_ext)
    low, high = (1, 15) if near else (0, 16)
    pre = dot(b0[low * C : high * C, :], first).reshape(high - low, C, WIDE)
    hidden_one = jnp.tanh(pre + bias_in[...][None]).astype(bf16)
    z_stack(hidden_one.reshape((high - low) * C, WIDE), stack, 1, low)
    for start in (1, 4, 7, 10) if near else (0, 3, 6, 9, 11):
        pre = middle_conv(w_fwd, stack, start, 1)
        hidden_two[start : start + 3] = jnp.tanh(pre + bias_mid[...][None]).astype(bf16)
    return first


def stepped(field_ext, kv_ext, bf, hidden_two):
    flux = dot(bf[...], hidden_two[1:13].reshape(12 * C, WIDE))
    correction = flux[0:8] + central_y(flux[8:16]) + central_z(flux[16:24])
    here, up, down = field_ext[8:16, :], field_ext[9:17, :], field_ext[7:15, :]
    laplace = (
        up + down + shifted(here, NZ) + shifted(here, -NZ) + lifted(here, 1) + lifted(here, -1)
    )
    laplace = laplace - 6.0 * here
    own = lambda values: values[:, OWN_LANES]
    cell = lambda number: kv_ext[number, OWN_ROWS, OWN_LANES]
    physics = cell(0) * own(laplace)
    physics = physics - cell(1) * own(0.5 * (up - down))
    physics = physics - cell(2) * own(central_y(here))
    physics = physics - cell(3) * own(central_z(here))
    return own(here) + time_step * (physics + own(correction))


def row_moved(values, count):
    return pltpu.roll(values, (-count) % values.shape[0], axis=0)


def flux_pair(here):
    parts = [
        -0.5 * time_step * (row_moved(here, 1) - row_moved(here, -1)),
        -time_step * central_y(here),
        -time_step * central_z(here),
    ]
    flux = jnp.concatenate(parts, axis=0)
    high = flux.astype(bf16)
    low = (flux - high.astype(f32)).astype(bf16)
    return jnp.concatenate([high, low], axis=0)


def cotangent_two(back, hidden_two, low, high):
    two = hidden_two[low:high].astype(f32)
    return (back.reshape(high - low, C, WIDE) * (1.0 - two * two)).astype(bf16)


def middle_terms(stack, own_two, spread):
    own = own_lanes_only(own_two.astype(f32))
    for number, b in enumerate(STEPS):
        moved = shifted(own, -NZ * b).astype(bf16)
        spread[:, number * C : (number + 1) * C, :] = moved.reshape(8, C, WIDE)
    term_mid = jnp.zeros((9 * C, 3 * C), f32)
    for x in range(ROWS):
        window = stack[x + 3 : x + 6].reshape(9 * C, WIDE)
        term_mid = term_mid + dot_lanes(window, spread[x])
    return term_mid


def out_terms(pair, hidden_two, own_two):
    own = own_lanes_only(own_two.astype(f32))
    bias_mid = jnp.sum(jnp.sum(own.reshape(8, C, WIDE), axis=0), axis=1, keepdims=True)
    masked = own_lanes_only(pair.astype(f32)).astype(bf16)
    outer = dot_lanes(hidden_two[3:11].reshape(8 * C, WIDE), masked)
    row_x = lax.broadcasted_iota(jnp.int32, outer.shape, 0) // C
    col = lax.broadcasted_iota(jnp.int32, outer.shape, 1)
    outer = jnp.where(col % 16 == row_x + 4, outer, 0.0)
    outer = jnp.sum(outer.reshape(8, C, outer.shape[1]), axis=0)
    kind = (lax.broadcasted_iota(jnp.int32, outer.shape, 1) // 16) % 3
    columns = [jnp.sum(jnp.where(kind == d, outer, 0.0), axis=1, keepdims=True) for d in range(3)]
    return [column_to_row(column) for column in [bias_mid] + columns]


def cotangent_one(w_bwd, stack, grad_stack, grad_one, starts):
    for start in starts:
        back = middle_conv(w_bwd, grad_stack, start, -1)
        one = stack[start + 2 : start + 5, C : 2 * C, :].astype(f32)
        grad_one[start : start + 3] = (back * (1.0 - one * one)).astype(bf16)


def first_terms(first, grad_one):
    own = own_lanes_only(grad_one[2:10].reshape(8 * C, WIDE).astype(f32))
    outer = dot_lanes(first, own.astype(bf16))
    row_x = lax.broadcasted_iota(jnp.int32, outer.shape, 0) % TALL
    col_x = lax.broadcasted_iota(jnp.int32, outer.shape, 1) // C
    parts = []
    for a in range(3):
        kept = jnp.where(row_x - col_x == a + 7, outer, 0.0)
        parts.append(jnp.sum(kept.reshape(9, TALL, 8 * C), axis=1))
    folded = jnp.concatenate(parts, axis=0)
    folded = folded[:, :128] + folded[:, 128:]
    folded = folded + pltpu.roll(folded, 64, axis=1)
    folded = folded + pltpu.roll(folded, 32, axis=1)
    bias_in = jnp.sum(jnp.sum(own.reshape(8, C, WIDE), axis=0), axis=1, keepdims=True)
    return folded[:, :C], column_to_row(bias_in)


def previous(here, kv_ext, bq, grad_one):
    spread = dot(bq[...], grad_one[...].reshape(12 * C, WIDE))
    total = 0.0
    for number, (b, c) in enumerate([(b, c) for b in STEPS for c in STEPS]):
        total = total + lifted(shifted(spread[number * 16 : number * 16 + 16], -NZ * b), -c)
    cell = lambda number: kv_ext[number, 4:20, :]
    scaled = cell(0) * here
    physics = row_moved(scaled, 1) + row_moved(scaled, -1) - 6.0 * scaled
    physics = physics + shifted(scaled, NZ) + shifted(scaled, -NZ)
    physics = physics + lifted(scaled, 1) + lifted(scaled, -1)
    scaled = cell(1) * here
    physics = physics + 0.5 * (row_moved(scaled, 1) - row_moved(scaled, -1))
    physics = physics + central_y(cell(2) * here) + central_z(cell(3) * here)
    return here + time_step * physics + total


def iota(shape, dimension):
    return lax.broadcasted_iota(jnp.int32, shape, dimension)


def ones_where(condition):
    return jnp.where(condition, 1.0, 0.0).astype(bf16)


def dot_rows(left, right):
    return lax.dot_general(left, right, (((0,), (0,)), ((), ())), preferred_element_type=f32)


def place_middle(conv_mid, wide, w_fwd, w_bwd):
    for target, backward in ((w_fwd, False), (w_bwd, True)):
        wide[...] = jnp.zeros_like(wide)
        for a in range(3):
            for b in range(3):
                for c in range(3):
                    block = conv_mid[a * 9 + b * 3 + c].astype(f32)
                    if not backward:
                        block = block.T
                    for x in range(3):
                        row = (x * 3 + b) * C
                        col = ((x + (2 - a if backward else a)) * 3 + c) * C
                        wide[row : row + C, col : col + C] = block
        target[...] = wide[...].astype(bf16)


def place_first(conv_in, b0, bq):
    taps = conv_in[...]
    shape = (27, 9 * TALL)
    spread = []
    for a in range(3):
        pick = ones_where(iota(shape, 0) == iota(shape, 1) // TALL + 9 * a)
        spread.append(dot_rows(taps, pick))
    j = iota(spread[0].shape, 1) % TALL
    for i in range(16):
        rows = sum(jnp.where(j == 3 + i + a, spread[a], 0.0) for a in range(3))
        b0[i * C : (i + 1) * C, :] = rows.astype(bf16)
    shape = (C, 12 * C)
    tiled = dot(taps, ones_where(iota(shape, 1) % C == iota(shape, 0))).astype(bf16)
    total = 0.0
    for a in range(3):
        pick = ones_where(iota((144, 27), 1) == iota((144, 27), 0) // 16 + 9 * a)
        rows = dot(pick, tiled)
        kept = iota(rows.shape, 1) // C == iota(rows.shape, 0) % 16 - a - 1
        total = total + jnp.where(kept, rows, 0.0)
    bq[...] = total.astype(bf16)


def place_flux(flux, bf, bb):
    taps = flux[...]
    shape = (C, 12 * C)
    tiled = dot(taps, ones_where(iota(shape, 1) % C == iota(shape, 0))).astype(bf16)
    rows = dot(ones_where(iota((24, 3), 1) == iota((24, 3), 0) // 8), tiled)
    x, i = iota(rows.shape, 0) % 8, iota(rows.shape, 1) // C
    first = iota(rows.shape, 0) < 8
    factor = jnp.where(i == x + 3, 0.5, jnp.where(i == x + 1, -0.5, 0.0))
    factor = jnp.where(first, factor, jnp.where(i == x + 2, 1.0, 0.0))
    bf[...] = (rows * factor).astype(bf16)
    pick = ones_where(iota((3, 96), 0) == (iota((3, 96), 1) // 16) % 3)
    columns = dot_rows(taps, pick)
    j = iota(columns.shape, 1) % 16
    for i in range(14):
        bb[i * C : (i + 1) * C, :] = jnp.where(j == i + 1, columns, 0.0).astype(bf16)


def row_to_column(row):
    size = row.shape[1]
    wide = jnp.broadcast_to(row, (size, size))
    return jnp.sum(
        jnp.where(iota((size, size), 0) == iota((size, size), 1), wide, 0.0),
        axis=1,
        keepdims=True,
    )


def remote(source, target, sems, peer):
    copy = pltpu.make_async_remote_copy(
        src_ref=source,
        dst_ref=target,
        send_sem=sems[0],
        recv_sem=sems[1],
        device_id=peer,
        device_id_type=MESH,
    )
    copy.start()


def send_around(ext, sems, place):
    (me_x, size_x), (me_y, size_y) = place
    width = ext.shape[-1]
    side = (width - LANES) // 2
    lead = (slice(None),) * (len(ext.shape) - 2)
    sources = {0: slice(side, side + LANES), 1: slice(LANES, side + LANES), -1: slice(side, 2 * side)}
    targets = {0: slice(side, side + LANES), 1: slice(0, side), -1: slice(side + LANES, width)}
    rows = {0: OWN_ROWS, 1: slice(0, ROWS), -1: slice(2 * ROWS, TALL)}
    for dx, dy in AROUND:
        peer = (
            lax.rem(me_x + dx + size_x, size_x),
            lax.rem(me_y + dy + size_y, size_y),
        )
        source = ext.at[lead + (OWN_ROWS, sources[dy])]
        remote(source, ext.at[lead + (rows[dx], targets[dy])], sems, peer)
    depth = ext.shape[0] if lead else 1
    return depth * (3 * width - LANES) // 128


def wait_tiles(sem, gauge, count):
    part = gauge.at[pl.ds(0, 8 * count)]
    pltpu.make_async_copy(part, part, sem).wait()


def kernel(
    size_x, size_y, scale,
    field, cotangent, kappa, vel, conv_in_in, bias_in_in, conv_mid_in, bias_mid_in, flux_in,
    out_field, out_sums, out_small,
    f_ext, f1_ext, g_ext, a_ext, kv_ext, conv_in, bias_in_row, conv_mid, bias_mid_row, flux,
    bias_in, bias_mid, wide, b0, w_fwd, bf, bb, w_bwd, bq,
    stack_one, stack_two, two_one, two_two, back_two, spread, grad_stack, grad_one,
    sums, recv_x, recv_y, gathered, small, small_x, small_y, gauge,
    local_sem, send_sem, recv_sem,
):
    me_x, me_y = lax.axis_index("gx"), lax.axis_index("gy")
    place = (me_x, size_x), (me_y, size_y)
    half_x, half_y = size_x // 2, size_y // 2
    mine_hi = lax.div(me_y, half_y)
    peers_x = [(lax.rem(me_x + k, size_x), me_y) for k in range(1, size_x)]
    peers_y = []
    for k in range(1, size_y):
        other = lax.rem(me_y + k, size_y)
        flip = lax.rem(mine_hi + lax.div(other, half_y), 2) * half_x
        peers_y.append((lax.rem(me_x + flip, size_x), other))
    near = [
        (lax.rem(me_x + dx + size_x, size_x), lax.rem(me_y + dy + size_y, size_y))
        for dx, dy in AROUND
        if dy != 0
    ]
    barrier = pltpu.get_barrier_semaphore()
    for peer in near + peers_x + peers_y:
        pl.semaphore_signal(barrier, inc=1, device_id=peer, device_id_type=MESH)
    own = (OWN_ROWS, OWN_LANES)
    arrivals = []
    for source, target in (
        (field, f_ext.at[own]),
        (cotangent, g_ext.at[own]),
        (kappa, kv_ext.at[(0,) + own]),
        (vel, kv_ext.at[(slice(1, 4),) + own]),
        (conv_in_in, conv_in),
        (bias_in_in, bias_in_row),
        (conv_mid_in, conv_mid),
        (bias_mid_in, bias_mid_row),
        (flux_in, flux),
    ):
        copy = pltpu.make_async_copy(source, target, local_sem.at[len(arrivals)])
        copy.start()
        arrivals.append(copy)
    for copy in arrivals:
        copy.wait()
    sems = lambda number: (send_sem.at[number], recv_sem.at[number])
    pl.semaphore_wait(barrier, len(near + peers_x + peers_y))
    tiles = [send_around(f_ext, sems(0), place), send_around(g_ext, sems(1), place)]
    tiles.append(send_around(kv_ext, sems(2), place))

    bias_in[...] = row_to_column(bias_in_row[...])
    bias_mid[...] = row_to_column(bias_mid_row[...])
    place_first(conv_in, b0, bq)
    place_middle(conv_mid, wide, w_fwd, w_bwd)
    place_flux(flux, bf, bb)

    weights = (b0, bias_in, w_fwd, bias_mid)
    wait_tiles(recv_sem.at[0], gauge, tiles[0])
    first_one = forward(f_ext, True, weights, stack_one, two_one)
    f1_ext[OWN_ROWS, 256 : 256 + LANES] = stepped(f_ext, kv_ext, bf, two_one)
    tiles.append(send_around(f1_ext, sems(3), place))

    wait_tiles(recv_sem.at[1], gauge, tiles[1])
    pair_two = flux_pair(g_ext[4:20, :])
    back_two[...] = dot(bb[...], pair_two)
    wait_tiles(recv_sem.at[3], gauge, tiles[3])
    first_two = forward(f1_ext, False, weights, stack_two, two_two)

    grad_two = cotangent_two(back_two[...], two_two, 0, 14).reshape(14 * C, WIDE)
    z_stack(grad_two, grad_stack, -1, 0)
    cotangent_one(w_bwd, stack_two, grad_stack, grad_one, (0, 3, 6, 9))
    wait_tiles(recv_sem.at[2], gauge, tiles[2])
    adjoint = previous(g_ext[4:20, :], kv_ext, bq, grad_one)
    a_ext[own] = adjoint[4:12, OWN_LANES]
    tiles.append(send_around(a_ext, sems(4), place))

    own_two = grad_two[3 * C : 11 * C]
    mid = middle_terms(stack_two, own_two, spread)
    pair_one = flux_pair(adjoint)
    own_one = cotangent_two(dot(bb[3 * C : 11 * C, :], pair_one), two_one, 3, 11)
    own_one = own_one.reshape(8 * C, WIDE)
    mid = mid + middle_terms(stack_one, own_one, spread)
    sums[:, 0 : 3 * C] = mid[0 : 8 * C]
    for number in range(3):
        sums[number * C : (number + 1) * C, 3 * C :] = mid[
            8 * C : 9 * C, number * C : (number + 1) * C
        ]
    sums[3 * C :, 3 * C :] = jnp.zeros((5 * C, C), f32)

    part = sums.shape[0] // size_x
    share = lambda x: pl.ds(
        pl.multiple_of(lax.rem(x + mine_hi * half_x, size_x) * part, part), part
    )
    for peer in peers_x:
        remote(sums.at[share(peer[0])], recv_x.at[me_x], sems(5), peer)

    in_two, bias_in_two = first_terms(first_two, grad_one)
    rows_two = out_terms(pair_two, two_two, own_two)
    rows_one = out_terms(pair_one, two_one, own_one)
    wait_tiles(recv_sem.at[4], gauge, tiles[4])
    here = a_ext[4:20, :]
    full = cotangent_two(dot(bb[C : 13 * C, :], flux_pair(here)), two_one, 1, 13)
    z_stack(full.reshape(12 * C, WIDE), grad_stack, -1, 1)
    cotangent_one(w_bwd, stack_one, grad_stack, grad_one, (1, 4, 7, 8))
    in_one, bias_in_one = first_terms(first_one, grad_one)
    matrix = jnp.concatenate(
        [in_one + in_two, bias_in_one + bias_in_two]
        + [one + two for one, two in zip(rows_one, rows_two)],
        axis=0,
    )
    for number in range(4):
        small[:, number * C : (number + 1) * C] = matrix[number * 8 : number * 8 + 8]
    small_x[me_x] = small[...]

    per = part // 8
    wait_tiles(recv_sem.at[5], gauge, per * (size_x - 1))
    recv_x[me_x] = sums[share(me_x), :]
    total = recv_x[0]
    for k in range(1, size_x):
        total = total + recv_x[k]
    recv_y[me_y] = total
    for peer in peers_y:
        remote(recv_y.at[me_y], recv_y.at[me_y], sems(6), peer)
    for peer in peers_x:
        remote(small, small_x.at[me_x], sems(8), peer)

    final = previous(here, kv_ext, bq, grad_one)
    out_field[...] = final[4:12, OWN_LANES]

    wait_tiles(recv_sem.at[8], gauge, size_x - 1)
    total = small_x[0]
    for k in range(1, size_x):
        total = total + small_x[k]
    small_y[me_y] = total
    for peer in peers_y:
        remote(small_y.at[me_y], small_y.at[me_y], sems(9), peer)

    wait_tiles(recv_sem.at[6], gauge, per * (size_y - 1))
    total = recv_y[0]
    for k in range(1, size_y):
        total = total + recv_y[k]
    gathered[share(me_x), :] = total * scale
    for peer in peers_x:
        remote(gathered.at[share(me_x)], gathered.at[share(me_x)], sems(7), peer)

    wait_tiles(recv_sem.at[9], gauge, size_y - 1)
    total = small_y[0]
    for k in range(1, size_y):
        total = total + small_y[k]
    out_small[...] = total * scale
    wait_tiles(recv_sem.at[7], gauge, per * (size_x - 1))
    out_sums[...] = gathered[...]

    for number in range(5):
        wait_tiles(send_sem.at[number], gauge, tiles[number])
    wait_tiles(send_sem.at[5], gauge, per * (size_x - 1))
    wait_tiles(send_sem.at[6], gauge, per * (size_y - 1))
    wait_tiles(send_sem.at[7], gauge, per * (size_x - 1))
    wait_tiles(send_sem.at[8], gauge, size_x - 1)
    wait_tiles(send_sem.at[9], gauge, size_y - 1)


def unpack(field, sums, small, out_field, out_in, out_bias_in, out_mid, out_bias_mid, out_out):
    out_field[...] = field[...]
    for a in range(3):
        for b in range(3):
            for c in range(3):
                row = (a * 3 + c) * C
                if row < 8 * C:
                    value = sums[row : row + C, b * C : (b + 1) * C]
                else:
                    value = sums[b * C : (b + 1) * C, 3 * C :]
                out_mid[a * 9 + b * 3 + c] = value
    for number in range(3):
        out_in[number * 8 : number * 8 + 8] = small[:, number * C : (number + 1) * C]
    last = small[:, 3 * C :]
    out_in[24:27] = last[0:3]
    out_bias_in[...] = last[3:4]
    out_bias_mid[...] = last[4:5]
    out_out[...] = last[5:8]


def solution(mesh):
    size_x, size_y = mesh.shape["gx"], mesh.shape["gy"]

    def shards(
        scalar_field, field_cotangent, diffusivity, velocity,
        conv_in, bias_in, conv_mid, bias_mid, flux_out,
    ):
        cells = scalar_field.size * size_x * size_y
        vmem = pl.BlockSpec(memory_space=pltpu.VMEM)
        anywhere = pl.BlockSpec(memory_space=pltpu.HBM)
        part = 256 // size_x
        ext = pltpu.VMEM((TALL, WIDE), f32)
        shape = jax.ShapeDtypeStruct
        outs = pl.pallas_call(
            lambda *refs: kernel(size_x, size_y, 1.0 / math.sqrt(cells), *refs),
            out_shape=[shape((ROWS, LANES), f32), shape((256, 128), f32), shape((8, 128), f32)],
            in_specs=[anywhere] * 9,
            out_specs=[vmem] * 3,
            scratch_shapes=[
                ext, pltpu.VMEM((TALL, WIDE + 256), f32), ext, ext,
                pltpu.VMEM((4, TALL, WIDE), f32),
                pltpu.VMEM((27, C), bf16),
                pltpu.VMEM((1, C), f32),
                pltpu.VMEM((27, C, C), bf16),
                pltpu.VMEM((1, C), f32),
                pltpu.VMEM((3, C), bf16),
                pltpu.VMEM((C, 1), f32),
                pltpu.VMEM((C, 1), f32),
                pltpu.VMEM((288, 480), f32),
                pltpu.VMEM((16 * C, 9 * TALL), bf16),
                pltpu.VMEM((288, 480), bf16),
                pltpu.VMEM((24, 12 * C), bf16),
                pltpu.VMEM((14 * C, 96), bf16),
                pltpu.VMEM((288, 480), bf16),
                pltpu.VMEM((144, 12 * C), bf16),
                pltpu.VMEM((16, 3 * C, WIDE), bf16),
                pltpu.VMEM((16, 3 * C, WIDE), bf16),
                pltpu.VMEM((14, C, WIDE), bf16),
                pltpu.VMEM((14, C, WIDE), bf16),
                pltpu.VMEM((14 * C, WIDE), f32),
                pltpu.VMEM((8, 3 * C, WIDE), bf16),
                pltpu.VMEM((14, 3 * C, WIDE), bf16),
                pltpu.VMEM((12, C, WIDE), bf16),
                pltpu.VMEM((256, 128), f32),
                pltpu.VMEM((size_x, part, 128), f32),
                pltpu.VMEM((size_y, part, 128), f32),
                pltpu.VMEM((256, 128), f32),
                pltpu.VMEM((8, 128), f32),
                pltpu.VMEM((size_x, 8, 128), f32),
                pltpu.VMEM((size_y, 8, 128), f32),
                pltpu.VMEM((448, 128), f32),
                pltpu.SemaphoreType.DMA((9,)),
                pltpu.SemaphoreType.DMA((10,)),
                pltpu.SemaphoreType.DMA((10,)),
            ],
            compiler_params=pltpu.CompilerParams(
                collective_id=0, has_side_effects=True, vmem_limit_bytes=60 * 1024 * 1024
            ),
        )(
            scalar_field, field_cotangent, diffusivity, velocity,
            conv_in, bias_in.reshape(1, C), conv_mid, bias_mid.reshape(1, C), flux_out.T,
        )
        outs = pl.pallas_call(
            unpack,
            out_shape=[
                shape((ROWS, LANES), f32),
                shape((27, C), f32),
                shape((1, C), f32),
                shape((27, C, C), f32),
                shape((1, C), f32),
                shape((3, C), f32),
            ],
            in_specs=[vmem] * 3,
            out_specs=[vmem] * 6,
        )(*outs)
        return (outs[0], outs[1], outs[2].reshape(C), outs[3], outs[4].reshape(C), outs[5].T)

    return jax.shard_map(
        shards,
        mesh=mesh,
        in_specs=(
            P("gx", "gy"), P("gx", "gy"), P("gx", "gy"), P(None, "gx", "gy"),
            P(), P(), P(), P(), P(),
        ),
        out_specs=(P("gx", "gy"), P(), P(), P(), P(), P()),
        check_vma=False,
    )
```

```python
import math

import jax
import jax.numpy as jnp
from jax import lax
from jax.experimental import pallas as pl
from jax.experimental.pallas import tpu as pltpu
from jax.sharding import PartitionSpec as P

NZ = 32
C = 32
ROWS = 8
LANES = 512
HALO = 128
WIDE = LANES + 2 * HALO
TALL = 3 * ROWS
BROAD = WIDE + 256
MIDDLE = slice(128, 128 + WIDE)
time_step = 0.2
MESH = pl.DeviceIdType.MESH
STEPS = (-1, 0, 1)
AROUND = ((1, 1), (1, -1), (-1, 1), (-1, -1), (0, 1), (0, -1), (1, 0), (-1, 0))
OWN_ROWS = slice(ROWS, 2 * ROWS)
OWN_LANES = slice(HALO, HALO + LANES)
bf16 = jnp.bfloat16
f32 = jnp.float32


def shifted(values, count):
    if count == 0:
        return values
    return pltpu.roll(values, (-count) % values.shape[-1], axis=values.ndim - 1)


def lane_index(values):
    return lax.broadcasted_iota(jnp.int32, values.shape, values.ndim - 1)


def lifted(values, step_z):
    if step_z == 0:
        return values
    edge = NZ - 1 if step_z == 1 else 0
    moved = shifted(values, step_z)
    return jnp.where(lane_index(values) % NZ == edge, jnp.zeros_like(moved), moved)


def own_lanes_only(values):
    lane = lane_index(values)
    return jnp.where((lane >= HALO) & (lane < HALO + LANES), values, jnp.zeros_like(values))


def dot(left, right):
    return lax.dot_general(left, right, (((1,), (0,)), ((), ())), preferred_element_type=f32)


def dot_lanes(left, right):
    return lax.dot_general(left, right, (((1,), (1,)), ((), ())), preferred_element_type=f32)


def central_y(values):
    return 0.5 * (shifted(values, NZ) - shifted(values, -NZ))


def central_z(values):
    return 0.5 * (lifted(values, 1) - lifted(values, -1))


def column_to_row(column):
    size = column.shape[0]
    wide = jnp.broadcast_to(column, (size, size))
    row = lax.broadcasted_iota(jnp.int32, (size, size), 0)
    col = lax.broadcasted_iota(jnp.int32, (size, size), 1)
    return jnp.sum(jnp.where(row == col, wide, 0.0), axis=0, keepdims=True)


def first_stack(field_ext):
    rounded = field_ext[...].astype(bf16).astype(f32)
    moves = [lifted(shifted(rounded, NZ * b), c) for b in STEPS for c in STEPS]
    return jnp.concatenate(moves, axis=0).astype(bf16)


def z_stack(values, target, sign, start):
    count, width = values.shape[0] // C, values.shape[1]
    wide = values.astype(f32)
    for number, c in enumerate(STEPS):
        moved = lifted(wide, sign * c).astype(bf16) if c else values
        target[start : start + count, number * C : (number + 1) * C, :] = moved.reshape(
            count, C, width
        )


def middle_conv(weights, stack, start, sign):
    width = stack.shape[2]
    window = stack[start : start + 5].reshape(5 * 3 * C, width)
    out = dot(weights[...], window).reshape(3, 3, C, width)
    result = out[:, 1]
    for number, b in ((0, -1), (2, 1)):
        part = out[:, number].reshape(3 * C, width)
        result = result + shifted(part, sign * NZ * b).reshape(3, C, width)
    return result


def forward(first, low, weights, stack, hidden_two):
    b0, bias_in, w_fwd, bias_mid = weights
    count, width = stack.shape[0], stack.shape[2]
    pre = dot(b0[low * C : (low + count) * C, :], first).reshape(count, C, width)
    hidden_one = jnp.tanh(pre + bias_in[...][None]).astype(bf16)
    z_stack(hidden_one.reshape(count * C, width), stack, 1, 0)
    for start in [*range(0, count - 5, 3), count - 5]:
        pre = middle_conv(w_fwd, stack, start, 1)
        hidden_two[start : start + 3] = jnp.tanh(pre + bias_mid[...][None]).astype(bf16)


def stepped(field_ext, kv_ext, bf, hidden_two):
    flux = dot(bf[...], hidden_two[...].reshape(20 * C, BROAD))
    correction = flux[0:TALL] + central_y(flux[TALL : 2 * TALL]) + central_z(flux[2 * TALL :])
    here = field_ext[...]
    up, down = row_moved(here, 1), row_moved(here, -1)
    laplace = (
        up + down + shifted(here, NZ) + shifted(here, -NZ) + lifted(here, 1) + lifted(here, -1)
    )
    physics = kv_ext[0] * (laplace - 6.0 * here)
    physics = physics - kv_ext[1] * (0.5 * (up - down))
    physics = physics - kv_ext[2] * central_y(here)
    physics = physics - kv_ext[3] * central_z(here)
    return here + time_step * (physics + correction)


def row_moved(values, count):
    return pltpu.roll(values, (-count) % values.shape[0], axis=0)


def flux_pair(here):
    parts = [
        -0.5 * time_step * (row_moved(here, 1) - row_moved(here, -1)),
        -time_step * central_y(here),
        -time_step * central_z(here),
    ]
    flux = jnp.concatenate(parts, axis=0)
    high = flux.astype(bf16)
    low = (flux - high.astype(f32)).astype(bf16)
    return jnp.concatenate([high, low], axis=0)


def cotangent_two(back, hidden_two, low, high):
    two = centre(hidden_two, low, high).astype(f32)
    return (back.reshape(high - low, C, WIDE) * (1.0 - two * two)).astype(bf16)


def centre(ref, low, high):
    margin = (ref.shape[2] - WIDE) // 2
    return ref[low:high, :, margin : margin + WIDE]


def middle_terms(stack, own_two, spread):
    first_row = (stack.shape[0] - ROWS) // 2 - 1
    own = own_lanes_only(own_two.astype(f32))
    for number, b in enumerate(STEPS):
        moved = shifted(own, -NZ * b).astype(bf16)
        spread[:, number * C : (number + 1) * C, :] = moved.reshape(8, C, WIDE)
    pairs = jnp.zeros((12 * C, 6 * C), f32)
    for x in range(0, ROWS, 2):
        window = centre(stack, first_row + x, first_row + x + 4).reshape(12 * C, WIDE)
        pairs = pairs + dot_lanes(window, spread[x : x + 2].reshape(6 * C, WIDE))
    term_mid = pairs[0 : 9 * C, 0 : 3 * C] + pairs[3 * C :, 3 * C :]
    return term_mid


def out_terms(pair, hidden_two, own_two):
    own = own_lanes_only(own_two.astype(f32))
    bias_mid = jnp.sum(jnp.sum(own.reshape(8, C, WIDE), axis=0), axis=1, keepdims=True)
    masked = own_lanes_only(pair.astype(f32)).astype(bf16)
    first_row = (hidden_two.shape[0] - ROWS) // 2
    two = centre(hidden_two, first_row, first_row + ROWS)
    outer = dot_lanes(two.reshape(8 * C, WIDE), masked)
    row_x = lax.broadcasted_iota(jnp.int32, outer.shape, 0) // C
    col = lax.broadcasted_iota(jnp.int32, outer.shape, 1)
    outer = jnp.where(col % 16 == row_x + 4, outer, 0.0)
    outer = jnp.sum(outer.reshape(8, C, outer.shape[1]), axis=0)
    kind = (lax.broadcasted_iota(jnp.int32, outer.shape, 1) // 16) % 3
    columns = [jnp.sum(jnp.where(kind == d, outer, 0.0), axis=1, keepdims=True) for d in range(3)]
    return [column_to_row(column) for column in [bias_mid] + columns]


def cotangent_one(w_bwd, stack, grad_stack, grad_one, starts):
    for start in starts:
        back = middle_conv(w_bwd, grad_stack, start, -1)
        low = start + (stack.shape[0] - 12) // 2
        one = centre(stack, low, low + 3)[:, C : 2 * C].astype(f32)
        grad_one[start : start + 3] = (back * (1.0 - one * one)).astype(bf16)


def first_terms(first, grad_one):
    own = own_lanes_only(grad_one[2:10].reshape(8 * C, WIDE).astype(f32))
    outer = dot_lanes(first, own.astype(bf16))
    row_x = lax.broadcasted_iota(jnp.int32, outer.shape, 0) % TALL
    col_x = lax.broadcasted_iota(jnp.int32, outer.shape, 1) // C
    parts = []
    for a in range(3):
        kept = jnp.where(row_x - col_x == a + 7, outer, 0.0)
        parts.append(jnp.sum(kept.reshape(9, TALL, 8 * C), axis=1))
    folded = jnp.concatenate(parts, axis=0)
    folded = folded[:, :128] + folded[:, 128:]
    folded = folded + pltpu.roll(folded, 64, axis=1)
    folded = folded + pltpu.roll(folded, 32, axis=1)
    bias_in = jnp.sum(jnp.sum(own.reshape(8, C, WIDE), axis=0), axis=1, keepdims=True)
    return folded[:, :C], column_to_row(bias_in)


def previous(here, kv_ext, bq, grad_one):
    spread = dot(bq[...], grad_one[...].reshape(12 * C, WIDE))
    total = 0.0
    for number, (b, c) in enumerate([(b, c) for b in STEPS for c in STEPS]):
        total = total + lifted(shifted(spread[number * 16 : number * 16 + 16], -NZ * b), -c)
    cell = lambda number: kv_ext[number, 4:20, MIDDLE]
    scaled = cell(0) * here
    physics = row_moved(scaled, 1) + row_moved(scaled, -1) - 6.0 * scaled
    physics = physics + shifted(scaled, NZ) + shifted(scaled, -NZ)
    physics = physics + lifted(scaled, 1) + lifted(scaled, -1)
    scaled = cell(1) * here
    physics = physics + 0.5 * (row_moved(scaled, 1) - row_moved(scaled, -1))
    physics = physics + central_y(cell(2) * here) + central_z(cell(3) * here)
    return here + time_step * physics + total


def iota(shape, dimension):
    return lax.broadcasted_iota(jnp.int32, shape, dimension)


def ones_where(condition):
    return jnp.where(condition, 1.0, 0.0).astype(bf16)


def dot_rows(left, right):
    return lax.dot_general(left, right, (((0,), (0,)), ((), ())), preferred_element_type=f32)


def place_middle(conv_mid, wide, w_fwd, w_bwd):
    for target, backward in ((w_fwd, False), (w_bwd, True)):
        wide[...] = jnp.zeros_like(wide)
        for a in range(3):
            for b in range(3):
                for c in range(3):
                    block = conv_mid[a * 9 + b * 3 + c].astype(f32)
                    if not backward:
                        block = block.T
                    for x in range(3):
                        row = (x * 3 + b) * C
                        col = ((x + (2 - a if backward else a)) * 3 + c) * C
                        wide[row : row + C, col : col + C] = block
        target[...] = wide[...].astype(bf16)


def place_first(conv_in, b0, bq):
    taps = conv_in[...]
    shape = (27, 9 * TALL)
    spread = []
    for a in range(3):
        pick = ones_where(iota(shape, 0) == iota(shape, 1) // TALL + 9 * a)
        spread.append(dot_rows(taps, pick))
    j = iota(spread[0].shape, 1) % TALL
    for i in range(22):
        rows = sum(jnp.where(j == i + a, spread[a], 0.0) for a in range(3))
        b0[i * C : (i + 1) * C, :] = rows.astype(bf16)
    shape = (C, 12 * C)
    tiled = dot(taps, ones_where(iota(shape, 1) % C == iota(shape, 0))).astype(bf16)
    total = 0.0
    for a in range(3):
        pick = ones_where(iota((144, 27), 1) == iota((144, 27), 0) // 16 + 9 * a)
        rows = dot(pick, tiled)
        kept = iota(rows.shape, 1) // C == iota(rows.shape, 0) % 16 - a - 1
        total = total + jnp.where(kept, rows, 0.0)
    bq[...] = total.astype(bf16)


def place_flux(flux, bf, bb):
    taps = flux[...]
    shape = (C, 20 * C)
    tiled = dot(taps, ones_where(iota(shape, 1) % C == iota(shape, 0))).astype(bf16)
    shape = (3 * TALL, 3)
    rows = dot(ones_where(iota(shape, 1) == iota(shape, 0) // TALL), tiled)
    x, i = iota(rows.shape, 0) % TALL, iota(rows.shape, 1) // C
    first = iota(rows.shape, 0) < TALL
    factor = jnp.where(i == x - 1, 0.5, jnp.where(i == x - 3, -0.5, 0.0))
    factor = jnp.where(first, factor, jnp.where(i == x - 2, 1.0, 0.0))
    bf[...] = (rows * factor).astype(bf16)
    pick = ones_where(iota((3, 96), 0) == (iota((3, 96), 1) // 16) % 3)
    columns = dot_rows(taps, pick)
    j = iota(columns.shape, 1) % 16
    for i in range(14):
        bb[i * C : (i + 1) * C, :] = jnp.where(j == i + 1, columns, 0.0).astype(bf16)


def row_to_column(row):
    size = row.shape[1]
    wide = jnp.broadcast_to(row, (size, size))
    return jnp.sum(
        jnp.where(iota((size, size), 0) == iota((size, size), 1), wide, 0.0),
        axis=1,
        keepdims=True,
    )


def remote(source, target, sems, peer):
    copy = pltpu.make_async_remote_copy(
        src_ref=source,
        dst_ref=target,
        send_sem=sems[0],
        recv_sem=sems[1],
        device_id=peer,
        device_id_type=MESH,
    )
    copy.start()


def send_around(ext, sems, place):
    (me_x, size_x), (me_y, size_y) = place
    width = ext.shape[-1]
    side = (width - LANES) // 2
    lead = (slice(None),) * (len(ext.shape) - 2)
    sources = {0: slice(side, side + LANES), 1: slice(LANES, side + LANES), -1: slice(side, 2 * side)}
    targets = {0: slice(side, side + LANES), 1: slice(0, side), -1: slice(side + LANES, width)}
    rows = {0: OWN_ROWS, 1: slice(0, ROWS), -1: slice(2 * ROWS, TALL)}
    for dx, dy in AROUND:
        peer = (
            lax.rem(me_x + dx + size_x, size_x),
            lax.rem(me_y + dy + size_y, size_y),
        )
        source = ext.at[lead + (OWN_ROWS, sources[dy])]
        remote(source, ext.at[lead + (rows[dx], targets[dy])], sems, peer)
    depth = ext.shape[0] if lead else 1
    return depth * (3 * width - LANES) // 128


def wait_tiles(sem, gauge, count):
    part = gauge.at[pl.ds(0, 8 * count)]
    pltpu.make_async_copy(part, part, sem).wait()


def far_first_x(me_x, me_y, size):
    groups, ring, cores = (2, size // 4, 2) if size % 8 == 0 else (1, size, 1)
    steps = [
        (g, r, c) for g in range(groups) for r in range(ring) for c in range(cores)
    ][1:]
    steps.sort(key=lambda step: (-step[0] - min(step[1], ring - step[1]), -step[2]))
    at = lax.div(me_x, ring * cores), lax.rem(lax.div(me_x, cores), ring), lax.rem(me_x, cores)
    peers = []
    for g, r, c in steps:
        to = lax.rem(at[0] + g, groups), lax.rem(at[1] + r, ring), lax.rem(at[2] + c, cores)
        peers.append(((to[0] * ring + to[1]) * cores + to[2], me_y))
    return peers


def far_first_y(me_x, me_y, size_x, size_y):
    ring = size_y // 2
    steps = [(g, r) for g in range(2) for r in range(ring)][1:]
    steps.sort(key=lambda step: -step[0] - min(step[1], ring - step[1]))
    high, at = lax.div(me_y, ring), lax.rem(me_y, ring)
    return [
        (
            lax.rem(me_x + g * (size_x // 2), size_x),
            lax.rem(high + g, 2) * ring + lax.rem(at + r, ring),
        )
        for g, r in steps
    ]


def kernel(
    size_x, size_y, scale,
    field, cotangent, kappa, vel, conv_in_in, bias_in_in, conv_mid_in, bias_mid_in, flux_in,
    out_field, out_sums, out_small,
    f_ext, f1_ext, g_ext, a_ext, kv_ext, conv_in, bias_in_row, conv_mid, bias_mid_row, flux,
    bias_in, bias_mid, wide, b0, w_fwd, bf, bb, w_bwd, bq,
    stack_one, stack_two, two_one, two_two, spread, grad_stack, grad_one,
    sums, recv_x, recv_y, gathered, small, small_x, small_y, gauge,
    local_sem, send_sem, recv_sem,
):
    me_x, me_y = lax.axis_index("gx"), lax.axis_index("gy")
    place = (me_x, size_x), (me_y, size_y)
    half_x, half_y = size_x // 2, size_y // 2
    mine_hi = lax.div(me_y, half_y)
    peers_x, peers_y = far_first_x(me_x, me_y, size_x), far_first_y(me_x, me_y, size_x, size_y)
    near = [
        (lax.rem(me_x + dx + size_x, size_x), lax.rem(me_y + dy + size_y, size_y))
        for dx, dy in AROUND
        if dy != 0
    ]
    barrier = pltpu.get_barrier_semaphore()
    for peer in peers_y + near + peers_x:
        pl.semaphore_signal(barrier, inc=1, device_id=peer, device_id_type=MESH)
    own = (OWN_ROWS, OWN_LANES)
    broad_own = (OWN_ROWS, slice(256, 256 + LANES))
    arrivals = []
    for source, target in (
        (field, f_ext.at[broad_own]),
        (cotangent, g_ext.at[own]),
        (kappa, kv_ext.at[(0,) + broad_own]),
        (vel, kv_ext.at[(slice(1, 4),) + broad_own]),
        (conv_in_in, conv_in),
        (bias_in_in, bias_in_row),
        (conv_mid_in, conv_mid),
        (bias_mid_in, bias_mid_row),
        (flux_in, flux),
    ):
        copy = pltpu.make_async_copy(source, target, local_sem.at[len(arrivals)])
        copy.start()
        arrivals.append(copy)
    for copy in arrivals:
        copy.wait()
    sems = lambda number: (send_sem.at[number], recv_sem.at[number])
    pl.semaphore_wait(barrier, len(near + peers_x + peers_y))
    tiles = [
        send_around(ext, sems(number), place) for number, ext in enumerate((f_ext, kv_ext, g_ext))
    ]

    bias_in[...] = row_to_column(bias_in_row[...])
    bias_mid[...] = row_to_column(bias_mid_row[...])
    place_first(conv_in, b0, bq)
    place_middle(conv_mid, wide, w_fwd, w_bwd)
    place_flux(flux, bf, bb)

    weights = (b0, bias_in, w_fwd, bias_mid)
    wait_tiles(recv_sem.at[0], gauge, tiles[0])
    first_one = first_stack(f_ext)
    forward(first_one, 0, weights, stack_one, two_one)
    first_one = first_one[:, MIDDLE]
    wait_tiles(recv_sem.at[1], gauge, tiles[1])
    f1_ext[...] = stepped(f_ext, kv_ext, bf, two_one)
    first_two = first_stack(f1_ext)[:, MIDDLE]
    forward(first_two, 3, weights, stack_two, two_two)

    wait_tiles(recv_sem.at[2], gauge, tiles[2])
    pair_two = flux_pair(g_ext[4:20, :])
    back_two = dot(bb[...], pair_two)
    grad_two = cotangent_two(back_two, two_two, 0, 14).reshape(14 * C, WIDE)
    z_stack(grad_two, grad_stack, -1, 0)
    cotangent_one(w_bwd, stack_two, grad_stack, grad_one, (0, 3, 6, 9))
    adjoint = previous(g_ext[4:20, :], kv_ext, bq, grad_one)
    a_ext[own] = adjoint[4:12, OWN_LANES]
    tiles.append(send_around(a_ext, sems(3), place))

    own_two = grad_two[3 * C : 11 * C]
    mid = middle_terms(stack_two, own_two, spread)
    pair_one = flux_pair(adjoint)
    own_one = cotangent_two(dot(bb[3 * C : 11 * C, :], pair_one), two_one, 6, 14)
    own_one = own_one.reshape(8 * C, WIDE)
    mid = mid + middle_terms(stack_one, own_one, spread)
    sums[:, 0 : 3 * C] = mid[0 : 8 * C]
    for number in range(3):
        sums[number * C : (number + 1) * C, 3 * C :] = mid[
            8 * C : 9 * C, number * C : (number + 1) * C
        ]
    sums[3 * C :, 3 * C :] = jnp.zeros((5 * C, C), f32)

    part = sums.shape[0] // size_x
    share = lambda x: pl.ds(
        pl.multiple_of(lax.rem(x + mine_hi * half_x, size_x) * part, part), part
    )
    for peer in peers_x:
        remote(sums.at[share(peer[0])], recv_x.at[me_x], sems(4), peer)

    in_two, bias_in_two = first_terms(first_two, grad_one)
    rows_two = out_terms(pair_two, two_two, own_two)
    rows_one = out_terms(pair_one, two_one, own_one)
    wait_tiles(recv_sem.at[3], gauge, tiles[3])
    here = a_ext[4:20, :]
    full = cotangent_two(dot(bb[C : 13 * C, :], flux_pair(here)), two_one, 4, 16)
    z_stack(full.reshape(12 * C, WIDE), grad_stack, -1, 1)
    cotangent_one(w_bwd, stack_one, grad_stack, grad_one, (1, 4, 7, 8))
    in_one, bias_in_one = first_terms(first_one, grad_one)
    matrix = jnp.concatenate(
        [in_one + in_two, bias_in_one + bias_in_two]
        + [one + two for one, two in zip(rows_one, rows_two)],
        axis=0,
    )
    for number in range(4):
        small[:, number * C : (number + 1) * C] = matrix[number * 8 : number * 8 + 8]
    small_x[me_x] = small[...]

    per = part // 8
    wait_tiles(recv_sem.at[4], gauge, per * (size_x - 1))
    recv_x[me_x] = sums[share(me_x), :]
    total = recv_x[0]
    for k in range(1, size_x):
        total = total + recv_x[k]
    recv_y[me_y] = total
    for peer in peers_y:
        remote(recv_y.at[me_y], recv_y.at[me_y], sems(5), peer)
    for peer in peers_x:
        remote(small, small_x.at[me_x], sems(7), peer)

    final = previous(here, kv_ext, bq, grad_one)
    out_field[...] = final[4:12, OWN_LANES]

    wait_tiles(recv_sem.at[7], gauge, size_x - 1)
    total = small_x[0]
    for k in range(1, size_x):
        total = total + small_x[k]
    small_y[me_y] = total
    for peer in peers_y:
        remote(small_y.at[me_y], small_y.at[me_y], sems(8), peer)

    wait_tiles(recv_sem.at[5], gauge, per * (size_y - 1))
    total = recv_y[0]
    for k in range(1, size_y):
        total = total + recv_y[k]
    gathered[share(me_x), :] = total * scale
    for peer in peers_x:
        remote(gathered.at[share(me_x)], gathered.at[share(me_x)], sems(6), peer)

    wait_tiles(recv_sem.at[8], gauge, size_y - 1)
    total = small_y[0]
    for k in range(1, size_y):
        total = total + small_y[k]
    out_small[...] = total * scale
    wait_tiles(recv_sem.at[6], gauge, per * (size_x - 1))
    out_sums[...] = gathered[...]

    for number in range(4):
        wait_tiles(send_sem.at[number], gauge, tiles[number])
    wait_tiles(send_sem.at[4], gauge, per * (size_x - 1))
    wait_tiles(send_sem.at[5], gauge, per * (size_y - 1))
    wait_tiles(send_sem.at[6], gauge, per * (size_x - 1))
    wait_tiles(send_sem.at[7], gauge, size_x - 1)
    wait_tiles(send_sem.at[8], gauge, size_y - 1)


def unpack(field, sums, small, out_field, out_in, out_bias_in, out_mid, out_bias_mid, out_out):
    out_field[...] = field[...]
    for a in range(3):
        for b in range(3):
            for c in range(3):
                row = (a * 3 + c) * C
                if row < 8 * C:
                    value = sums[row : row + C, b * C : (b + 1) * C]
                else:
                    value = sums[b * C : (b + 1) * C, 3 * C :]
                out_mid[a * 9 + b * 3 + c] = value
    for number in range(3):
        out_in[number * 8 : number * 8 + 8] = small[:, number * C : (number + 1) * C]
    last = small[:, 3 * C :]
    out_in[24:27] = last[0:3]
    out_bias_in[...] = last[3:4]
    out_bias_mid[...] = last[4:5]
    out_out[...] = last[5:8]


def solution(mesh):
    size_x, size_y = mesh.shape["gx"], mesh.shape["gy"]

    def shards(
        scalar_field, field_cotangent, diffusivity, velocity,
        conv_in, bias_in, conv_mid, bias_mid, flux_out,
    ):
        cells = scalar_field.size * size_x * size_y
        vmem = pl.BlockSpec(memory_space=pltpu.VMEM)
        anywhere = pl.BlockSpec(memory_space=pltpu.HBM)
        part = 256 // size_x
        ext, broad = pltpu.VMEM((TALL, WIDE), f32), pltpu.VMEM((TALL, BROAD), f32)
        shape = jax.ShapeDtypeStruct
        outs = pl.pallas_call(
            lambda *refs: kernel(size_x, size_y, 1.0 / math.sqrt(cells), *refs),
            out_shape=[shape((ROWS, LANES), f32), shape((256, 128), f32), shape((8, 128), f32)],
            in_specs=[anywhere] * 9,
            out_specs=[vmem] * 3,
            scratch_shapes=[
                broad, broad, ext, ext,
                pltpu.VMEM((4, TALL, BROAD), f32),
                pltpu.VMEM((27, C), bf16),
                pltpu.VMEM((1, C), f32),
                pltpu.VMEM((27, C, C), bf16),
                pltpu.VMEM((1, C), f32),
                pltpu.VMEM((3, C), bf16),
                pltpu.VMEM((C, 1), f32),
                pltpu.VMEM((C, 1), f32),
                pltpu.VMEM((288, 480), f32),
                pltpu.VMEM((22 * C, 9 * TALL), bf16),
                pltpu.VMEM((288, 480), bf16),
                pltpu.VMEM((3 * TALL, 20 * C), bf16),
                pltpu.VMEM((14 * C, 96), bf16),
                pltpu.VMEM((288, 480), bf16),
                pltpu.VMEM((144, 12 * C), bf16),
                pltpu.VMEM((22, 3 * C, BROAD), bf16),
                pltpu.VMEM((16, 3 * C, WIDE), bf16),
                pltpu.VMEM((20, C, BROAD), bf16),
                pltpu.VMEM((14, C, WIDE), bf16),
                pltpu.VMEM((8, 3 * C, WIDE), bf16),
                pltpu.VMEM((14, 3 * C, WIDE), bf16),
                pltpu.VMEM((12, C, WIDE), bf16),
                pltpu.VMEM((256, 128), f32),
                pltpu.VMEM((size_x, part, 128), f32),
                pltpu.VMEM((size_y, part, 128), f32),
                pltpu.VMEM((256, 128), f32),
                pltpu.VMEM((8, 128), f32),
                pltpu.VMEM((size_x, 8, 128), f32),
                pltpu.VMEM((size_y, 8, 128), f32),
                pltpu.VMEM((640, 128), f32),
                pltpu.SemaphoreType.DMA((9,)),
                pltpu.SemaphoreType.DMA((9,)),
                pltpu.SemaphoreType.DMA((9,)),
            ],
            compiler_params=pltpu.CompilerParams(
                collective_id=0, has_side_effects=True, vmem_limit_bytes=60 * 1024 * 1024
            ),
        )(
            scalar_field, field_cotangent, diffusivity, velocity,
            conv_in, bias_in.reshape(1, C), conv_mid, bias_mid.reshape(1, C), flux_out.T,
        )
        outs = pl.pallas_call(
            unpack,
            out_shape=[
                shape((ROWS, LANES), f32),
                shape((27, C), f32),
                shape((1, C), f32),
                shape((27, C, C), f32),
                shape((1, C), f32),
                shape((3, C), f32),
            ],
            in_specs=[vmem] * 3,
            out_specs=[vmem] * 6,
        )(*outs)
        return (outs[0], outs[1], outs[2].reshape(C), outs[3], outs[4].reshape(C), outs[5].T)

    return jax.shard_map(
        shards,
        mesh=mesh,
        in_specs=(
            P("gx", "gy"), P("gx", "gy"), P("gx", "gy"), P(None, "gx", "gy"),
            P(), P(), P(), P(), P(),
        ),
        out_specs=(P("gx", "gy"), P(), P(), P(), P(), P()),
        check_vma=False,
    )
```

```python
import math

import jax
import jax.numpy as jnp
from jax import lax
from jax.experimental import pallas as pl
from jax.experimental.pallas import tpu as pltpu
from jax.sharding import PartitionSpec as P

NZ = 32
C = 32
ROWS = 8
LANES = 512
HALO = 128
WIDE = LANES + 2 * HALO
TALL = 3 * ROWS
BROAD = WIDE + 256
MIDDLE = slice(128, 128 + WIDE)
time_step = 0.2
MESH = pl.DeviceIdType.MESH
STEPS = (-1, 0, 1)
AROUND = ((1, 1), (1, -1), (-1, 1), (-1, -1), (0, 1), (0, -1), (1, 0), (-1, 0))
OWN_ROWS = slice(ROWS, 2 * ROWS)
OWN_LANES = slice(HALO, HALO + LANES)
bf16 = jnp.bfloat16
f32 = jnp.float32


def shifted(values, count):
    if count == 0:
        return values
    return pltpu.roll(values, (-count) % values.shape[-1], axis=values.ndim - 1)


def lane_index(values):
    return lax.broadcasted_iota(jnp.int32, values.shape, values.ndim - 1)


def lifted(values, step_z):
    if step_z == 0:
        return values
    edge = NZ - 1 if step_z == 1 else 0
    moved = shifted(values, step_z)
    return jnp.where(lane_index(values) % NZ == edge, jnp.zeros_like(moved), moved)


def own_lanes_only(values):
    lane = lane_index(values)
    return jnp.where((lane >= HALO) & (lane < HALO + LANES), values, jnp.zeros_like(values))


def dot(left, right):
    return lax.dot_general(left, right, (((1,), (0,)), ((), ())), preferred_element_type=f32)


def dot_lanes(left, right):
    return lax.dot_general(left, right, (((1,), (1,)), ((), ())), preferred_element_type=f32)


def central_y(values):
    return 0.5 * (shifted(values, NZ) - shifted(values, -NZ))


def central_z(values):
    return 0.5 * (lifted(values, 1) - lifted(values, -1))


def column_to_row(column):
    size = column.shape[0]
    wide = jnp.broadcast_to(column, (size, size))
    row = lax.broadcasted_iota(jnp.int32, (size, size), 0)
    col = lax.broadcasted_iota(jnp.int32, (size, size), 1)
    return jnp.sum(jnp.where(row == col, wide, 0.0), axis=0, keepdims=True)


def first_stack(field_ext):
    rounded = field_ext[...].astype(bf16).astype(f32)
    rows = [shifted(rounded, NZ * b) for b in STEPS]
    moves = [lifted(row, c) for row in rows for c in STEPS]
    return jnp.concatenate(moves, axis=0).astype(bf16)


def z_stack(values, target, sign, start):
    count, width = values.shape[0] // C, values.shape[1]
    wide = values.astype(f32)
    for number, c in enumerate(STEPS):
        moved = lifted(wide, sign * c).astype(bf16) if c else values
        target[start : start + count, number * C : (number + 1) * C, :] = moved.reshape(
            count, C, width
        )


def middle_conv(weights, stack, start, count, sign):
    width = stack.shape[2]
    window = stack[start : start + count + 2].reshape((count + 2) * 3 * C, width)
    banded = weights[0 : count * 3 * C, 0 : (count + 2) * 3 * C]
    out = dot(banded, window).reshape(count, 3, C, width)
    result = out[:, 1]
    for number, b in ((0, -1), (2, 1)):
        part = out[:, number].reshape(count * C, width)
        result = result + shifted(part, sign * NZ * b).reshape(count, C, width)
    return result


def groups(low, high):
    return [(start, min(3, high - start)) for start in range(low, high, 3)]


def forward(first, low, weights, stack, hidden_two):
    b0, bias_in, w_fwd, bias_mid = weights
    count, width = stack.shape[0], stack.shape[2]
    pre = dot(b0[low * C : (low + count) * C, :], first).reshape(count, C, width)
    filled = 0
    for start, rows in groups(0, count - 2):
        until = min(start + rows + 5, count) if start else 5
        if start == 0 or until > filled:
            hidden_one = jnp.tanh(pre[filled:until] + bias_in[...][None]).astype(bf16)
            z_stack(hidden_one.reshape((until - filled) * C, width), stack, 1, filled)
            filled = until
        out = middle_conv(w_fwd, stack, start, rows, 1)
        hidden_two[start : start + rows] = jnp.tanh(out + bias_mid[...][None]).astype(bf16)


def stepped(field_ext, kv_ext, bf, hidden_two):
    flux = dot(bf[...], hidden_two[...].reshape(20 * C, BROAD))
    correction = flux[0:TALL] + central_y(flux[TALL : 2 * TALL]) + central_z(flux[2 * TALL :])
    here = field_ext[...]
    up, down = row_moved(here, 1), row_moved(here, -1)
    laplace = (
        up + down + shifted(here, NZ) + shifted(here, -NZ) + lifted(here, 1) + lifted(here, -1)
    )
    physics = kv_ext[0] * (laplace - 6.0 * here)
    physics = physics - kv_ext[1] * (0.5 * (up - down))
    physics = physics - kv_ext[2] * central_y(here)
    physics = physics - kv_ext[3] * central_z(here)
    return here + time_step * (physics + correction)


def row_moved(values, count):
    return pltpu.roll(values, (-count) % values.shape[0], axis=0)


def flux_pair(here):
    parts = [
        -0.5 * time_step * (row_moved(here, 1) - row_moved(here, -1)),
        -time_step * central_y(here),
        -time_step * central_z(here),
    ]
    flux = jnp.concatenate(parts, axis=0)
    high = flux.astype(bf16)
    low = (flux - high.astype(f32)).astype(bf16)
    return jnp.concatenate([high, low], axis=0)


def cotangent_two(back, hidden_two, low, high):
    two = centre(hidden_two, low, high).astype(f32)
    return (back.reshape(high - low, C, WIDE) * (1.0 - two * two)).astype(bf16)


def centre(ref, low, high):
    margin = (ref.shape[2] - WIDE) // 2
    return ref[low:high, :, margin : margin + WIDE]


def middle_terms(stack, own_two, spread):
    first_row = (stack.shape[0] - ROWS) // 2 - 1
    own = own_lanes_only(own_two.astype(f32))
    for number, b in enumerate(STEPS):
        moved = shifted(own, -NZ * b).astype(bf16)
        spread[:, number * C : (number + 1) * C, :] = moved.reshape(8, C, WIDE)
    pairs = jnp.zeros((12 * C, 6 * C), f32)
    for x in range(0, ROWS, 2):
        window = centre(stack, first_row + x, first_row + x + 4).reshape(12 * C, WIDE)
        pairs = pairs + dot_lanes(window, spread[x : x + 2].reshape(6 * C, WIDE))
    term_mid = pairs[0 : 9 * C, 0 : 3 * C] + pairs[3 * C :, 3 * C :]
    return term_mid


def out_terms(pair, hidden_two, own_two):
    own = own_lanes_only(own_two.astype(f32))
    bias_mid = jnp.sum(jnp.sum(own.reshape(8, C, WIDE), axis=0), axis=1, keepdims=True)
    masked = own_lanes_only(pair.astype(f32)).astype(bf16)
    first_row = (hidden_two.shape[0] - ROWS) // 2
    two = centre(hidden_two, first_row, first_row + ROWS)
    outer = dot_lanes(two.reshape(8 * C, WIDE), masked)
    row_x = lax.broadcasted_iota(jnp.int32, outer.shape, 0) // C
    col = lax.broadcasted_iota(jnp.int32, outer.shape, 1)
    outer = jnp.where(col % 16 == row_x + 4, outer, 0.0)
    outer = jnp.sum(outer.reshape(8, C, outer.shape[1]), axis=0)
    kind = (lax.broadcasted_iota(jnp.int32, outer.shape, 1) // 16) % 3
    columns = [jnp.sum(jnp.where(kind == d, outer, 0.0), axis=1, keepdims=True) for d in range(3)]
    return [column_to_row(column) for column in [bias_mid] + columns]


def cotangent_one(w_bwd, stack, grad_stack, grad_one, low, high):
    for start, rows in groups(low, high):
        back = middle_conv(w_bwd, grad_stack, start, rows, -1)
        first = start + (stack.shape[0] - 12) // 2
        one = centre(stack, first, first + rows)[:, C : 2 * C].astype(f32)
        grad_one[start : start + rows] = (back * (1.0 - one * one)).astype(bf16)


def first_terms(first, grad_one):
    own = own_lanes_only(grad_one[2:10].reshape(8 * C, WIDE).astype(f32))
    outer = dot_lanes(first, own.astype(bf16))
    row_x = lax.broadcasted_iota(jnp.int32, outer.shape, 0) % TALL
    col_x = lax.broadcasted_iota(jnp.int32, outer.shape, 1) // C
    parts = []
    for a in range(3):
        kept = jnp.where(row_x - col_x == a + 7, outer, 0.0)
        parts.append(jnp.sum(kept.reshape(9, TALL, 8 * C), axis=1))
    folded = jnp.concatenate(parts, axis=0)
    folded = folded[:, :128] + folded[:, 128:]
    folded = folded + pltpu.roll(folded, 64, axis=1)
    folded = folded + pltpu.roll(folded, 32, axis=1)
    bias_in = jnp.sum(jnp.sum(own.reshape(8, C, WIDE), axis=0), axis=1, keepdims=True)
    return folded[:, :C], column_to_row(bias_in)


def previous(here, kv_ext, bq, grad_one):
    spread = dot(bq[...], grad_one[...].reshape(12 * C, WIDE))
    total = here
    for row, b in enumerate(STEPS):
        taps = [spread[(row * 3 + i) * 16 : (row * 3 + i + 1) * 16] for i in range(3)]
        lift = lifted(taps[0], 1) + taps[1] + lifted(taps[2], -1)
        total = total + shifted(lift, -NZ * b)
    cell = lambda number: kv_ext[number, 4:20, MIDDLE]
    scaled = cell(0) * here
    physics = row_moved(scaled, 1) + row_moved(scaled, -1) - 6.0 * scaled
    physics = physics + shifted(scaled, NZ) + shifted(scaled, -NZ)
    physics = physics + lifted(scaled, 1) + lifted(scaled, -1)
    scaled = cell(1) * here
    physics = physics + 0.5 * (row_moved(scaled, 1) - row_moved(scaled, -1))
    physics = physics + central_y(cell(2) * here) + central_z(cell(3) * here)
    return total + time_step * physics


def iota(shape, dimension):
    return lax.broadcasted_iota(jnp.int32, shape, dimension)


def ones_where(condition):
    return jnp.where(condition, 1.0, 0.0).astype(bf16)


def dot_rows(left, right):
    return lax.dot_general(left, right, (((0,), (0,)), ((), ())), preferred_element_type=f32)


def place_middle(conv_mid, wide, w_fwd, w_bwd):
    for target, backward in ((w_fwd, False), (w_bwd, True)):
        wide[...] = jnp.zeros_like(wide)
        for a in range(3):
            for b in range(3):
                for c in range(3):
                    block = conv_mid[a * 9 + b * 3 + c].astype(f32)
                    if not backward:
                        block = block.T
                    for x in range(3):
                        row = (x * 3 + b) * C
                        col = ((x + (2 - a if backward else a)) * 3 + c) * C
                        wide[row : row + C, col : col + C] = block
        target[...] = wide[...].astype(bf16)


def place_first(conv_in, b0, bq):
    taps = conv_in[...]
    shape = (27, 9 * TALL)
    spread = []
    for a in range(3):
        pick = ones_where(iota(shape, 0) == iota(shape, 1) // TALL + 9 * a)
        spread.append(dot_rows(taps, pick))
    j = iota(spread[0].shape, 1) % TALL
    for i in range(22):
        rows = sum(jnp.where(j == i + a, spread[a], 0.0) for a in range(3))
        b0[i * C : (i + 1) * C, :] = rows.astype(bf16)
    shape = (C, 12 * C)
    tiled = dot(taps, ones_where(iota(shape, 1) % C == iota(shape, 0))).astype(bf16)
    total = 0.0
    for a in range(3):
        pick = ones_where(iota((144, 27), 1) == iota((144, 27), 0) // 16 + 9 * a)
        rows = dot(pick, tiled)
        kept = iota(rows.shape, 1) // C == iota(rows.shape, 0) % 16 - a - 1
        total = total + jnp.where(kept, rows, 0.0)
    bq[...] = total.astype(bf16)


def place_flux(flux, bf, bb):
    taps = flux[...]
    shape = (C, 20 * C)
    tiled = dot(taps, ones_where(iota(shape, 1) % C == iota(shape, 0))).astype(bf16)
    shape = (3 * TALL, 3)
    rows = dot(ones_where(iota(shape, 1) == iota(shape, 0) // TALL), tiled)
    x, i = iota(rows.shape, 0) % TALL, iota(rows.shape, 1) // C
    first = iota(rows.shape, 0) < TALL
    factor = jnp.where(i == x - 1, 0.5, jnp.where(i == x - 3, -0.5, 0.0))
    factor = jnp.where(first, factor, jnp.where(i == x - 2, 1.0, 0.0))
    bf[...] = (rows * factor).astype(bf16)
    pick = ones_where(iota((3, 96), 0) == (iota((3, 96), 1) // 16) % 3)
    columns = dot_rows(taps, pick)
    j = iota(columns.shape, 1) % 16
    for i in range(14):
        bb[i * C : (i + 1) * C, :] = jnp.where(j == i + 1, columns, 0.0).astype(bf16)


def row_to_column(row):
    size = row.shape[1]
    wide = jnp.broadcast_to(row, (size, size))
    return jnp.sum(
        jnp.where(iota((size, size), 0) == iota((size, size), 1), wide, 0.0),
        axis=1,
        keepdims=True,
    )


def remote(source, target, sems, peer):
    copy = pltpu.make_async_remote_copy(
        src_ref=source,
        dst_ref=target,
        send_sem=sems[0],
        recv_sem=sems[1],
        device_id=peer,
        device_id_type=MESH,
    )
    copy.start()


def send_around(ext, sems, place):
    (me_x, size_x), (me_y, size_y) = place
    width = ext.shape[-1]
    side = (width - LANES) // 2
    lead = (slice(None),) * (len(ext.shape) - 2)
    sources = {0: slice(side, side + LANES), 1: slice(LANES, side + LANES), -1: slice(side, 2 * side)}
    targets = {0: slice(side, side + LANES), 1: slice(0, side), -1: slice(side + LANES, width)}
    rows = {0: OWN_ROWS, 1: slice(0, ROWS), -1: slice(2 * ROWS, TALL)}
    for dx, dy in AROUND:
        peer = (
            lax.rem(me_x + dx + size_x, size_x),
            lax.rem(me_y + dy + size_y, size_y),
        )
        source = ext.at[lead + (OWN_ROWS, sources[dy])]
        remote(source, ext.at[lead + (rows[dx], targets[dy])], sems, peer)
    depth = ext.shape[0] if lead else 1
    return depth * (3 * width - LANES) // 128


def wait_tiles(sem, gauge, count):
    part = gauge.at[pl.ds(0, 8 * count)]
    pltpu.make_async_copy(part, part, sem).wait()


def far_first_x(me_x, me_y, size):
    groups, ring, cores = (2, size // 4, 2) if size % 8 == 0 else (1, size, 1)
    steps = [
        (g, r, c) for g in range(groups) for r in range(ring) for c in range(cores)
    ][1:]
    steps.sort(key=lambda step: (-step[0] - min(step[1], ring - step[1]), -step[2]))
    at = lax.div(me_x, ring * cores), lax.rem(lax.div(me_x, cores), ring), lax.rem(me_x, cores)
    peers = []
    for g, r, c in steps:
        to = lax.rem(at[0] + g, groups), lax.rem(at[1] + r, ring), lax.rem(at[2] + c, cores)
        peers.append(((to[0] * ring + to[1]) * cores + to[2], me_y))
    return peers


def far_first_y(me_x, me_y, size_x, size_y):
    ring = size_y // 2
    steps = [(g, r) for g in range(2) for r in range(ring)][1:]
    steps.sort(key=lambda step: -step[0] - min(step[1], ring - step[1]))
    high, at = lax.div(me_y, ring), lax.rem(me_y, ring)
    return [
        (
            lax.rem(me_x + g * (size_x // 2), size_x),
            lax.rem(high + g, 2) * ring + lax.rem(at + r, ring),
        )
        for g, r in steps
    ]


def kernel(
    size_x, size_y, scale,
    field, cotangent, kappa, vel, conv_in_in, bias_in_in, conv_mid_in, bias_mid_in, flux_in,
    out_field, out_sums, out_small,
    f_ext, f1_ext, g_ext, a_ext, kv_ext, conv_in, bias_in_row, conv_mid, bias_mid_row, flux,
    bias_in, bias_mid, wide, b0, w_fwd, bf, bb, w_bwd, bq,
    stack_one, stack_two, two_one, two_two, spread, grad_stack, grad_one,
    sums, recv_x, recv_y, gathered, small, small_x, small_y, gauge,
    local_sem, send_sem, recv_sem,
):
    me_x, me_y = lax.axis_index("gx"), lax.axis_index("gy")
    place = (me_x, size_x), (me_y, size_y)
    half_x, half_y = size_x // 2, size_y // 2
    mine_hi = lax.div(me_y, half_y)
    peers_x, peers_y = far_first_x(me_x, me_y, size_x), far_first_y(me_x, me_y, size_x, size_y)
    near = [
        (lax.rem(me_x + dx + size_x, size_x), lax.rem(me_y + dy + size_y, size_y))
        for dx, dy in AROUND
        if dy != 0
    ]
    barrier = pltpu.get_barrier_semaphore()
    for peer in peers_y + near + peers_x:
        pl.semaphore_signal(barrier, inc=1, device_id=peer, device_id_type=MESH)
    own = (OWN_ROWS, OWN_LANES)
    broad_own = (OWN_ROWS, slice(256, 256 + LANES))
    arrivals = []
    for source, target in (
        (field, f_ext.at[broad_own]),
        (cotangent, g_ext.at[own]),
        (kappa, kv_ext.at[(0,) + broad_own]),
        (vel, kv_ext.at[(slice(1, 4),) + broad_own]),
        (conv_in_in, conv_in),
        (bias_in_in, bias_in_row),
        (conv_mid_in, conv_mid),
        (bias_mid_in, bias_mid_row),
        (flux_in, flux),
    ):
        copy = pltpu.make_async_copy(source, target, local_sem.at[len(arrivals)])
        copy.start()
        arrivals.append(copy)
    for copy in arrivals:
        copy.wait()
    sems = lambda number: (send_sem.at[number], recv_sem.at[number])
    pl.semaphore_wait(barrier, len(near + peers_x + peers_y))
    tiles = [
        send_around(ext, sems(number), place) for number, ext in enumerate((f_ext, kv_ext, g_ext))
    ]

    bias_in[...] = row_to_column(bias_in_row[...])
    bias_mid[...] = row_to_column(bias_mid_row[...])
    place_first(conv_in, b0, bq)
    place_middle(conv_mid, wide, w_fwd, w_bwd)
    place_flux(flux, bf, bb)

    weights = (b0, bias_in, w_fwd, bias_mid)
    wait_tiles(recv_sem.at[0], gauge, tiles[0])
    first_one = first_stack(f_ext)
    forward(first_one, 0, weights, stack_one, two_one)
    first_one = first_one[:, MIDDLE]
    wait_tiles(recv_sem.at[1], gauge, tiles[1])
    f1_ext[...] = stepped(f_ext, kv_ext, bf, two_one)
    first_two = first_stack(f1_ext)[:, MIDDLE]
    forward(first_two, 3, weights, stack_two, two_two)

    wait_tiles(recv_sem.at[2], gauge, tiles[2])
    pair_two = flux_pair(g_ext[4:20, :])
    back_two = dot(bb[...], pair_two)
    grad_two = cotangent_two(back_two, two_two, 0, 14).reshape(14 * C, WIDE)
    z_stack(grad_two, grad_stack, -1, 0)
    cotangent_one(w_bwd, stack_two, grad_stack, grad_one, 0, 12)
    adjoint = previous(g_ext[4:20, :], kv_ext, bq, grad_one)
    a_ext[own] = adjoint[4:12, OWN_LANES]
    tiles.append(send_around(a_ext, sems(3), place))

    own_two = grad_two[3 * C : 11 * C]
    mid = middle_terms(stack_two, own_two, spread)
    pair_one = flux_pair(adjoint)
    own_one = cotangent_two(dot(bb[3 * C : 11 * C, :], pair_one), two_one, 6, 14)
    own_one = own_one.reshape(8 * C, WIDE)
    mid = mid + middle_terms(stack_one, own_one, spread)
    sums[:, 0 : 3 * C] = mid[0 : 8 * C]
    for number in range(3):
        sums[number * C : (number + 1) * C, 3 * C :] = mid[
            8 * C : 9 * C, number * C : (number + 1) * C
        ]
    sums[3 * C :, 3 * C :] = jnp.zeros((5 * C, C), f32)

    part = sums.shape[0] // size_x
    share = lambda x: pl.ds(
        pl.multiple_of(lax.rem(x + mine_hi * half_x, size_x) * part, part), part
    )
    for peer in peers_x:
        remote(sums.at[share(peer[0])], recv_x.at[me_x], sems(4), peer)

    in_two, bias_in_two = first_terms(first_two, grad_one)
    rows_two = out_terms(pair_two, two_two, own_two)
    rows_one = out_terms(pair_one, two_one, own_one)
    wait_tiles(recv_sem.at[3], gauge, tiles[3])
    here = a_ext[4:20, :]
    full = cotangent_two(dot(bb[C : 13 * C, :], flux_pair(here)), two_one, 4, 16)
    z_stack(full.reshape(12 * C, WIDE), grad_stack, -1, 1)
    cotangent_one(w_bwd, stack_one, grad_stack, grad_one, 1, 11)
    in_one, bias_in_one = first_terms(first_one, grad_one)
    matrix = jnp.concatenate(
        [in_one + in_two, bias_in_one + bias_in_two]
        + [one + two for one, two in zip(rows_one, rows_two)],
        axis=0,
    )
    for number in range(4):
        small[:, number * C : (number + 1) * C] = matrix[number * 8 : number * 8 + 8]
    small_x[me_x] = small[...]

    per = part // 8
    wait_tiles(recv_sem.at[4], gauge, per * (size_x - 1))
    recv_x[me_x] = sums[share(me_x), :]
    total = recv_x[0]
    for k in range(1, size_x):
        total = total + recv_x[k]
    recv_y[me_y] = total
    for peer in peers_y:
        remote(recv_y.at[me_y], recv_y.at[me_y], sems(5), peer)
    for peer in peers_x:
        remote(small, small_x.at[me_x], sems(7), peer)

    final = previous(here, kv_ext, bq, grad_one)
    out_field[...] = final[4:12, OWN_LANES]

    wait_tiles(recv_sem.at[7], gauge, size_x - 1)
    total = small_x[0]
    for k in range(1, size_x):
        total = total + small_x[k]
    small_y[me_y] = total
    for peer in peers_y:
        remote(small_y.at[me_y], small_y.at[me_y], sems(8), peer)

    wait_tiles(recv_sem.at[5], gauge, per * (size_y - 1))
    total = recv_y[0]
    for k in range(1, size_y):
        total = total + recv_y[k]
    gathered[share(me_x), :] = (total * scale).astype(bf16)
    for peer in peers_x:
        remote(gathered.at[share(me_x)], gathered.at[share(me_x)], sems(6), peer)

    wait_tiles(recv_sem.at[8], gauge, size_y - 1)
    total = small_y[0]
    for k in range(1, size_y):
        total = total + small_y[k]
    out_small[...] = total * scale
    wait_tiles(recv_sem.at[6], gauge, per // 2 * (size_x - 1))
    out_sums[...] = gathered[...]

    for number in range(4):
        wait_tiles(send_sem.at[number], gauge, tiles[number])
    wait_tiles(send_sem.at[4], gauge, per * (size_x - 1))
    wait_tiles(send_sem.at[5], gauge, per * (size_y - 1))
    wait_tiles(send_sem.at[6], gauge, per // 2 * (size_x - 1))
    wait_tiles(send_sem.at[7], gauge, size_x - 1)
    wait_tiles(send_sem.at[8], gauge, size_y - 1)


def unpack(field, sums, small, out_field, out_in, out_bias_in, out_mid, out_bias_mid, out_out):
    out_field[...] = field[...]
    for a in range(3):
        for b in range(3):
            for c in range(3):
                row = (a * 3 + c) * C
                if row < 8 * C:
                    value = sums[row : row + C, b * C : (b + 1) * C]
                else:
                    value = sums[b * C : (b + 1) * C, 3 * C :]
                out_mid[a * 9 + b * 3 + c] = value.astype(f32)
    for number in range(3):
        out_in[number * 8 : number * 8 + 8] = small[:, number * C : (number + 1) * C]
    last = small[:, 3 * C :]
    out_in[24:27] = last[0:3]
    out_bias_in[...] = last[3:4]
    out_bias_mid[...] = last[4:5]
    out_out[...] = last[5:8]


def solution(mesh):
    size_x, size_y = mesh.shape["gx"], mesh.shape["gy"]

    def shards(
        scalar_field, field_cotangent, diffusivity, velocity,
        conv_in, bias_in, conv_mid, bias_mid, flux_out,
    ):
        cells = scalar_field.size * size_x * size_y
        vmem = pl.BlockSpec(memory_space=pltpu.VMEM)
        anywhere = pl.BlockSpec(memory_space=pltpu.HBM)
        part = 256 // size_x
        ext, broad = pltpu.VMEM((TALL, WIDE), f32), pltpu.VMEM((TALL, BROAD), f32)
        shape = jax.ShapeDtypeStruct
        outs = pl.pallas_call(
            lambda *refs: kernel(size_x, size_y, 1.0 / math.sqrt(cells), *refs),
            out_shape=[shape((ROWS, LANES), f32), shape((256, 128), bf16), shape((8, 128), f32)],
            in_specs=[anywhere] * 9,
            out_specs=[vmem] * 3,
            scratch_shapes=[
                broad, broad, ext, ext,
                pltpu.VMEM((4, TALL, BROAD), f32),
                pltpu.VMEM((27, C), bf16),
                pltpu.VMEM((1, C), f32),
                pltpu.VMEM((27, C, C), bf16),
                pltpu.VMEM((1, C), f32),
                pltpu.VMEM((3, C), bf16),
                pltpu.VMEM((C, 1), f32),
                pltpu.VMEM((C, 1), f32),
                pltpu.VMEM((288, 480), f32),
                pltpu.VMEM((22 * C, 9 * TALL), bf16),
                pltpu.VMEM((288, 480), bf16),
                pltpu.VMEM((3 * TALL, 20 * C), bf16),
                pltpu.VMEM((14 * C, 96), bf16),
                pltpu.VMEM((288, 480), bf16),
                pltpu.VMEM((144, 12 * C), bf16),
                pltpu.VMEM((22, 3 * C, BROAD), bf16),
                pltpu.VMEM((16, 3 * C, WIDE), bf16),
                pltpu.VMEM((20, C, BROAD), bf16),
                pltpu.VMEM((14, C, WIDE), bf16),
                pltpu.VMEM((8, 3 * C, WIDE), bf16),
                pltpu.VMEM((14, 3 * C, WIDE), bf16),
                pltpu.VMEM((12, C, WIDE), bf16),
                pltpu.VMEM((256, 128), f32),
                pltpu.VMEM((size_x, part, 128), f32),
                pltpu.VMEM((size_y, part, 128), f32),
                pltpu.VMEM((256, 128), bf16),
                pltpu.VMEM((8, 128), f32),
                pltpu.VMEM((size_x, 8, 128), f32),
                pltpu.VMEM((size_y, 8, 128), f32),
                pltpu.VMEM((640, 128), f32),
                pltpu.SemaphoreType.DMA((9,)),
                pltpu.SemaphoreType.DMA((9,)),
                pltpu.SemaphoreType.DMA((9,)),
            ],
            compiler_params=pltpu.CompilerParams(
                collective_id=0, has_side_effects=True, vmem_limit_bytes=60 * 1024 * 1024
            ),
        )(
            scalar_field, field_cotangent, diffusivity, velocity,
            conv_in, bias_in.reshape(1, C), conv_mid, bias_mid.reshape(1, C), flux_out.T,
        )
        outs = pl.pallas_call(
            unpack,
            out_shape=[
                shape((ROWS, LANES), f32),
                shape((27, C), f32),
                shape((1, C), f32),
                shape((27, C, C), f32),
                shape((1, C), f32),
                shape((3, C), f32),
            ],
            in_specs=[vmem] * 3,
            out_specs=[vmem] * 6,
        )(*outs)
        return (outs[0], outs[1], outs[2].reshape(C), outs[3], outs[4].reshape(C), outs[5].T)

    return jax.shard_map(
        shards,
        mesh=mesh,
        in_specs=(
            P("gx", "gy"), P("gx", "gy"), P("gx", "gy"), P(None, "gx", "gy"),
            P(), P(), P(), P(), P(),
        ),
        out_specs=(P("gx", "gy"), P(), P(), P(), P(), P()),
        check_vma=False,
    )
```

```python
import math

import jax
import jax.numpy as jnp
from jax import lax
from jax.experimental import pallas as pl
from jax.experimental.pallas import tpu as pltpu
from jax.sharding import PartitionSpec as P

NZ = 32
C = 32
ROWS = 8
LANES = 512
HALO = 128
WIDE = LANES + 2 * HALO
TALL = 3 * ROWS
BROAD = WIDE + 256
MIDDLE = slice(128, 128 + WIDE)
time_step = 0.2
MESH = pl.DeviceIdType.MESH
STEPS = (-1, 0, 1)
AROUND = ((1, 1), (1, -1), (-1, 1), (-1, -1), (0, 1), (0, -1), (1, 0), (-1, 0))
OWN_ROWS = slice(ROWS, 2 * ROWS)
OWN_LANES = slice(HALO, HALO + LANES)
bf16 = jnp.bfloat16
f32 = jnp.float32


def shifted(values, count):
    if count == 0:
        return values
    return pltpu.roll(values, (-count) % values.shape[-1], axis=values.ndim - 1)


def lane_index(values):
    return lax.broadcasted_iota(jnp.int32, values.shape, values.ndim - 1)


def lifted(values, step_z):
    if step_z == 0:
        return values
    edge = NZ - 1 if step_z == 1 else 0
    moved = shifted(values, step_z)
    return jnp.where(lane_index(values) % NZ == edge, jnp.zeros_like(moved), moved)


def own_lanes_only(values):
    lane = lane_index(values)
    return jnp.where((lane >= HALO) & (lane < HALO + LANES), values, jnp.zeros_like(values))


def dot(left, right):
    return lax.dot_general(left, right, (((1,), (0,)), ((), ())), preferred_element_type=f32)


def dot_lanes(left, right):
    return lax.dot_general(left, right, (((1,), (1,)), ((), ())), preferred_element_type=f32)


def central_y(values):
    return 0.5 * (shifted(values, NZ) - shifted(values, -NZ))


def central_z(values):
    return 0.5 * (lifted(values, 1) - lifted(values, -1))


def column_to_row(column):
    size = column.shape[0]
    wide = jnp.broadcast_to(column, (size, size))
    row = lax.broadcasted_iota(jnp.int32, (size, size), 0)
    col = lax.broadcasted_iota(jnp.int32, (size, size), 1)
    return jnp.sum(jnp.where(row == col, wide, 0.0), axis=0, keepdims=True)


def first_stack(field_ext):
    rounded = field_ext[...].astype(bf16).astype(f32)
    rows = [shifted(rounded, NZ * b) for b in STEPS]
    moves = [lifted(row, c) for row in rows for c in STEPS]
    return jnp.concatenate(moves, axis=0).astype(bf16)


def z_stack(values, target, sign, start):
    count, width = values.shape[0] // C, values.shape[1]
    wide = values.astype(f32)
    for number, c in enumerate(STEPS):
        moved = lifted(wide, sign * c).astype(bf16) if c else values
        target[start : start + count, number * C : (number + 1) * C, :] = moved.reshape(
            count, C, width
        )


def middle_conv(weights, stack, start, count, sign):
    width = stack.shape[2]
    window = stack[start : start + count + 2].reshape((count + 2) * 3 * C, width)
    banded = weights[0 : count * 3 * C, 0 : (count + 2) * 3 * C]
    out = dot(banded, window).reshape(count, 3, C, width)
    result = out[:, 1]
    for number, b in ((0, -1), (2, 1)):
        part = out[:, number].reshape(count * C, width)
        result = result + shifted(part, sign * NZ * b).reshape(count, C, width)
    return result


def groups(low, high):
    return [(start, min(3, high - start)) for start in range(low, high, 3)]


def forward(first, low, weights, stack, hidden_two):
    b0, bias_in, w_fwd, bias_mid = weights
    count, width = stack.shape[0], stack.shape[2]
    pre = dot(b0[low * C : (low + count) * C, :], first).reshape(count, C, width)
    filled = 0
    for start, rows in groups(0, count - 2):
        until = min(start + rows + 5, count) if start else 5
        if start == 0 or until > filled:
            hidden_one = jnp.tanh(pre[filled:until] + bias_in[...][None]).astype(bf16)
            z_stack(hidden_one.reshape((until - filled) * C, width), stack, 1, filled)
            filled = until
        out = middle_conv(w_fwd, stack, start, rows, 1)
        hidden_two[start : start + rows] = jnp.tanh(out + bias_mid[...][None]).astype(bf16)


def stepped(field_ext, kv_ext, bf, hidden_two):
    flux = dot(bf[...], hidden_two[...].reshape(18 * C, BROAD))
    correction = flux[0:TALL] + central_y(flux[TALL : 2 * TALL]) + central_z(flux[2 * TALL :])
    here = field_ext[...]
    up, down = row_moved(here, 1), row_moved(here, -1)
    laplace = (
        up + down + shifted(here, NZ) + shifted(here, -NZ) + lifted(here, 1) + lifted(here, -1)
    )
    physics = kv_ext[0] * (laplace - 6.0 * here)
    physics = physics - kv_ext[1] * (0.5 * (up - down))
    physics = physics - kv_ext[2] * central_y(here)
    physics = physics - kv_ext[3] * central_z(here)
    return here + time_step * (physics + correction)


def row_moved(values, count):
    return pltpu.roll(values, (-count) % values.shape[0], axis=0)


def flux_pair(here):
    parts = [
        -0.5 * time_step * (row_moved(here, 1) - row_moved(here, -1)),
        -time_step * central_y(here),
        -time_step * central_z(here),
    ]
    flux = jnp.concatenate(parts, axis=0)
    high = flux.astype(bf16)
    low = (flux - high.astype(f32)).astype(bf16)
    return jnp.concatenate([high, low], axis=0)


def cotangent_two(back, hidden_two, low, high):
    two = centre(hidden_two, low, high).astype(f32)
    return (back.reshape(high - low, C, WIDE) * (1.0 - two * two)).astype(bf16)


def centre(ref, low, high):
    margin = (ref.shape[2] - WIDE) // 2
    return ref[low:high, :, margin : margin + WIDE]


def middle_terms(stack, values, spread):
    rows = values.shape[0] // C
    first_row = (stack.shape[0] - rows) // 2 - 1
    wide = values.astype(f32)
    for number, b in enumerate(STEPS):
        moved = shifted(wide, -NZ * b).astype(bf16) if b else values
        spread[0:rows, number * C : (number + 1) * C, :] = moved.reshape(rows, C, WIDE)
    pairs = jnp.zeros((12 * C, 6 * C), f32)
    for x in range(0, rows, 2):
        window = centre(stack, first_row + x, first_row + x + 4).reshape(12 * C, WIDE)
        pairs = pairs + dot_lanes(window, spread[x : x + 2].reshape(6 * C, WIDE))
    return pairs[0 : 9 * C, 0 : 3 * C] + pairs[3 * C :, 3 * C :]


def channel_sums(values):
    wide = values.astype(f32).reshape(values.shape[0] // C, C, WIDE)
    return column_to_row(jnp.sum(jnp.sum(wide, axis=0), axis=1, keepdims=True))


def out_terms(pair, hidden_two, rows):
    first_row = (hidden_two.shape[0] - rows) // 2
    two = centre(hidden_two, first_row, first_row + rows)
    outer = dot_lanes(two.reshape(rows * C, WIDE), pair)
    row_x = lax.broadcasted_iota(jnp.int32, outer.shape, 0) // C
    col = lax.broadcasted_iota(jnp.int32, outer.shape, 1)
    outer = jnp.where(col % 16 == row_x + 8 - rows // 2, outer, 0.0)
    outer = jnp.sum(outer.reshape(rows, C, outer.shape[1]), axis=0)
    kind = (lax.broadcasted_iota(jnp.int32, outer.shape, 1) // 16) % 3
    columns = [jnp.sum(jnp.where(kind == d, outer, 0.0), axis=1, keepdims=True) for d in range(3)]
    return [column_to_row(column) for column in columns]


def cotangent_one(w_bwd, stack, grad_stack, grad_one):
    for start, rows in groups(0, 10):
        back = middle_conv(w_bwd, grad_stack, start, rows, -1)
        first = start + (stack.shape[0] - 10) // 2
        one = centre(stack, first, first + rows)[:, C : 2 * C].astype(f32)
        grad_one[start : start + rows] = (back * (1.0 - one * one)).astype(bf16)


def first_terms(first, grad_one):
    own = own_lanes_only(grad_one[1:9].reshape(8 * C, WIDE).astype(f32))
    outer = dot_lanes(first, own.astype(bf16))
    row_x = lax.broadcasted_iota(jnp.int32, outer.shape, 0) % TALL
    col_x = lax.broadcasted_iota(jnp.int32, outer.shape, 1) // C
    parts = []
    for a in range(3):
        kept = jnp.where(row_x - col_x == a + 7, outer, 0.0)
        parts.append(jnp.sum(kept.reshape(9, TALL, 8 * C), axis=1))
    folded = jnp.concatenate(parts, axis=0)
    folded = folded[:, :128] + folded[:, 128:]
    folded = folded + pltpu.roll(folded, 64, axis=1)
    folded = folded + pltpu.roll(folded, 32, axis=1)
    return folded[:, :C], channel_sums(own)


def previous(here, kv_ext, bq, grad_one):
    spread = dot(bq[...], grad_one[...].reshape(10 * C, WIDE))
    total = here
    for row, b in enumerate(STEPS):
        taps = [spread[(row * 3 + i) * 16 : (row * 3 + i + 1) * 16] for i in range(3)]
        lift = lifted(taps[0], 1) + taps[1] + lifted(taps[2], -1)
        total = total + shifted(lift, -NZ * b)
    cell = lambda number: kv_ext[number, 4:20, MIDDLE]
    scaled = cell(0) * here
    physics = row_moved(scaled, 1) + row_moved(scaled, -1) - 6.0 * scaled
    physics = physics + shifted(scaled, NZ) + shifted(scaled, -NZ)
    physics = physics + lifted(scaled, 1) + lifted(scaled, -1)
    scaled = cell(1) * here
    physics = physics + 0.5 * (row_moved(scaled, 1) - row_moved(scaled, -1))
    physics = physics + central_y(cell(2) * here) + central_z(cell(3) * here)
    return total + time_step * physics


def iota(shape, dimension):
    return lax.broadcasted_iota(jnp.int32, shape, dimension)


def ones_where(condition):
    return jnp.where(condition, 1.0, 0.0).astype(bf16)


def dot_rows(left, right):
    return lax.dot_general(left, right, (((0,), (0,)), ((), ())), preferred_element_type=f32)


def place_middle(conv_mid, wide, w_fwd, w_bwd):
    for target, backward in ((w_fwd, False), (w_bwd, True)):
        wide[...] = jnp.zeros_like(wide)
        for a in range(3):
            for b in range(3):
                for c in range(3):
                    block = conv_mid[a * 9 + b * 3 + c].astype(f32)
                    if not backward:
                        block = block.T
                    for x in range(3):
                        row = (x * 3 + b) * C
                        col = ((x + (2 - a if backward else a)) * 3 + c) * C
                        wide[row : row + C, col : col + C] = block
        target[...] = wide[...].astype(bf16)


def place_first(conv_in, b0, bq):
    taps = conv_in[...]
    shape = (27, 9 * TALL)
    spread = []
    for a in range(3):
        pick = ones_where(iota(shape, 0) == iota(shape, 1) // TALL + 9 * a)
        spread.append(dot_rows(taps, pick))
    j = iota(spread[0].shape, 1) % TALL
    for i in range(22):
        rows = sum(jnp.where(j == i + a, spread[a], 0.0) for a in range(3))
        b0[i * C : (i + 1) * C, :] = rows.astype(bf16)
    shape = (C, 10 * C)
    tiled = dot(taps, ones_where(iota(shape, 1) % C == iota(shape, 0))).astype(bf16)
    total = 0.0
    for a in range(3):
        pick = ones_where(iota((144, 27), 1) == iota((144, 27), 0) // 16 + 9 * a)
        rows = dot(pick, tiled)
        kept = iota(rows.shape, 1) // C == iota(rows.shape, 0) % 16 - a - 2
        total = total + jnp.where(kept, rows, 0.0)
    bq[...] = total.astype(bf16)


def place_flux(flux, bf, bb):
    taps = flux[...]
    shape = (C, 18 * C)
    tiled = dot(taps, ones_where(iota(shape, 1) % C == iota(shape, 0))).astype(bf16)
    shape = (3 * TALL, 3)
    rows = dot(ones_where(iota(shape, 1) == iota(shape, 0) // TALL), tiled)
    x, i = iota(rows.shape, 0) % TALL, iota(rows.shape, 1) // C
    first = iota(rows.shape, 0) < TALL
    factor = jnp.where(i == x - 2, 0.5, jnp.where(i == x - 4, -0.5, 0.0))
    factor = jnp.where(first, factor, jnp.where(i == x - 3, 1.0, 0.0))
    bf[...] = (rows * factor).astype(bf16)
    pick = ones_where(iota((3, 96), 0) == (iota((3, 96), 1) // 16) % 3)
    columns = dot_rows(taps, pick)
    j = iota(columns.shape, 1) % 16
    for i in range(14):
        bb[i * C : (i + 1) * C, :] = jnp.where(j == i + 1, columns, 0.0).astype(bf16)


def row_to_column(row):
    size = row.shape[1]
    wide = jnp.broadcast_to(row, (size, size))
    return jnp.sum(
        jnp.where(iota((size, size), 0) == iota((size, size), 1), wide, 0.0),
        axis=1,
        keepdims=True,
    )


def remote(source, target, sems, peer):
    copy = pltpu.make_async_remote_copy(
        src_ref=source,
        dst_ref=target,
        send_sem=sems[0],
        recv_sem=sems[1],
        device_id=peer,
        device_id_type=MESH,
    )
    copy.start()


def send_around(ext, sems, place):
    (me_x, size_x), (me_y, size_y) = place
    width = ext.shape[-1]
    side = (width - LANES) // 2
    lead = (slice(None),) * (len(ext.shape) - 2)
    sources = {0: slice(side, side + LANES), 1: slice(LANES, side + LANES), -1: slice(side, 2 * side)}
    targets = {0: slice(side, side + LANES), 1: slice(0, side), -1: slice(side + LANES, width)}
    rows = {0: OWN_ROWS, 1: slice(0, ROWS), -1: slice(2 * ROWS, TALL)}
    for dx, dy in AROUND:
        peer = (
            lax.rem(me_x + dx + size_x, size_x),
            lax.rem(me_y + dy + size_y, size_y),
        )
        source = ext.at[lead + (OWN_ROWS, sources[dy])]
        remote(source, ext.at[lead + (rows[dx], targets[dy])], sems, peer)
    depth = ext.shape[0] if lead else 1
    return depth * (3 * width - LANES) // 128


def wait_tiles(sem, gauge, count):
    part = gauge.at[pl.ds(0, 8 * count)]
    pltpu.make_async_copy(part, part, sem).wait()


def far_first_x(me_x, me_y, size):
    groups, ring, cores = (2, size // 4, 2) if size % 8 == 0 else (1, size, 1)
    steps = [
        (g, r, c) for g in range(groups) for r in range(ring) for c in range(cores)
    ][1:]
    steps.sort(key=lambda step: (-step[0] - min(step[1], ring - step[1]), -step[2]))
    at = lax.div(me_x, ring * cores), lax.rem(lax.div(me_x, cores), ring), lax.rem(me_x, cores)
    peers = []
    for g, r, c in steps:
        to = lax.rem(at[0] + g, groups), lax.rem(at[1] + r, ring), lax.rem(at[2] + c, cores)
        peers.append(((to[0] * ring + to[1]) * cores + to[2], me_y))
    return peers


def far_first_y(me_x, me_y, size_x, size_y):
    ring = size_y // 2
    steps = [(g, r) for g in range(2) for r in range(ring)][1:]
    steps.sort(key=lambda step: -step[0] - min(step[1], ring - step[1]))
    high, at = lax.div(me_y, ring), lax.rem(me_y, ring)
    return [
        (
            lax.rem(me_x + g * (size_x // 2), size_x),
            lax.rem(high + g, 2) * ring + lax.rem(at + r, ring),
        )
        for g, r in steps
    ]


def kernel(
    size_x, size_y, scale,
    field, cotangent, kappa, vel, conv_in_in, bias_in_in, conv_mid_in, bias_mid_in, flux_in,
    out_field, out_sums, out_small,
    f_ext, f1_ext, g_ext, a_ext, kv_ext, conv_in, bias_in_row, conv_mid, bias_mid_row, flux,
    bias_in, bias_mid, wide, b0, w_fwd, bf, bb, w_bwd, bq,
    stack_one, stack_two, two_one, two_two, spread, grad_stack, grad_one,
    sums, recv_x, recv_y, gathered, small, small_x, small_y, gauge,
    local_sem, send_sem, recv_sem,
):
    me_x, me_y = lax.axis_index("gx"), lax.axis_index("gy")
    place = (me_x, size_x), (me_y, size_y)
    half_x, half_y = size_x // 2, size_y // 2
    mine_hi = lax.div(me_y, half_y)
    peers_x, peers_y = far_first_x(me_x, me_y, size_x), far_first_y(me_x, me_y, size_x, size_y)
    near = [
        (lax.rem(me_x + dx + size_x, size_x), lax.rem(me_y + dy + size_y, size_y))
        for dx, dy in AROUND
        if dy != 0
    ]
    barrier = pltpu.get_barrier_semaphore()
    for peer in peers_y + near + peers_x:
        pl.semaphore_signal(barrier, inc=1, device_id=peer, device_id_type=MESH)
    own = (OWN_ROWS, OWN_LANES)
    broad_own = (OWN_ROWS, slice(256, 256 + LANES))
    arrivals = []
    for source, target in (
        (field, f_ext.at[broad_own]),
        (cotangent, g_ext.at[own]),
        (kappa, kv_ext.at[(0,) + broad_own]),
        (vel, kv_ext.at[(slice(1, 4),) + broad_own]),
        (conv_in_in, conv_in),
        (bias_in_in, bias_in_row),
        (conv_mid_in, conv_mid),
        (bias_mid_in, bias_mid_row),
        (flux_in, flux),
    ):
        copy = pltpu.make_async_copy(source, target, local_sem.at[len(arrivals)])
        copy.start()
        arrivals.append(copy)
    for copy in arrivals:
        copy.wait()
    sems = lambda number: (send_sem.at[number], recv_sem.at[number])
    pl.semaphore_wait(barrier, len(near + peers_x + peers_y))
    tiles = [
        send_around(ext, sems(number), place) for number, ext in enumerate((f_ext, kv_ext, g_ext))
    ]

    bias_in[...] = row_to_column(bias_in_row[...])
    bias_mid[...] = row_to_column(bias_mid_row[...])
    place_first(conv_in, b0, bq)
    place_middle(conv_mid, wide, w_fwd, w_bwd)
    place_flux(flux, bf, bb)

    weights = (b0, bias_in, w_fwd, bias_mid)
    wait_tiles(recv_sem.at[0], gauge, tiles[0])
    first_one = first_stack(f_ext)
    forward(first_one, 1, weights, stack_one, two_one)
    first_one = first_one[:, MIDDLE]
    wait_tiles(recv_sem.at[1], gauge, tiles[1])
    f1_ext[...] = stepped(f_ext, kv_ext, bf, two_one)
    first_two = first_stack(f1_ext)[:, MIDDLE]
    forward(first_two, 4, weights, stack_two, two_two)

    wait_tiles(recv_sem.at[2], gauge, tiles[2])
    pair_two = flux_pair(g_ext[4:20, :])
    back_two = dot(bb[C : 13 * C, :], pair_two)
    grad_two = cotangent_two(back_two, two_two, 0, 12).reshape(12 * C, WIDE)
    z_stack(grad_two, grad_stack, -1, 0)
    cotangent_one(w_bwd, stack_two, grad_stack, grad_one)
    adjoint = previous(g_ext[4:20, :], kv_ext, bq, grad_one)
    a_ext[own] = adjoint[4:12, OWN_LANES]
    tiles.append(send_around(a_ext, sems(3), place))

    own_two = own_lanes_only(grad_two[2 * C : 10 * C].astype(f32)).astype(bf16)
    mid = middle_terms(stack_two, own_two, spread)
    row = lax.broadcasted_iota(jnp.int32, adjoint.shape, 0)
    share_one = own_lanes_only(jnp.where((row >= 4) & (row < 12), adjoint, 0.0))
    pair_one = flux_pair(share_one)
    back_one = dot(bb[2 * C : 12 * C, :], pair_one)
    own_one = cotangent_two(back_one, two_one, 4, 14).reshape(10 * C, WIDE)
    mid = mid + middle_terms(stack_one, own_one, spread)
    sums[:, 0 : 3 * C] = mid[0 : 8 * C]
    for number in range(3):
        sums[number * C : (number + 1) * C, 3 * C :] = mid[
            8 * C : 9 * C, number * C : (number + 1) * C
        ]
    sums[3 * C :, 3 * C :] = jnp.zeros((5 * C, C), f32)

    part = sums.shape[0] // size_x
    share = lambda x: pl.ds(
        pl.multiple_of(lax.rem(x + mine_hi * half_x, size_x) * part, part), part
    )
    for peer in peers_x:
        remote(sums.at[share(peer[0])], recv_x.at[me_x], sems(4), peer)

    in_two, bias_in_two = first_terms(first_two, grad_one)
    pair_two = own_lanes_only(pair_two.astype(f32)).astype(bf16)
    rows_two = [channel_sums(own_two)] + out_terms(pair_two, two_two, 8)
    rows_one = out_terms(pair_one, two_one, 10)
    wait_tiles(recv_sem.at[3], gauge, tiles[3])
    here = a_ext[4:20, :]
    full = cotangent_two(dot(bb[C : 13 * C, :], flux_pair(here)), two_one, 3, 15)
    full = full.reshape(12 * C, WIDE)
    z_stack(full, grad_stack, -1, 0)
    rows_one = [channel_sums(own_lanes_only(full[2 * C : 10 * C].astype(f32)))] + rows_one
    cotangent_one(w_bwd, stack_one, grad_stack, grad_one)
    in_one, bias_in_one = first_terms(first_one, grad_one)
    matrix = jnp.concatenate(
        [in_one + in_two, bias_in_one + bias_in_two]
        + [one + two for one, two in zip(rows_one, rows_two)],
        axis=0,
    )
    for number in range(4):
        small[:, number * C : (number + 1) * C] = matrix[number * 8 : number * 8 + 8]
    small_x[me_x] = small[...]

    per = part // 8
    wait_tiles(recv_sem.at[4], gauge, per * (size_x - 1))
    recv_x[me_x] = sums[share(me_x), :]
    total = recv_x[0]
    for k in range(1, size_x):
        total = total + recv_x[k]
    recv_y[me_y] = total
    for peer in peers_y:
        remote(recv_y.at[me_y], recv_y.at[me_y], sems(5), peer)
    for peer in peers_x:
        remote(small, small_x.at[me_x], sems(7), peer)

    final = previous(here, kv_ext, bq, grad_one)
    out_field[...] = final[4:12, OWN_LANES]

    wait_tiles(recv_sem.at[7], gauge, size_x - 1)
    total = small_x[0]
    for k in range(1, size_x):
        total = total + small_x[k]
    small_y[me_y] = total
    for peer in peers_y:
        remote(small_y.at[me_y], small_y.at[me_y], sems(8), peer)

    wait_tiles(recv_sem.at[5], gauge, per * (size_y - 1))
    total = recv_y[0]
    for k in range(1, size_y):
        total = total + recv_y[k]
    gathered[share(me_x), :] = (total * scale).astype(bf16)
    for peer in peers_x:
        remote(gathered.at[share(me_x)], gathered.at[share(me_x)], sems(6), peer)

    wait_tiles(recv_sem.at[8], gauge, size_y - 1)
    total = small_y[0]
    for k in range(1, size_y):
        total = total + small_y[k]
    out_small[...] = total * scale
    wait_tiles(recv_sem.at[6], gauge, per // 2 * (size_x - 1))
    out_sums[...] = gathered[...]

    for number in range(4):
        wait_tiles(send_sem.at[number], gauge, tiles[number])
    wait_tiles(send_sem.at[4], gauge, per * (size_x - 1))
    wait_tiles(send_sem.at[5], gauge, per * (size_y - 1))
    wait_tiles(send_sem.at[6], gauge, per // 2 * (size_x - 1))
    wait_tiles(send_sem.at[7], gauge, size_x - 1)
    wait_tiles(send_sem.at[8], gauge, size_y - 1)


def unpack(field, sums, small, out_field, out_in, out_bias_in, out_mid, out_bias_mid, out_out):
    out_field[...] = field[...]
    for a in range(3):
        for b in range(3):
            for c in range(3):
                row = (a * 3 + c) * C
                if row < 8 * C:
                    value = sums[row : row + C, b * C : (b + 1) * C]
                else:
                    value = sums[b * C : (b + 1) * C, 3 * C :]
                out_mid[a * 9 + b * 3 + c] = value.astype(f32)
    for number in range(3):
        out_in[number * 8 : number * 8 + 8] = small[:, number * C : (number + 1) * C]
    last = small[:, 3 * C :]
    out_in[24:27] = last[0:3]
    out_bias_in[...] = last[3:4]
    out_bias_mid[...] = last[4:5]
    out_out[...] = last[5:8]


def solution(mesh):
    size_x, size_y = mesh.shape["gx"], mesh.shape["gy"]

    def shards(
        scalar_field, field_cotangent, diffusivity, velocity,
        conv_in, bias_in, conv_mid, bias_mid, flux_out,
    ):
        cells = scalar_field.size * size_x * size_y
        vmem = pl.BlockSpec(memory_space=pltpu.VMEM)
        anywhere = pl.BlockSpec(memory_space=pltpu.HBM)
        part = 256 // size_x
        ext, broad = pltpu.VMEM((TALL, WIDE), f32), pltpu.VMEM((TALL, BROAD), f32)
        shape = jax.ShapeDtypeStruct
        outs = pl.pallas_call(
            lambda *refs: kernel(size_x, size_y, 1.0 / math.sqrt(cells), *refs),
            out_shape=[shape((ROWS, LANES), f32), shape((256, 128), bf16), shape((8, 128), f32)],
            in_specs=[anywhere] * 9,
            out_specs=[vmem] * 3,
            scratch_shapes=[
                broad, broad, ext, ext,
                pltpu.VMEM((4, TALL, BROAD), f32),
                pltpu.VMEM((27, C), bf16),
                pltpu.VMEM((1, C), f32),
                pltpu.VMEM((27, C, C), bf16),
                pltpu.VMEM((1, C), f32),
                pltpu.VMEM((3, C), bf16),
                pltpu.VMEM((C, 1), f32),
                pltpu.VMEM((C, 1), f32),
                pltpu.VMEM((288, 480), f32),
                pltpu.VMEM((22 * C, 9 * TALL), bf16),
                pltpu.VMEM((288, 480), bf16),
                pltpu.VMEM((3 * TALL, 18 * C), bf16),
                pltpu.VMEM((14 * C, 96), bf16),
                pltpu.VMEM((288, 480), bf16),
                pltpu.VMEM((144, 10 * C), bf16),
                pltpu.VMEM((20, 3 * C, BROAD), bf16),
                pltpu.VMEM((14, 3 * C, WIDE), bf16),
                pltpu.VMEM((18, C, BROAD), bf16),
                pltpu.VMEM((12, C, WIDE), bf16),
                pltpu.VMEM((10, 3 * C, WIDE), bf16),
                pltpu.VMEM((12, 3 * C, WIDE), bf16),
                pltpu.VMEM((10, C, WIDE), bf16),
                pltpu.VMEM((256, 128), f32),
                pltpu.VMEM((size_x, part, 128), f32),
                pltpu.VMEM((size_y, part, 128), f32),
                pltpu.VMEM((256, 128), bf16),
                pltpu.VMEM((8, 128), f32),
                pltpu.VMEM((size_x, 8, 128), f32),
                pltpu.VMEM((size_y, 8, 128), f32),
                pltpu.VMEM((640, 128), f32),
                pltpu.SemaphoreType.DMA((9,)),
                pltpu.SemaphoreType.DMA((9,)),
                pltpu.SemaphoreType.DMA((9,)),
            ],
            compiler_params=pltpu.CompilerParams(
                collective_id=0, has_side_effects=True, vmem_limit_bytes=60 * 1024 * 1024
            ),
        )(
            scalar_field, field_cotangent, diffusivity, velocity,
            conv_in, bias_in.reshape(1, C), conv_mid, bias_mid.reshape(1, C), flux_out.T,
        )
        outs = pl.pallas_call(
            unpack,
            out_shape=[
                shape((ROWS, LANES), f32),
                shape((27, C), f32),
                shape((1, C), f32),
                shape((27, C, C), f32),
                shape((1, C), f32),
                shape((3, C), f32),
            ],
            in_specs=[vmem] * 3,
            out_specs=[vmem] * 6,
        )(*outs)
        return (outs[0], outs[1], outs[2].reshape(C), outs[3], outs[4].reshape(C), outs[5].T)

    return jax.shard_map(
        shards,
        mesh=mesh,
        in_specs=(
            P("gx", "gy"), P("gx", "gy"), P("gx", "gy"), P(None, "gx", "gy"),
            P(), P(), P(), P(), P(),
        ),
        out_specs=(P("gx", "gy"), P(), P(), P(), P(), P()),
        check_vma=False,
    )
```

```python
import math

import jax
import jax.numpy as jnp
from jax import lax
from jax.experimental import pallas as pl
from jax.experimental.pallas import tpu as pltpu
from jax.sharding import PartitionSpec as P

NZ = 32
C = 32
ROWS = 8
LANES = 512
HALO = 128
WIDE = LANES + 2 * HALO
TALL = 3 * ROWS
BROAD = WIDE + 256
MIDDLE = slice(128, 128 + WIDE)
time_step = 0.2
MESH = pl.DeviceIdType.MESH
STEPS = (-1, 0, 1)
AROUND = ((1, 1), (1, -1), (-1, 1), (-1, -1), (0, 1), (0, -1), (1, 0), (-1, 0))
OWN_ROWS = slice(ROWS, 2 * ROWS)
OWN_LANES = slice(HALO, HALO + LANES)
bf16 = jnp.bfloat16
f32 = jnp.float32


def shifted(values, count):
    if count == 0:
        return values
    return pltpu.roll(values, (-count) % values.shape[-1], axis=values.ndim - 1)


def lane_index(values):
    return lax.broadcasted_iota(jnp.int32, values.shape, values.ndim - 1)


def lifted(values, step_z):
    if step_z == 0:
        return values
    edge = NZ - 1 if step_z == 1 else 0
    moved = shifted(values, step_z)
    return jnp.where(lane_index(values) % NZ == edge, jnp.zeros_like(moved), moved)


def own_lanes_only(values):
    lane = lane_index(values)
    return jnp.where((lane >= HALO) & (lane < HALO + LANES), values, jnp.zeros_like(values))


def dot(left, right):
    return lax.dot_general(left, right, (((1,), (0,)), ((), ())), preferred_element_type=f32)


def dot_lanes(left, right):
    return lax.dot_general(left, right, (((1,), (1,)), ((), ())), preferred_element_type=f32)


def central_y(values):
    return 0.5 * (shifted(values, NZ) - shifted(values, -NZ))


def central_z(values):
    return 0.5 * (lifted(values, 1) - lifted(values, -1))


def column_to_row(column):
    size = column.shape[0]
    wide = jnp.broadcast_to(column, (size, size))
    row = lax.broadcasted_iota(jnp.int32, (size, size), 0)
    col = lax.broadcasted_iota(jnp.int32, (size, size), 1)
    return jnp.sum(jnp.where(row == col, wide, 0.0), axis=0, keepdims=True)


def first_stack(field_ext):
    rounded = field_ext[...].astype(bf16).astype(f32)
    rows = [shifted(rounded, NZ * b) for b in STEPS]
    moves = [lifted(row, c) for row in rows for c in STEPS]
    return jnp.concatenate(moves, axis=0).astype(bf16)


def z_stack(values, target, sign, start):
    count, width = values.shape[0] // C, values.shape[1]
    wide = values.astype(f32)
    for number, c in enumerate(STEPS):
        moved = lifted(wide, sign * c).astype(bf16) if c else values
        target[start : start + count, number * C : (number + 1) * C, :] = moved.reshape(
            count, C, width
        )


def middle_conv(weights, stack, start, count, sign):
    width = stack.shape[2]
    window = stack[start : start + count + 2].reshape((count + 2) * 3 * C, width)
    banded = weights[0 : count * 3 * C, 0 : (count + 2) * 3 * C]
    out = dot(banded, window).reshape(count, 3, C, width)
    result = out[:, 1]
    for number, b in ((0, -1), (2, 1)):
        part = out[:, number].reshape(count * C, width)
        result = result + shifted(part, sign * NZ * b).reshape(count, C, width)
    return result


def groups(low, high):
    return [(start, min(3, high - start)) for start in range(low, high, 3)]


def forward(first, low, weights, stack, hidden_two):
    b0, bias_in, w_fwd, bias_mid = weights
    count, width = stack.shape[0], stack.shape[2]
    pre = dot(b0[low * C : (low + count) * C, :], first).reshape(count, C, width)
    filled = 0
    for start, rows in groups(0, count - 2):
        until = min(start + rows + 5, count) if start else 5
        if start == 0 or until > filled:
            hidden_one = jnp.tanh(pre[filled:until] + bias_in[...][None]).astype(bf16)
            z_stack(hidden_one.reshape((until - filled) * C, width), stack, 1, filled)
            filled = until
        out = middle_conv(w_fwd, stack, start, rows, 1)
        hidden_two[start : start + rows] = jnp.tanh(out + bias_mid[...][None]).astype(bf16)


def stepped(field_ext, kv_ext, bf, hidden_two):
    flux = dot(bf[...], hidden_two[...].reshape(18 * C, BROAD))
    correction = flux[0:TALL] + central_y(flux[TALL : 2 * TALL]) + central_z(flux[2 * TALL :])
    here = field_ext[...]
    y_up, y_down = shifted(here, NZ)[:, MIDDLE], shifted(here, -NZ)[:, MIDDLE]
    here = here[:, MIDDLE]
    up, down = row_moved(here, 1), row_moved(here, -1)
    laplace = up + down + y_up + y_down + lifted(here, 1) + lifted(here, -1)
    physics = kv_ext[0] * (laplace - 6.0 * here)
    physics = physics - kv_ext[1] * (0.5 * (up - down))
    physics = physics - kv_ext[2] * (0.5 * (y_up - y_down))
    physics = physics - kv_ext[3] * central_z(here)
    return here + time_step * (physics + correction[:, MIDDLE])


def row_moved(values, count):
    return pltpu.roll(values, (-count) % values.shape[0], axis=0)


def flux_pair(here):
    parts = [
        -0.5 * time_step * (row_moved(here, 1) - row_moved(here, -1)),
        -time_step * central_y(here),
        -time_step * central_z(here),
    ]
    flux = jnp.concatenate(parts, axis=0)
    high = flux.astype(bf16)
    low = (flux - high.astype(f32)).astype(bf16)
    return jnp.concatenate([high, low], axis=0)


def cotangent_two(back, hidden_two, low, high):
    two = centre(hidden_two, low, high).astype(f32)
    return (back.reshape(high - low, C, WIDE) * (1.0 - two * two)).astype(bf16)


def centre(ref, low, high):
    margin = (ref.shape[2] - WIDE) // 2
    return ref[low:high, :, margin : margin + WIDE]


def middle_terms(stack, values, spread):
    rows = values.shape[0] // C
    first_row = (stack.shape[0] - rows) // 2 - 1
    wide = values.astype(f32)
    for number, b in enumerate(STEPS):
        moved = shifted(wide, -NZ * b).astype(bf16) if b else values
        spread[0:rows, number * C : (number + 1) * C, :] = moved.reshape(rows, C, WIDE)
    pairs = jnp.zeros((12 * C, 6 * C), f32)
    for x in range(0, rows, 2):
        window = centre(stack, first_row + x, first_row + x + 4).reshape(12 * C, WIDE)
        pairs = pairs + dot_lanes(window, spread[x : x + 2].reshape(6 * C, WIDE))
    return pairs[0 : 9 * C, 0 : 3 * C] + pairs[3 * C :, 3 * C :]


def channel_sums(values):
    wide = values.astype(f32).reshape(values.shape[0] // C, C, WIDE)
    return column_to_row(jnp.sum(jnp.sum(wide, axis=0), axis=1, keepdims=True))


def out_terms(pair, hidden_two, rows):
    first_row = (hidden_two.shape[0] - rows) // 2
    two = centre(hidden_two, first_row, first_row + rows)
    outer = dot_lanes(two.reshape(rows * C, WIDE), pair)
    row_x = lax.broadcasted_iota(jnp.int32, outer.shape, 0) // C
    col = lax.broadcasted_iota(jnp.int32, outer.shape, 1)
    outer = jnp.where(col % 16 == row_x + 8 - rows // 2, outer, 0.0)
    outer = jnp.sum(outer.reshape(rows, C, outer.shape[1]), axis=0)
    kind = (lax.broadcasted_iota(jnp.int32, outer.shape, 1) // 16) % 3
    columns = [jnp.sum(jnp.where(kind == d, outer, 0.0), axis=1, keepdims=True) for d in range(3)]
    return [column_to_row(column) for column in columns]


def cotangent_one(w_bwd, stack, grad_stack, grad_one):
    for start, rows in groups(0, 10):
        back = middle_conv(w_bwd, grad_stack, start, rows, -1)
        first = start + (stack.shape[0] - 10) // 2
        one = centre(stack, first, first + rows)[:, C : 2 * C].astype(f32)
        grad_one[start : start + rows] = (back * (1.0 - one * one)).astype(bf16)


def first_terms(first, grad_one):
    own = own_lanes_only(grad_one[1:9].reshape(8 * C, WIDE).astype(f32))
    outer = dot_lanes(first, own.astype(bf16))
    row_x = lax.broadcasted_iota(jnp.int32, outer.shape, 0) % TALL
    col_x = lax.broadcasted_iota(jnp.int32, outer.shape, 1) // C
    parts = []
    for a in range(3):
        kept = jnp.where(row_x - col_x == a + 7, outer, 0.0)
        parts.append(jnp.sum(kept.reshape(9, TALL, 8 * C), axis=1))
    folded = jnp.concatenate(parts, axis=0)
    folded = folded[:, :128] + folded[:, 128:]
    folded = folded + pltpu.roll(folded, 64, axis=1)
    folded = folded + pltpu.roll(folded, 32, axis=1)
    return folded[:, :C], channel_sums(own)


def previous(here, kv_ext, bq, grad_one):
    spread = dot(bq[...], grad_one[...].reshape(10 * C, WIDE))
    total = here
    for row, b in enumerate(STEPS):
        taps = [spread[(row * 3 + i) * 16 : (row * 3 + i + 1) * 16] for i in range(3)]
        lift = lifted(taps[0], 1) + taps[1] + lifted(taps[2], -1)
        total = total + shifted(lift, -NZ * b)
    cell = lambda number: kv_ext[number, 4:20, :]
    scaled = cell(0) * here
    physics = row_moved(scaled, 1) + row_moved(scaled, -1) - 6.0 * scaled
    physics = physics + shifted(scaled, NZ) + shifted(scaled, -NZ)
    physics = physics + lifted(scaled, 1) + lifted(scaled, -1)
    scaled = cell(1) * here
    physics = physics + 0.5 * (row_moved(scaled, 1) - row_moved(scaled, -1))
    physics = physics + central_y(cell(2) * here) + central_z(cell(3) * here)
    return total + time_step * physics


def iota(shape, dimension):
    return lax.broadcasted_iota(jnp.int32, shape, dimension)


def ones_where(condition):
    return jnp.where(condition, 1.0, 0.0).astype(bf16)


def dot_rows(left, right):
    return lax.dot_general(left, right, (((0,), (0,)), ((), ())), preferred_element_type=f32)


def place_middle(conv_mid, wide, w_fwd, w_bwd):
    for target, backward in ((w_fwd, False), (w_bwd, True)):
        wide[...] = jnp.zeros_like(wide)
        for a in range(3):
            for b in range(3):
                for c in range(3):
                    block = conv_mid[a * 9 + b * 3 + c].astype(f32)
                    if not backward:
                        block = block.T
                    for x in range(3):
                        row = (x * 3 + b) * C
                        col = ((x + (2 - a if backward else a)) * 3 + c) * C
                        wide[row : row + C, col : col + C] = block
        target[...] = wide[...].astype(bf16)


def place_first(conv_in, b0, bq):
    taps = conv_in[...]
    shape = (27, 9 * TALL)
    spread = []
    for a in range(3):
        pick = ones_where(iota(shape, 0) == iota(shape, 1) // TALL + 9 * a)
        spread.append(dot_rows(taps, pick))
    j = iota(spread[0].shape, 1) % TALL
    for i in range(22):
        rows = sum(jnp.where(j == i + a, spread[a], 0.0) for a in range(3))
        b0[i * C : (i + 1) * C, :] = rows.astype(bf16)
    shape = (C, 10 * C)
    tiled = dot(taps, ones_where(iota(shape, 1) % C == iota(shape, 0))).astype(bf16)
    total = 0.0
    for a in range(3):
        pick = ones_where(iota((144, 27), 1) == iota((144, 27), 0) // 16 + 9 * a)
        rows = dot(pick, tiled)
        kept = iota(rows.shape, 1) // C == iota(rows.shape, 0) % 16 - a - 2
        total = total + jnp.where(kept, rows, 0.0)
    bq[...] = total.astype(bf16)


def place_flux(flux, bf, bb):
    taps = flux[...]
    shape = (C, 18 * C)
    tiled = dot(taps, ones_where(iota(shape, 1) % C == iota(shape, 0))).astype(bf16)
    shape = (3 * TALL, 3)
    rows = dot(ones_where(iota(shape, 1) == iota(shape, 0) // TALL), tiled)
    x, i = iota(rows.shape, 0) % TALL, iota(rows.shape, 1) // C
    first = iota(rows.shape, 0) < TALL
    factor = jnp.where(i == x - 2, 0.5, jnp.where(i == x - 4, -0.5, 0.0))
    factor = jnp.where(first, factor, jnp.where(i == x - 3, 1.0, 0.0))
    bf[...] = (rows * factor).astype(bf16)
    pick = ones_where(iota((3, 96), 0) == (iota((3, 96), 1) // 16) % 3)
    columns = dot_rows(taps, pick)
    j = iota(columns.shape, 1) % 16
    for i in range(14):
        bb[i * C : (i + 1) * C, :] = jnp.where(j == i + 1, columns, 0.0).astype(bf16)


def row_to_column(row):
    size = row.shape[1]
    wide = jnp.broadcast_to(row, (size, size))
    return jnp.sum(
        jnp.where(iota((size, size), 0) == iota((size, size), 1), wide, 0.0),
        axis=1,
        keepdims=True,
    )


def remote(source, target, sems, peer):
    copy = pltpu.make_async_remote_copy(
        src_ref=source,
        dst_ref=target,
        send_sem=sems[0],
        recv_sem=sems[1],
        device_id=peer,
        device_id_type=MESH,
    )
    copy.start()


def send_around(ext, sems, place, block=None):
    (me_x, size_x), (me_y, size_y) = place
    width = ext.shape[-1]
    side = (width - LANES) // 2
    lead = (slice(None),) * (len(ext.shape) - 2)
    sources = {0: slice(side, side + LANES), 1: slice(LANES, side + LANES), -1: slice(side, 2 * side)}
    targets = {0: slice(side, side + LANES), 1: slice(0, side), -1: slice(side + LANES, width)}
    rows = {0: OWN_ROWS, 1: slice(0, ROWS), -1: slice(2 * ROWS, TALL)}
    for dx, dy in AROUND:
        peer = (
            lax.rem(me_x + dx + size_x, size_x),
            lax.rem(me_y + dy + size_y, size_y),
        )
        source = ext.at[lead + (OWN_ROWS, sources[dy])]
        if block is not None:
            lanes = sources[dy]
            source = block.at[:, pl.ds(lanes.start - side, lanes.stop - lanes.start)]
        remote(source, ext.at[lead + (rows[dx], targets[dy])], sems, peer)
    depth = ext.shape[0] if lead else 1
    return depth * (3 * width - LANES) // 128


def wait_tiles(sem, gauge, count):
    part = gauge.at[pl.ds(0, 8 * count)]
    pltpu.make_async_copy(part, part, sem).wait()


def far_first_x(me_x, me_y, size):
    groups, ring, cores = (2, size // 4, 2) if size % 8 == 0 else (1, size, 1)
    steps = [
        (g, r, c) for g in range(groups) for r in range(ring) for c in range(cores)
    ][1:]
    steps.sort(key=lambda step: (-step[0] - min(step[1], ring - step[1]), -step[2]))
    at = lax.div(me_x, ring * cores), lax.rem(lax.div(me_x, cores), ring), lax.rem(me_x, cores)
    peers = []
    for g, r, c in steps:
        to = lax.rem(at[0] + g, groups), lax.rem(at[1] + r, ring), lax.rem(at[2] + c, cores)
        peers.append(((to[0] * ring + to[1]) * cores + to[2], me_y))
    return peers


def far_first_y(me_x, me_y, size_x, size_y):
    ring = size_y // 2
    steps = [(g, r) for g in range(2) for r in range(ring)][1:]
    steps.sort(key=lambda step: -step[0] - min(step[1], ring - step[1]))
    high, at = lax.div(me_y, ring), lax.rem(me_y, ring)
    return [
        (
            lax.rem(me_x + g * (size_x // 2), size_x),
            lax.rem(high + g, 2) * ring + lax.rem(at + r, ring),
        )
        for g, r in steps
    ]


def kernel(
    size_x, size_y, scale,
    field, cotangent, kappa, vel, conv_in_in, bias_in_in, conv_mid_in, bias_mid_in, flux_in,
    out_field, out_sums, out_small,
    f_ext, f1_ext, g_ext, a_ext, kv_ext, conv_in, bias_in_row, conv_mid, bias_mid_row, flux,
    bias_in, bias_mid, wide, b0, w_fwd, bf, bb, w_bwd, bq,
    stack_one, stack_two, two_one, two_two, spread, grad_stack, grad_one,
    sums, recv_x, recv_y, gathered, small, small_x, small_y, gauge,
    local_sem, send_sem, recv_sem,
):
    me_x, me_y = lax.axis_index("gx"), lax.axis_index("gy")
    place = (me_x, size_x), (me_y, size_y)
    half_x, half_y = size_x // 2, size_y // 2
    mine_hi = lax.div(me_y, half_y)
    peers_x, peers_y = far_first_x(me_x, me_y, size_x), far_first_y(me_x, me_y, size_x, size_y)
    near = [
        (lax.rem(me_x + dx + size_x, size_x), lax.rem(me_y + dy + size_y, size_y))
        for dx, dy in AROUND
        if dy != 0
    ]
    barrier = pltpu.get_barrier_semaphore()
    for peer in peers_y + near + peers_x:
        pl.semaphore_signal(barrier, inc=1, device_id=peer, device_id_type=MESH)
    own = (OWN_ROWS, OWN_LANES)
    broad_own = (OWN_ROWS, slice(256, 256 + LANES))
    arrivals = []
    for source, target in (
        (field, f_ext.at[broad_own]),
        (cotangent, g_ext.at[own]),
        (kappa, kv_ext.at[(0,) + own]),
        (vel, kv_ext.at[(slice(1, 4),) + own]),
        (conv_in_in, conv_in),
        (bias_in_in, bias_in_row),
        (conv_mid_in, conv_mid),
        (bias_mid_in, bias_mid_row),
        (flux_in, flux),
    ):
        copy = pltpu.make_async_copy(source, target, local_sem.at[len(arrivals)])
        copy.start()
        arrivals.append(copy)
    sems = lambda number: (send_sem.at[number], recv_sem.at[number])
    pl.semaphore_wait(barrier, len(near + peers_x + peers_y))
    tiles = [send_around(f_ext, sems(0), place, field)]
    for copy in arrivals:
        copy.wait()
    tiles += [send_around(kv_ext, sems(1), place), send_around(g_ext, sems(2), place)]

    bias_in[...] = row_to_column(bias_in_row[...])
    bias_mid[...] = row_to_column(bias_mid_row[...])
    place_first(conv_in, b0, bq)
    place_middle(conv_mid, wide, w_fwd, w_bwd)
    place_flux(flux, bf, bb)

    weights = (b0, bias_in, w_fwd, bias_mid)
    wait_tiles(recv_sem.at[0], gauge, tiles[0])
    first_one = first_stack(f_ext)
    forward(first_one, 1, weights, stack_one, two_one)
    first_one = first_one[:, MIDDLE]
    wait_tiles(recv_sem.at[1], gauge, tiles[1])
    f1_ext[...] = stepped(f_ext, kv_ext, bf, two_one)
    first_two = first_stack(f1_ext)
    forward(first_two, 4, weights, stack_two, two_two)

    wait_tiles(recv_sem.at[2], gauge, tiles[2])
    pair_two = flux_pair(g_ext[4:20, :])
    back_two = dot(bb[C : 13 * C, :], pair_two)
    grad_two = cotangent_two(back_two, two_two, 0, 12).reshape(12 * C, WIDE)
    z_stack(grad_two, grad_stack, -1, 0)
    cotangent_one(w_bwd, stack_two, grad_stack, grad_one)
    adjoint = previous(g_ext[4:20, :], kv_ext, bq, grad_one)
    a_ext[own] = adjoint[4:12, OWN_LANES]

    own_two = own_lanes_only(grad_two[2 * C : 10 * C].astype(f32)).astype(bf16)
    mid = middle_terms(stack_two, own_two, spread)
    tiles.append(send_around(a_ext, sems(3), place))
    row = lax.broadcasted_iota(jnp.int32, adjoint.shape, 0)
    share_one = own_lanes_only(jnp.where((row >= 4) & (row < 12), adjoint, 0.0))
    pair_one = flux_pair(share_one)
    back_one = dot(bb[2 * C : 12 * C, :], pair_one)
    own_one = cotangent_two(back_one, two_one, 4, 14).reshape(10 * C, WIDE)
    mid = mid + middle_terms(stack_one, own_one, spread)
    sums[:, 0 : 3 * C] = mid[0 : 8 * C]
    for number in range(3):
        sums[number * C : (number + 1) * C, 3 * C :] = mid[
            8 * C : 9 * C, number * C : (number + 1) * C
        ]
    sums[3 * C :, 3 * C :] = jnp.zeros((5 * C, C), f32)

    part = sums.shape[0] // size_x
    share = lambda x: pl.ds(
        pl.multiple_of(lax.rem(x + mine_hi * half_x, size_x) * part, part), part
    )
    for peer in peers_x:
        remote(sums.at[share(peer[0])], recv_x.at[me_x], sems(4), peer)

    in_two, bias_in_two = first_terms(first_two, grad_one)
    pair_two = own_lanes_only(pair_two.astype(f32)).astype(bf16)
    rows_two = [channel_sums(own_two)] + out_terms(pair_two, two_two, 8)
    rows_one = out_terms(pair_one, two_one, 10)
    wait_tiles(recv_sem.at[3], gauge, tiles[3])
    here = a_ext[4:20, :]
    full = cotangent_two(dot(bb[C : 13 * C, :], flux_pair(here)), two_one, 3, 15)
    full = full.reshape(12 * C, WIDE)
    z_stack(full, grad_stack, -1, 0)
    rows_one = [channel_sums(own_lanes_only(full[2 * C : 10 * C].astype(f32)))] + rows_one
    cotangent_one(w_bwd, stack_one, grad_stack, grad_one)
    in_one, bias_in_one = first_terms(first_one, grad_one)
    matrix = jnp.concatenate(
        [in_one + in_two, bias_in_one + bias_in_two]
        + [one + two for one, two in zip(rows_one, rows_two)],
        axis=0,
    )
    for number in range(4):
        small[:, number * C : (number + 1) * C] = matrix[number * 8 : number * 8 + 8]
    small_x[me_x] = small[...]

    per = part // 8
    wait_tiles(recv_sem.at[4], gauge, per * (size_x - 1))
    recv_x[me_x] = sums[share(me_x), :]
    total = recv_x[0]
    for k in range(1, size_x):
        total = total + recv_x[k]
    recv_y[me_y] = total
    for peer in peers_y:
        remote(recv_y.at[me_y], recv_y.at[me_y], sems(5), peer)
    for peer in peers_x:
        remote(small, small_x.at[me_x], sems(7), peer)

    final = previous(here, kv_ext, bq, grad_one)
    out_field[...] = final[4:12, OWN_LANES]

    wait_tiles(recv_sem.at[7], gauge, size_x - 1)
    total = small_x[0]
    for k in range(1, size_x):
        total = total + small_x[k]
    small_y[me_y] = total
    for peer in peers_y:
        remote(small_y.at[me_y], small_y.at[me_y], sems(8), peer)

    wait_tiles(recv_sem.at[5], gauge, per * (size_y - 1))
    total = recv_y[0]
    for k in range(1, size_y):
        total = total + recv_y[k]
    gathered[share(me_x), :] = (total * scale).astype(bf16)
    for peer in peers_x:
        remote(gathered.at[share(me_x)], gathered.at[share(me_x)], sems(6), peer)

    wait_tiles(recv_sem.at[8], gauge, size_y - 1)
    total = small_y[0]
    for k in range(1, size_y):
        total = total + small_y[k]
    out_small[...] = total * scale
    wait_tiles(recv_sem.at[6], gauge, per // 2 * (size_x - 1))
    out_sums[...] = gathered[...]

    for number in range(4):
        wait_tiles(send_sem.at[number], gauge, tiles[number])
    wait_tiles(send_sem.at[4], gauge, per * (size_x - 1))
    wait_tiles(send_sem.at[5], gauge, per * (size_y - 1))
    wait_tiles(send_sem.at[6], gauge, per // 2 * (size_x - 1))
    wait_tiles(send_sem.at[7], gauge, size_x - 1)
    wait_tiles(send_sem.at[8], gauge, size_y - 1)


def unpack(field, sums, small, out_field, out_in, out_bias_in, out_mid, out_bias_mid, out_out):
    out_field[...] = field[...]
    for a in range(3):
        for b in range(3):
            for c in range(3):
                row = (a * 3 + c) * C
                if row < 8 * C:
                    value = sums[row : row + C, b * C : (b + 1) * C]
                else:
                    value = sums[b * C : (b + 1) * C, 3 * C :]
                out_mid[a * 9 + b * 3 + c] = value.astype(f32)
    for number in range(3):
        out_in[number * 8 : number * 8 + 8] = small[:, number * C : (number + 1) * C]
    last = small[:, 3 * C :]
    out_in[24:27] = last[0:3]
    out_bias_in[...] = last[3:4]
    out_bias_mid[...] = last[4:5]
    out_out[...] = last[5:8]


def solution(mesh):
    size_x, size_y = mesh.shape["gx"], mesh.shape["gy"]

    def shards(
        scalar_field, field_cotangent, diffusivity, velocity,
        conv_in, bias_in, conv_mid, bias_mid, flux_out,
    ):
        cells = scalar_field.size * size_x * size_y
        vmem = pl.BlockSpec(memory_space=pltpu.VMEM)
        anywhere = pl.BlockSpec(memory_space=pltpu.HBM)
        part = 256 // size_x
        ext, broad = pltpu.VMEM((TALL, WIDE), f32), pltpu.VMEM((TALL, BROAD), f32)
        shape = jax.ShapeDtypeStruct
        outs = pl.pallas_call(
            lambda *refs: kernel(size_x, size_y, 1.0 / math.sqrt(cells), *refs),
            out_shape=[shape((ROWS, LANES), f32), shape((256, 128), bf16), shape((8, 128), f32)],
            in_specs=[anywhere] * 9,
            out_specs=[vmem] * 3,
            scratch_shapes=[
                broad, ext, ext, ext,
                pltpu.VMEM((4, TALL, WIDE), f32),
                pltpu.VMEM((27, C), bf16),
                pltpu.VMEM((1, C), f32),
                pltpu.VMEM((27, C, C), bf16),
                pltpu.VMEM((1, C), f32),
                pltpu.VMEM((3, C), bf16),
                pltpu.VMEM((C, 1), f32),
                pltpu.VMEM((C, 1), f32),
                pltpu.VMEM((288, 480), f32),
                pltpu.VMEM((22 * C, 9 * TALL), bf16),
                pltpu.VMEM((288, 480), bf16),
                pltpu.VMEM((3 * TALL, 18 * C), bf16),
                pltpu.VMEM((14 * C, 96), bf16),
                pltpu.VMEM((288, 480), bf16),
                pltpu.VMEM((144, 10 * C), bf16),
                pltpu.VMEM((20, 3 * C, BROAD), bf16),
                pltpu.VMEM((14, 3 * C, WIDE), bf16),
                pltpu.VMEM((18, C, BROAD), bf16),
                pltpu.VMEM((12, C, WIDE), bf16),
                pltpu.VMEM((10, 3 * C, WIDE), bf16),
                pltpu.VMEM((12, 3 * C, WIDE), bf16),
                pltpu.VMEM((10, C, WIDE), bf16),
                pltpu.VMEM((256, 128), f32),
                pltpu.VMEM((size_x, part, 128), f32),
                pltpu.VMEM((size_y, part, 128), f32),
                pltpu.VMEM((256, 128), bf16),
                pltpu.VMEM((8, 128), f32),
                pltpu.VMEM((size_x, 8, 128), f32),
                pltpu.VMEM((size_y, 8, 128), f32),
                pltpu.VMEM((640, 128), f32),
                pltpu.SemaphoreType.DMA((9,)),
                pltpu.SemaphoreType.DMA((9,)),
                pltpu.SemaphoreType.DMA((9,)),
            ],
            compiler_params=pltpu.CompilerParams(
                collective_id=0, has_side_effects=True, vmem_limit_bytes=60 * 1024 * 1024
            ),
        )(
            scalar_field, field_cotangent, diffusivity, velocity,
            conv_in, bias_in.reshape(1, C), conv_mid, bias_mid.reshape(1, C), flux_out.T,
        )
        outs = pl.pallas_call(
            unpack,
            out_shape=[
                shape((ROWS, LANES), f32),
                shape((27, C), f32),
                shape((1, C), f32),
                shape((27, C, C), f32),
                shape((1, C), f32),
                shape((3, C), f32),
            ],
            in_specs=[vmem] * 3,
            out_specs=[vmem] * 6,
        )(*outs)
        return (outs[0], outs[1], outs[2].reshape(C), outs[3], outs[4].reshape(C), outs[5].T)

    return jax.shard_map(
        shards,
        mesh=mesh,
        in_specs=(
            P("gx", "gy"), P("gx", "gy"), P("gx", "gy"), P(None, "gx", "gy"),
            P(), P(), P(), P(), P(),
        ),
        out_specs=(P("gx", "gy"), P(), P(), P(), P(), P()),
        check_vma=False,
    )
```

```python
import math

import jax
import jax.numpy as jnp
from jax import lax
from jax.experimental import pallas as pl
from jax.experimental.pallas import tpu as pltpu
from jax.sharding import PartitionSpec as P

NZ = 32
C = 32
ROWS = 8
LANES = 512
HALO = 128
WIDE = LANES + 2 * HALO
TALL = 3 * ROWS
BROAD = WIDE + 256
MIDDLE = slice(128, 128 + WIDE)
time_step = 0.2
MESH = pl.DeviceIdType.MESH
STEPS = (-1, 0, 1)
AROUND = ((1, 1), (1, -1), (-1, 1), (-1, -1), (0, 1), (0, -1), (1, 0), (-1, 0))
OWN_ROWS = slice(ROWS, 2 * ROWS)
OWN_LANES = slice(HALO, HALO + LANES)
bf16 = jnp.bfloat16
f32 = jnp.float32


def shifted(values, count):
    if count == 0:
        return values
    return pltpu.roll(values, (-count) % values.shape[-1], axis=values.ndim - 1)


def lane_index(values):
    return lax.broadcasted_iota(jnp.int32, values.shape, values.ndim - 1)


def lifted(values, step_z):
    if step_z == 0:
        return values
    edge = NZ - 1 if step_z == 1 else 0
    moved = shifted(values, step_z)
    return jnp.where(lane_index(values) % NZ == edge, jnp.zeros_like(moved), moved)


def own_lanes_only(values):
    lane = lane_index(values)
    return jnp.where((lane >= HALO) & (lane < HALO + LANES), values, jnp.zeros_like(values))


def dot(left, right):
    return lax.dot_general(left, right, (((1,), (0,)), ((), ())), preferred_element_type=f32)


def dot_lanes(left, right):
    return lax.dot_general(left, right, (((1,), (1,)), ((), ())), preferred_element_type=f32)


def central_y(values):
    return 0.5 * (shifted(values, NZ) - shifted(values, -NZ))


def central_z(values):
    return 0.5 * (lifted(values, 1) - lifted(values, -1))


def column_to_row(column):
    size = column.shape[0]
    wide = jnp.broadcast_to(column, (size, size))
    row = lax.broadcasted_iota(jnp.int32, (size, size), 0)
    col = lax.broadcasted_iota(jnp.int32, (size, size), 1)
    return jnp.sum(jnp.where(row == col, wide, 0.0), axis=0, keepdims=True)


def first_stack(field_ext):
    rounded = field_ext[...].astype(bf16).astype(f32)
    rows = [shifted(rounded, NZ * b) for b in STEPS]
    moves = [lifted(row, c) for row in rows for c in STEPS]
    return jnp.concatenate(moves, axis=0).astype(bf16)


def z_stack(values, target, sign, start):
    count, width = values.shape[0] // C, values.shape[1]
    wide = values.astype(f32)
    for number, c in enumerate(STEPS):
        moved = lifted(wide, sign * c).astype(bf16) if c else values
        target[start : start + count, number * C : (number + 1) * C, :] = moved.reshape(
            count, C, width
        )


def middle_conv(weights, stack, start, count, sign):
    width = stack.shape[2]
    window = stack[start : start + count + 2].reshape((count + 2) * 3 * C, width)
    banded = weights[0 : count * 3 * C, 0 : (count + 2) * 3 * C]
    out = dot(banded, window).reshape(count, 3, C, width)
    result = out[:, 1]
    for number, b in ((0, -1), (2, 1)):
        part = out[:, number].reshape(count * C, width)
        result = result + shifted(part, sign * NZ * b).reshape(count, C, width)
    return result


def groups(low, high):
    return [(start, min(3, high - start)) for start in range(low, high, 3)]


def forward(first, low, weights, stack, hidden_two):
    b0, bias_in, w_fwd, bias_mid = weights
    count, width = stack.shape[0], stack.shape[2]
    pre = dot(b0[low * C : (low + count) * C, :], first).reshape(count, C, width)
    filled = 0
    for start, rows in groups(0, count - 2):
        until = min(start + rows + 5, count) if start else 5
        if start == 0 or until > filled:
            hidden_one = jnp.tanh(pre[filled:until] + bias_in[...][None]).astype(bf16)
            z_stack(hidden_one.reshape((until - filled) * C, width), stack, 1, filled)
            filled = until
        out = middle_conv(w_fwd, stack, start, rows, 1)
        hidden_two[start : start + rows] = jnp.tanh(out + bias_mid[...][None]).astype(bf16)


def stepped(field_ext, kv_ext, bf, hidden_two):
    flux = dot(bf[...], hidden_two[...].reshape(18 * C, BROAD))
    correction = flux[0:TALL] + central_y(flux[TALL : 2 * TALL]) + central_z(flux[2 * TALL :])
    here = field_ext[...]
    y_up, y_down = shifted(here, NZ)[:, MIDDLE], shifted(here, -NZ)[:, MIDDLE]
    here = here[:, MIDDLE]
    up, down = row_moved(here, 1), row_moved(here, -1)
    laplace = up + down + y_up + y_down + lifted(here, 1) + lifted(here, -1)
    physics = kv_ext[0] * (laplace - 6.0 * here)
    physics = physics - kv_ext[1] * (0.5 * (up - down))
    physics = physics - kv_ext[2] * (0.5 * (y_up - y_down))
    physics = physics - kv_ext[3] * central_z(here)
    return here + time_step * (physics + correction[:, MIDDLE])


def row_moved(values, count):
    return pltpu.roll(values, (-count) % values.shape[0], axis=0)


def flux_pair(here):
    parts = [
        -0.5 * time_step * (row_moved(here, 1) - row_moved(here, -1)),
        -time_step * central_y(here),
        -time_step * central_z(here),
    ]
    flux = jnp.concatenate(parts, axis=0)
    high = flux.astype(bf16)
    low = (flux - high.astype(f32)).astype(bf16)
    return jnp.concatenate([high, low], axis=0)


def cotangent_two(back, hidden_two, low, high):
    two = centre(hidden_two, low, high).astype(f32)
    return (back.reshape(high - low, C, WIDE) * (1.0 - two * two)).astype(bf16)


def centre(ref, low, high):
    margin = (ref.shape[2] - WIDE) // 2
    return ref[low:high, :, margin : margin + WIDE]


def middle_terms(stack, values, spread):
    rows = values.shape[0] // C
    first_row = (stack.shape[0] - rows) // 2 - 1
    wide = values.astype(f32)
    for number, b in enumerate(STEPS):
        moved = shifted(wide, -NZ * b).astype(bf16) if b else values
        spread[0:rows, number * C : (number + 1) * C, :] = moved.reshape(rows, C, WIDE)
    pairs = jnp.zeros((12 * C, 6 * C), f32)
    for x in range(0, rows, 2):
        window = centre(stack, first_row + x, first_row + x + 4).reshape(12 * C, WIDE)
        pairs = pairs + dot_lanes(window, spread[x : x + 2].reshape(6 * C, WIDE))
    return pairs[0 : 9 * C, 0 : 3 * C] + pairs[3 * C :, 3 * C :]


def channel_sums(values):
    wide = values.astype(f32).reshape(values.shape[0] // C, C, WIDE)
    return column_to_row(jnp.sum(jnp.sum(wide, axis=0), axis=1, keepdims=True))


def out_terms(pair, hidden_two, rows):
    first_row = (hidden_two.shape[0] - rows) // 2
    two = centre(hidden_two, first_row, first_row + rows)
    outer = dot_lanes(two.reshape(rows * C, WIDE), pair)
    row_x = lax.broadcasted_iota(jnp.int32, outer.shape, 0) // C
    col = lax.broadcasted_iota(jnp.int32, outer.shape, 1)
    outer = jnp.where(col % 16 == row_x + 8 - rows // 2, outer, 0.0)
    outer = jnp.sum(outer.reshape(rows, C, outer.shape[1]), axis=0)
    kind = (lax.broadcasted_iota(jnp.int32, outer.shape, 1) // 16) % 3
    columns = [jnp.sum(jnp.where(kind == d, outer, 0.0), axis=1, keepdims=True) for d in range(3)]
    return [column_to_row(column) for column in columns]


def cotangent_one(w_bwd, stack, grad_stack, grad_one):
    for start, rows in groups(0, 10):
        back = middle_conv(w_bwd, grad_stack, start, rows, -1)
        first = start + (stack.shape[0] - 10) // 2
        one = centre(stack, first, first + rows)[:, C : 2 * C].astype(f32)
        grad_one[start : start + rows] = (back * (1.0 - one * one)).astype(bf16)


def first_terms(first, grad_one):
    own = own_lanes_only(grad_one[1:9].reshape(8 * C, WIDE).astype(f32))
    outer = dot_lanes(first, own.astype(bf16))
    row_x = lax.broadcasted_iota(jnp.int32, outer.shape, 0) % TALL
    col_x = lax.broadcasted_iota(jnp.int32, outer.shape, 1) // C
    parts = []
    for a in range(3):
        kept = jnp.where(row_x - col_x == a + 7, outer, 0.0)
        parts.append(jnp.sum(kept.reshape(9, TALL, 8 * C), axis=1))
    folded = jnp.concatenate(parts, axis=0)
    folded = folded[:, :128] + folded[:, 128:]
    folded = folded + pltpu.roll(folded, 64, axis=1)
    folded = folded + pltpu.roll(folded, 32, axis=1)
    return folded[:, :C], channel_sums(own)


def previous(here, kv_ext, bq, grad_one):
    spread = dot(bq[...], grad_one[...].reshape(10 * C, WIDE))
    total = here
    for row, b in enumerate(STEPS):
        taps = [spread[(row * 3 + i) * 16 : (row * 3 + i + 1) * 16] for i in range(3)]
        lift = lifted(taps[0], 1) + taps[1] + lifted(taps[2], -1)
        total = total + shifted(lift, -NZ * b)
    cell = lambda number: kv_ext[number, 4:20, :]
    scaled = cell(0) * here
    physics = row_moved(scaled, 1) + row_moved(scaled, -1) - 6.0 * scaled
    physics = physics + shifted(scaled, NZ) + shifted(scaled, -NZ)
    physics = physics + lifted(scaled, 1) + lifted(scaled, -1)
    scaled = cell(1) * here
    physics = physics + 0.5 * (row_moved(scaled, 1) - row_moved(scaled, -1))
    physics = physics + central_y(cell(2) * here) + central_z(cell(3) * here)
    return total + time_step * physics


def iota(shape, dimension):
    return lax.broadcasted_iota(jnp.int32, shape, dimension)


def ones_where(condition):
    return jnp.where(condition, 1.0, 0.0).astype(bf16)


def dot_rows(left, right):
    return lax.dot_general(left, right, (((0,), (0,)), ((), ())), preferred_element_type=f32)


def place_middle(conv_mid, wide, w_fwd, w_bwd):
    for target, backward in ((w_fwd, False), (w_bwd, True)):
        wide[...] = jnp.zeros_like(wide)
        for a in range(3):
            for b in range(3):
                for c in range(3):
                    block = conv_mid[a * 9 + b * 3 + c].astype(f32)
                    if not backward:
                        block = block.T
                    for x in range(3):
                        row = (x * 3 + b) * C
                        col = ((x + (2 - a if backward else a)) * 3 + c) * C
                        wide[row : row + C, col : col + C] = block
        target[...] = wide[...].astype(bf16)


def place_first(conv_in, b0, bq):
    taps = conv_in[...]
    shape = (27, 9 * TALL)
    spread = []
    for a in range(3):
        pick = ones_where(iota(shape, 0) == iota(shape, 1) // TALL + 9 * a)
        spread.append(dot_rows(taps, pick))
    j = iota(spread[0].shape, 1) % TALL
    for i in range(22):
        rows = sum(jnp.where(j == i + a, spread[a], 0.0) for a in range(3))
        b0[i * C : (i + 1) * C, :] = rows.astype(bf16)
    shape = (C, 10 * C)
    tiled = dot(taps, ones_where(iota(shape, 1) % C == iota(shape, 0))).astype(bf16)
    total = 0.0
    for a in range(3):
        pick = ones_where(iota((144, 27), 1) == iota((144, 27), 0) // 16 + 9 * a)
        rows = dot(pick, tiled)
        kept = iota(rows.shape, 1) // C == iota(rows.shape, 0) % 16 - a - 2
        total = total + jnp.where(kept, rows, 0.0)
    bq[...] = total.astype(bf16)


def place_flux(flux, bf, bb):
    taps = flux[...]
    shape = (C, 18 * C)
    tiled = dot(taps, ones_where(iota(shape, 1) % C == iota(shape, 0))).astype(bf16)
    shape = (3 * TALL, 3)
    rows = dot(ones_where(iota(shape, 1) == iota(shape, 0) // TALL), tiled)
    x, i = iota(rows.shape, 0) % TALL, iota(rows.shape, 1) // C
    first = iota(rows.shape, 0) < TALL
    factor = jnp.where(i == x - 2, 0.5, jnp.where(i == x - 4, -0.5, 0.0))
    factor = jnp.where(first, factor, jnp.where(i == x - 3, 1.0, 0.0))
    bf[...] = (rows * factor).astype(bf16)
    pick = ones_where(iota((3, 96), 0) == (iota((3, 96), 1) // 16) % 3)
    columns = dot_rows(taps, pick)
    j = iota(columns.shape, 1) % 16
    for i in range(14):
        bb[i * C : (i + 1) * C, :] = jnp.where(j == i + 1, columns, 0.0).astype(bf16)


def row_to_column(row):
    size = row.shape[1]
    wide = jnp.broadcast_to(row, (size, size))
    return jnp.sum(
        jnp.where(iota((size, size), 0) == iota((size, size), 1), wide, 0.0),
        axis=1,
        keepdims=True,
    )


def remote(source, target, sems, peer):
    copy = pltpu.make_async_remote_copy(
        src_ref=source,
        dst_ref=target,
        send_sem=sems[0],
        recv_sem=sems[1],
        device_id=peer,
        device_id_type=MESH,
    )
    copy.start()


def send_around(ext, sems, place, block=None):
    (me_x, size_x), (me_y, size_y) = place
    width = ext.shape[-1]
    side = (width - LANES) // 2
    lead = (slice(None),) * (len(ext.shape) - 2)
    sources = {0: slice(side, side + LANES), 1: slice(LANES, side + LANES), -1: slice(side, 2 * side)}
    targets = {0: slice(side, side + LANES), 1: slice(0, side), -1: slice(side + LANES, width)}
    rows = {0: OWN_ROWS, 1: slice(0, ROWS), -1: slice(2 * ROWS, TALL)}
    for dx, dy in AROUND:
        peer = (
            lax.rem(me_x + dx + size_x, size_x),
            lax.rem(me_y + dy + size_y, size_y),
        )
        source = ext.at[lead + (OWN_ROWS, sources[dy])]
        if block is not None:
            lanes = sources[dy]
            source = block.at[:, pl.ds(lanes.start - side, lanes.stop - lanes.start)]
        remote(source, ext.at[lead + (rows[dx], targets[dy])], sems, peer)
    depth = ext.shape[0] if lead else 1
    return depth * (3 * width - LANES) // 128


def wait_tiles(sem, gauge, count):
    part = gauge.at[pl.ds(0, 8 * count)]
    pltpu.make_async_copy(part, part, sem).wait()


def far_first_x(me_x, me_y, size):
    groups, ring, cores = (2, size // 4, 2) if size % 8 == 0 else (1, size, 1)
    steps = [
        (g, r, c) for g in range(groups) for r in range(ring) for c in range(cores)
    ][1:]
    steps.sort(key=lambda step: (-step[0] - min(step[1], ring - step[1]), -step[2]))
    at = lax.div(me_x, ring * cores), lax.rem(lax.div(me_x, cores), ring), lax.rem(me_x, cores)
    peers = []
    for g, r, c in steps:
        to = lax.rem(at[0] + g, groups), lax.rem(at[1] + r, ring), lax.rem(at[2] + c, cores)
        peers.append(((to[0] * ring + to[1]) * cores + to[2], me_y))
    return peers


def far_first_y(me_x, me_y, size_x, size_y):
    ring = size_y // 2
    steps = [(g, r) for g in range(2) for r in range(ring)][1:]
    steps.sort(key=lambda step: -step[0] - min(step[1], ring - step[1]))
    high, at = lax.div(me_y, ring), lax.rem(me_y, ring)
    return [
        (
            lax.rem(me_x + g * (size_x // 2), size_x),
            lax.rem(high + g, 2) * ring + lax.rem(at + r, ring),
        )
        for g, r in steps
    ]


def kernel(
    size_x, size_y, scale,
    field, cotangent, kappa, vel, conv_in_in, bias_in_in, conv_mid_in, bias_mid_in, flux_in,
    out_field, out_sums, out_small,
    f_ext, f1_ext, g_ext, a_ext, kv_ext, conv_in, bias_in_row, conv_mid, bias_mid_row, flux,
    bias_in, bias_mid, wide, b0, w_fwd, bf, bb, w_bwd, bq,
    stack_one, stack_two, two_one, two_two, spread, grad_stack, grad_one,
    sums, recv_x, recv_y, gathered, small, small_x, small_y, last_field, last_small, gauge,
    local_sem, send_sem, recv_sem,
):
    me_x, me_y = lax.axis_index("gx"), lax.axis_index("gy")
    place = (me_x, size_x), (me_y, size_y)
    half_x, half_y = size_x // 2, size_y // 2
    mine_hi = lax.div(me_y, half_y)
    peers_x, peers_y = far_first_x(me_x, me_y, size_x), far_first_y(me_x, me_y, size_x, size_y)
    near = [
        (lax.rem(me_x + dx + size_x, size_x), lax.rem(me_y + dy + size_y, size_y))
        for dx, dy in AROUND
        if dy != 0
    ]
    barrier = pltpu.get_barrier_semaphore()
    for peer in peers_y + near + peers_x:
        pl.semaphore_signal(barrier, inc=1, device_id=peer, device_id_type=MESH)
    own = (OWN_ROWS, OWN_LANES)
    broad_own = (OWN_ROWS, slice(256, 256 + LANES))
    arrivals = []
    for source, target in (
        (field, f_ext.at[broad_own]),
        (cotangent, g_ext.at[own]),
        (kappa, kv_ext.at[(0,) + own]),
        (vel, kv_ext.at[(slice(1, 4),) + own]),
        (conv_in_in, conv_in),
        (bias_in_in, bias_in_row),
        (conv_mid_in, conv_mid),
        (bias_mid_in, bias_mid_row),
        (flux_in, flux),
    ):
        copy = pltpu.make_async_copy(source, target, local_sem.at[len(arrivals)])
        copy.start()
        arrivals.append(copy)
    sems = lambda number: (send_sem.at[number], recv_sem.at[number])
    pl.semaphore_wait(barrier, len(near + peers_x + peers_y))
    tiles = [send_around(f_ext, sems(0), place, field)]
    for copy in arrivals:
        copy.wait()
    tiles += [send_around(kv_ext, sems(1), place), send_around(g_ext, sems(2), place)]

    bias_in[...] = row_to_column(bias_in_row[...])
    bias_mid[...] = row_to_column(bias_mid_row[...])
    place_first(conv_in, b0, bq)
    place_middle(conv_mid, wide, w_fwd, w_bwd)
    place_flux(flux, bf, bb)

    weights = (b0, bias_in, w_fwd, bias_mid)
    wait_tiles(recv_sem.at[0], gauge, tiles[0])
    first_one = first_stack(f_ext)
    forward(first_one, 1, weights, stack_one, two_one)
    first_one = first_one[:, MIDDLE]
    wait_tiles(recv_sem.at[1], gauge, tiles[1])
    f1_ext[...] = stepped(f_ext, kv_ext, bf, two_one)
    first_two = first_stack(f1_ext)
    forward(first_two, 4, weights, stack_two, two_two)

    wait_tiles(recv_sem.at[2], gauge, tiles[2])
    pair_two = flux_pair(g_ext[4:20, :])
    back_two = dot(bb[C : 13 * C, :], pair_two)
    grad_two = cotangent_two(back_two, two_two, 0, 12).reshape(12 * C, WIDE)
    z_stack(grad_two, grad_stack, -1, 0)
    cotangent_one(w_bwd, stack_two, grad_stack, grad_one)
    adjoint = previous(g_ext[4:20, :], kv_ext, bq, grad_one)
    a_ext[own] = adjoint[4:12, OWN_LANES]

    own_two = own_lanes_only(grad_two[2 * C : 10 * C].astype(f32)).astype(bf16)
    mid = middle_terms(stack_two, own_two, spread)
    tiles.append(send_around(a_ext, sems(3), place))
    row = lax.broadcasted_iota(jnp.int32, adjoint.shape, 0)
    share_one = own_lanes_only(jnp.where((row >= 4) & (row < 12), adjoint, 0.0))
    pair_one = flux_pair(share_one)
    back_one = dot(bb[2 * C : 12 * C, :], pair_one)
    own_one = cotangent_two(back_one, two_one, 4, 14).reshape(10 * C, WIDE)
    mid = mid + middle_terms(stack_one, own_one, spread)
    sums[:, 0 : 3 * C] = mid[0 : 8 * C]
    for number in range(3):
        sums[number * C : (number + 1) * C, 3 * C :] = mid[
            8 * C : 9 * C, number * C : (number + 1) * C
        ]
    sums[3 * C :, 3 * C :] = jnp.zeros((5 * C, C), f32)

    part = sums.shape[0] // size_x
    share = lambda x: pl.ds(
        pl.multiple_of(lax.rem(x + mine_hi * half_x, size_x) * part, part), part
    )
    for peer in peers_x:
        remote(sums.at[share(peer[0])], recv_x.at[me_x], sems(4), peer)

    in_two, bias_in_two = first_terms(first_two, grad_one)
    pair_two = own_lanes_only(pair_two.astype(f32)).astype(bf16)
    rows_two = [channel_sums(own_two)] + out_terms(pair_two, two_two, 8)
    rows_one = out_terms(pair_one, two_one, 10)
    wait_tiles(recv_sem.at[3], gauge, tiles[3])
    here = a_ext[4:20, :]
    full = cotangent_two(dot(bb[C : 13 * C, :], flux_pair(here)), two_one, 3, 15)
    full = full.reshape(12 * C, WIDE)
    z_stack(full, grad_stack, -1, 0)
    rows_one = [channel_sums(own_lanes_only(full[2 * C : 10 * C].astype(f32)))] + rows_one
    cotangent_one(w_bwd, stack_one, grad_stack, grad_one)
    in_one, bias_in_one = first_terms(first_one, grad_one)
    matrix = jnp.concatenate(
        [in_one + in_two, bias_in_one + bias_in_two]
        + [one + two for one, two in zip(rows_one, rows_two)],
        axis=0,
    )
    for number in range(4):
        small[:, number * C : (number + 1) * C] = matrix[number * 8 : number * 8 + 8]
    small_x[me_x] = small[...]

    per = part // 8
    wait_tiles(recv_sem.at[4], gauge, per * (size_x - 1))
    recv_x[me_x] = sums[share(me_x), :]
    total = recv_x[0]
    for k in range(1, size_x):
        total = total + recv_x[k]
    recv_y[me_y] = total
    for peer in peers_y:
        remote(recv_y.at[me_y], recv_y.at[me_y], sems(5), peer)
    for peer in peers_x:
        remote(small, small_x.at[me_x], sems(7), peer)

    final = previous(here, kv_ext, bq, grad_one)
    last_field[...] = final[4:12, OWN_LANES]
    results = [pltpu.make_async_copy(last_field, out_field, local_sem.at[0])]
    results[0].start()

    wait_tiles(recv_sem.at[7], gauge, size_x - 1)
    total = small_x[0]
    for k in range(1, size_x):
        total = total + small_x[k]
    small_y[me_y] = total
    for peer in peers_y:
        remote(small_y.at[me_y], small_y.at[me_y], sems(8), peer)

    wait_tiles(recv_sem.at[5], gauge, per * (size_y - 1))
    total = recv_y[0]
    for k in range(1, size_y):
        total = total + recv_y[k]
    gathered[share(me_x), :] = (total * scale).astype(bf16)
    for peer in peers_x:
        remote(gathered.at[share(me_x)], gathered.at[share(me_x)], sems(6), peer)

    wait_tiles(recv_sem.at[8], gauge, size_y - 1)
    total = small_y[0]
    for k in range(1, size_y):
        total = total + small_y[k]
    last_small[...] = total * scale
    results.append(pltpu.make_async_copy(last_small, out_small, local_sem.at[1]))
    results[1].start()
    wait_tiles(recv_sem.at[6], gauge, per // 2 * (size_x - 1))
    results.append(pltpu.make_async_copy(gathered, out_sums, local_sem.at[2]))
    results[2].start()

    for number in range(4):
        wait_tiles(send_sem.at[number], gauge, tiles[number])
    wait_tiles(send_sem.at[4], gauge, per * (size_x - 1))
    wait_tiles(send_sem.at[5], gauge, per * (size_y - 1))
    wait_tiles(send_sem.at[6], gauge, per // 2 * (size_x - 1))
    wait_tiles(send_sem.at[7], gauge, size_x - 1)
    wait_tiles(send_sem.at[8], gauge, size_y - 1)
    for copy in results:
        copy.wait()


def unpack(field, sums, small, out_field, out_in, out_bias_in, out_mid, out_bias_mid, out_out):
    out_field[...] = field[...]
    for a in range(3):
        for b in range(3):
            for c in range(3):
                row = (a * 3 + c) * C
                if row < 8 * C:
                    value = sums[row : row + C, b * C : (b + 1) * C]
                else:
                    value = sums[b * C : (b + 1) * C, 3 * C :]
                out_mid[a * 9 + b * 3 + c] = value.astype(f32)
    for number in range(3):
        out_in[number * 8 : number * 8 + 8] = small[:, number * C : (number + 1) * C]
    last = small[:, 3 * C :]
    out_in[24:27] = last[0:3]
    out_bias_in[...] = last[3:4]
    out_bias_mid[...] = last[4:5]
    out_out[...] = last[5:8]


def solution(mesh):
    size_x, size_y = mesh.shape["gx"], mesh.shape["gy"]

    def shards(
        scalar_field, field_cotangent, diffusivity, velocity,
        conv_in, bias_in, conv_mid, bias_mid, flux_out,
    ):
        cells = scalar_field.size * size_x * size_y
        vmem = pl.BlockSpec(memory_space=pltpu.VMEM)
        anywhere = pl.BlockSpec(memory_space=pltpu.HBM)
        part = 256 // size_x
        ext, broad = pltpu.VMEM((TALL, WIDE), f32), pltpu.VMEM((TALL, BROAD), f32)
        shape = jax.ShapeDtypeStruct
        outs = pl.pallas_call(
            lambda *refs: kernel(size_x, size_y, 1.0 / math.sqrt(cells), *refs),
            out_shape=[shape((ROWS, LANES), f32), shape((256, 128), bf16), shape((8, 128), f32)],
            in_specs=[anywhere] * 9,
            out_specs=[anywhere] * 3,
            scratch_shapes=[
                broad, ext, ext, ext,
                pltpu.VMEM((4, TALL, WIDE), f32),
                pltpu.VMEM((27, C), bf16),
                pltpu.VMEM((1, C), f32),
                pltpu.VMEM((27, C, C), bf16),
                pltpu.VMEM((1, C), f32),
                pltpu.VMEM((3, C), bf16),
                pltpu.VMEM((C, 1), f32),
                pltpu.VMEM((C, 1), f32),
                pltpu.VMEM((288, 480), f32),
                pltpu.VMEM((22 * C, 9 * TALL), bf16),
                pltpu.VMEM((288, 480), bf16),
                pltpu.VMEM((3 * TALL, 18 * C), bf16),
                pltpu.VMEM((14 * C, 96), bf16),
                pltpu.VMEM((288, 480), bf16),
                pltpu.VMEM((144, 10 * C), bf16),
                pltpu.VMEM((20, 3 * C, BROAD), bf16),
                pltpu.VMEM((14, 3 * C, WIDE), bf16),
                pltpu.VMEM((18, C, BROAD), bf16),
                pltpu.VMEM((12, C, WIDE), bf16),
                pltpu.VMEM((10, 3 * C, WIDE), bf16),
                pltpu.VMEM((12, 3 * C, WIDE), bf16),
                pltpu.VMEM((10, C, WIDE), bf16),
                pltpu.VMEM((256, 128), f32),
                pltpu.VMEM((size_x, part, 128), f32),
                pltpu.VMEM((size_y, part, 128), f32),
                pltpu.VMEM((256, 128), bf16),
                pltpu.VMEM((8, 128), f32),
                pltpu.VMEM((size_x, 8, 128), f32),
                pltpu.VMEM((size_y, 8, 128), f32),
                pltpu.VMEM((ROWS, LANES), f32),
                pltpu.VMEM((8, 128), f32),
                pltpu.VMEM((640, 128), f32),
                pltpu.SemaphoreType.DMA((9,)),
                pltpu.SemaphoreType.DMA((9,)),
                pltpu.SemaphoreType.DMA((9,)),
            ],
            compiler_params=pltpu.CompilerParams(
                collective_id=0, has_side_effects=True, vmem_limit_bytes=60 * 1024 * 1024
            ),
        )(
            scalar_field, field_cotangent, diffusivity, velocity,
            conv_in, bias_in.reshape(1, C), conv_mid, bias_mid.reshape(1, C), flux_out.T,
        )
        outs = pl.pallas_call(
            unpack,
            out_shape=[
                shape((ROWS, LANES), f32),
                shape((27, C), f32),
                shape((1, C), f32),
                shape((27, C, C), f32),
                shape((1, C), f32),
                shape((3, C), f32),
            ],
            in_specs=[vmem] * 3,
            out_specs=[vmem] * 6,
        )(*outs)
        return (outs[0], outs[1], outs[2].reshape(C), outs[3], outs[4].reshape(C), outs[5].T)

    return jax.shard_map(
        shards,
        mesh=mesh,
        in_specs=(
            P("gx", "gy"), P("gx", "gy"), P("gx", "gy"), P(None, "gx", "gy"),
            P(), P(), P(), P(), P(),
        ),
        out_specs=(P("gx", "gy"), P(), P(), P(), P(), P()),
        check_vma=False,
    )
```
